32 devices in a mesh: dp: 16 (over z, y, x), cent: 2 (over core).
Axes of the slice: x: 2, y: 2, z: 4, core: 2. Of those that a mesh axis runs over, the one named last changes fastest.
Arguments:
- embeddings: float32 [6144, 1024], P(('dp', 'cent')), may hold values from -128 to 128
- centroids: float32 [4096, 1024], P(('dp', 'cent')), may hold values from -6 to 6
Outputs:
- updated: float32 [4096, 1024], P(('dp', 'cent'))
- entropy: float32 [6144], P(('dp', 'cent'))
The draws below stay inside these ranges and needn't reach their ends.
All inputs are finite; a program needn't handle non-finite values.
Results may differ from the reference program's by a relative error of at most 0.024.
Values may be sent and summed in bfloat16 or wider, within the bound.
No kernel may reach another device: no remote copies, remote signals or barrier semaphores. Data moves between devices by JAX's collectives and lax.ppermute only.
A program may use at most 64 MiB of HBM per device.

```python
import math
import jax
import jax.numpy as jnp
from jax import lax

D = 1024
K = 4096
GROUP = 384
ROWS = 6144


def shared_centroids(key):
    key = jax.random.fold_in(key, 301)
    return jnp.clip(jax.random.normal(key, (K, D), jnp.float32), -6.0, 6.0)


def draw_centroids(key, part):
    shared = shared_centroids(key)
    return shared


def draw_embeddings(key, part):
    shared = shared_centroids(key)
    key = jax.random.fold_in(key, 11)
    keys_all = jax.random.split(key, 8)
    key_noise = keys_all[0]
    key_rough = keys_all[1]
    key_single = keys_all[3]
    key_jitter = keys_all[4]
    key_first = keys_all[5]
    key_second = keys_all[6]
    key_margin = keys_all[7]
    position = jnp.arange(ROWS, dtype=jnp.float32) / ROWS
    noise = jnp.clip(jax.random.normal(key_noise, (ROWS, D), jnp.float32), -6.0, 6.0)
    rough = jnp.exp(jax.random.uniform(key_rough, (ROWS,), jnp.float32, 0.0, math.log(2.0)))
    scale = (1.0 + 2.0 * position) * rough
    drawn_rows = scale[:, None] * noise
    planted = ROWS // 32
    blocks = jnp.arange(planted, dtype=jnp.int32)
    single_pick = jax.random.randint(key_single, (planted,), 0, K)
    single_gain = (8 + 4 * (blocks % 4)).astype(jnp.float32)
    jitter = jnp.clip(jax.random.normal(key_jitter, (planted, D), jnp.float32), -6.0, 6.0)
    single_rows = single_gain[:, None] * shared[single_pick] + 0.5 * jitter
    first_pick = jax.random.randint(key_first, (planted,), 0, K)
    second_pick = (first_pick + jax.random.randint(key_second, (planted,), 1, K)) % K
    closer = shared[first_pick]
    farther = shared[second_pick]
    paired_improvement = (8 + 2 * (blocks % 3)).astype(jnp.float32)
    logit_margin = jax.random.uniform(key_margin, (planted,), jnp.float32, 1.5, 2.5)
    between = closer - farther
    norm_difference = jnp.sum(closer * closer - farther * farther, axis=1)
    separation_squared = jnp.sum(between * between, axis=1)
    logit_shift = (2.0 * sampled_softness() * logit_margin - (paired_improvement - 1.0) * norm_difference) / (2.0 * separation_squared)
    pair_rows = 0.5 * paired_improvement[:, None] * (closer + farther) + logit_shift[:, None] * between
    lattice = drawn_rows.reshape(planted, 32, D)
    lattice = lattice.at[:, 5, :].set(single_rows)
    lattice = lattice.at[:, 21, :].set(pair_rows)
    return jnp.clip(lattice.reshape(ROWS, D), -128.0, 128.0).astype(jnp.float32)


def sampled_softness():
    return 32.0


def setup_inputs(seed: int = 0) -> dict:
    arg_keys = jax.random.split(jax.random.key(seed), 3)
    embeddings = draw_embeddings(jax.random.fold_in(arg_keys[2], 71), 0)
    centroids = draw_centroids(jax.random.fold_in(arg_keys[2], 71), 0)
    return dict(embeddings=embeddings, centroids=centroids)


softness_level = 32.0
prior_mass = 4.0


def to_bf(values):
    return lax.optimization_barrier(values.astype(jnp.bfloat16)).astype(jnp.float32)


def scores_of(rows, row_norms, cents, centroid_norm):
    inner_products = jnp.dot(rows, cents.T, precision=lax.Precision.HIGHEST, preferred_element_type=jnp.float32)
    return -(row_norms[:, None] - 2.0 * inner_products + centroid_norm[None, :]) / (2.0 * softness_level)


def reference(embeddings, centroids):
    rows_b = to_bf(embeddings)
    row_squared_norm = jnp.sum(rows_b * rows_b, axis=1)
    row_blocks = rows_b.reshape(ROWS // GROUP, GROUP, D)
    norm_blocks = row_squared_norm.reshape(ROWS // GROUP, GROUP)
    cent_b = to_bf(centroids)
    centroid_squared_norm = jnp.sum(cent_b * cent_b, axis=1)

    def accumulate(carry, item):
        rows, row_norms = item
        score = scores_of(rows, row_norms, cent_b, centroid_squared_norm)
        top = jnp.max(score, axis=1)
        weight = jnp.exp(score - top[:, None])
        total = jnp.sum(weight, axis=1)
        resp = to_bf(weight / total[:, None])
        sums = carry[0] + jnp.dot(resp.T, rows, precision=lax.Precision.HIGHEST, preferred_element_type=jnp.float32)
        counts = carry[1] + jnp.sum(resp, axis=0)
        return (sums, counts), 0.0

    start = (jnp.zeros((K, D), jnp.float32), jnp.zeros((K,), jnp.float32))
    (sums, counts), unused = lax.scan(accumulate, start, (row_blocks, norm_blocks))
    updated = (sums + prior_mass * centroids) / (counts + prior_mass)[:, None]
    new_b = to_bf(updated)
    new_sq = jnp.sum(new_b * new_b, axis=1)

    def entropy_block(item):
        rows, row_norms = item
        score = scores_of(rows, row_norms, new_b, new_sq)
        top = jnp.max(score, axis=1)
        shifted = score - top[:, None]
        weight = jnp.exp(shifted)
        total = jnp.sum(weight, axis=1)
        spread = jnp.sum(weight * shifted, axis=1)
        return jnp.log(total) - spread / total

    entropy = lax.map(entropy_block, (row_blocks, norm_blocks)).reshape(ROWS)
    return updated, entropy
```

```python
import functools

import jax
import jax.numpy as jnp
from jax import lax
from jax.experimental import pallas as pl
from jax.experimental.pallas import tpu as pltpu
from jax.sharding import PartitionSpec as P

softness_level = 32.0
prior_mass = 4.0
PLANE = 4


def vmem_limit(*arrays):
    held = sum(2 * v.size * v.dtype.itemsize for v in arrays)
    return min(56 << 20, held + (16 << 20))


def load_chunks(chunks, rows_v, sems, shard):
    copies = []
    for i, chunk in enumerate(chunks):
        copy = pltpu.make_async_copy(chunk, rows_v.at[pl.ds(i * shard, shard)], sems.at[i])
        copy.start()
        copies.append(copy)
    return copies


def row_squares(rows):
    wide = rows.astype(jnp.float32)
    square = wide * wide
    part = square[:, :128]
    for j in range(128, square.shape[1], 128):
        part = part + square[:, j : j + 128]
    return jnp.sum(part.T, axis=0, keepdims=True)


def centroid_squares(piece):
    wide = piece.astype(jnp.float32)
    return jnp.sum(wide * wide, axis=1, keepdims=True)


def scores(piece, cent_sq, rows, row_sq):
    inner = lax.dot_general(piece, rows, (((1,), (1,)), ((), ())), preferred_element_type=jnp.float32)
    return -(row_sq - 2.0 * inner + cent_sq) / (2.0 * softness_level)


def first_kernel(shard, cents, *refs):
    chunks = refs[:PLANE]
    weight_ref, stats_ref, row_sq_ref, rows_v, sems = refs[PLANE:]
    copies = load_chunks(chunks, rows_v, sems, shard)
    piece = cents[...]
    cent_sq = centroid_squares(piece)
    tile = 2 * shard
    for j in range(PLANE // 2):
        copies[2 * j].wait()
        copies[2 * j + 1].wait()
        rows = rows_v[j * tile : (j + 1) * tile, :]
        row_sq = row_squares(rows)
        score = scores(piece, cent_sq, rows, row_sq)
        top = jnp.max(score, axis=0, keepdims=True)
        weight = jnp.exp(score - top)
        total = jnp.sum(weight, axis=0, keepdims=True)
        weight_ref[:, j * tile : (j + 1) * tile] = weight
        row_sq_ref[:, j * tile : (j + 1) * tile] = row_sq
        for i in range(2):
            stats_ref[0, 2 * j + i : 2 * j + i + 1, :] = top[:, i * shard : (i + 1) * shard]
            stats_ref[1, 2 * j + i : 2 * j + i + 1, :] = total[:, i * shard : (i + 1) * shard]


def first_pass(cents, chunks):
    shard, width = chunks[0].shape
    n_k = cents.shape[0]
    n_rows = PLANE * shard
    vmem = pl.BlockSpec(memory_space=pltpu.VMEM)
    hbm = pl.BlockSpec(memory_space=pl.ANY)
    return pl.pallas_call(
        functools.partial(first_kernel, shard),
        out_shape=(
            jax.ShapeDtypeStruct((n_k, n_rows), jnp.float32),
            jax.ShapeDtypeStruct((2, PLANE, shard), jnp.float32),
            jax.ShapeDtypeStruct((1, n_rows), jnp.float32),
        ),
        in_specs=[vmem] + [hbm] * PLANE,
        out_specs=(vmem, vmem, vmem),
        scratch_shapes=[pltpu.VMEM((n_rows, width), jnp.bfloat16), pltpu.SemaphoreType.DMA((PLANE,))],
        compiler_params=pltpu.CompilerParams(vmem_limit_bytes=vmem_limit(cents, *chunks)),
        cost_estimate=pl.CostEstimate(
            flops=2 * n_k * n_rows * width, bytes_accessed=2 * n_rows * width, transcendentals=n_k * n_rows
        ),
        name="first_pass",
    )(cents, *chunks)


def sums_kernel(shard, n_slots, scale, *refs):
    weights = refs[:n_slots]
    n_chunks = PLANE * n_slots
    chunks = refs[n_slots : n_slots + n_chunks]
    out_ref, rows_v, sems = refs[n_slots + n_chunks :]
    copies = load_chunks(chunks, rows_v, sems, shard)
    width = rows_v.shape[1]
    n_rows = PLANE * shard
    counts = jnp.zeros((out_ref.shape[0], 1), jnp.float32)
    for s in range(n_slots):
        resp = (weights[s][...] * scale[s : s + 1, :]).astype(jnp.bfloat16)
        counts = counts + jnp.sum(resp.astype(jnp.float32), axis=1, keepdims=True)
        for i in range(PLANE):
            copies[PLANE * s + i].wait()
        part = jnp.dot(resp, rows_v[s * n_rows : (s + 1) * n_rows, :], preferred_element_type=jnp.float32)
        if s:
            part = part + out_ref[:, :width]
        out_ref[:, :width] = part
    out_ref[:, width:] = jnp.broadcast_to(counts, (out_ref.shape[0], 128))


def sums_pass(scale, weights, chunks):
    shard, width = chunks[0].shape
    n_slots = len(weights)
    n_k = weights[0].shape[0]
    n_rows = len(chunks) * shard
    vmem = pl.BlockSpec(memory_space=pltpu.VMEM)
    hbm = pl.BlockSpec(memory_space=pl.ANY)
    return pl.pallas_call(
        functools.partial(sums_kernel, shard, n_slots),
        out_shape=jax.ShapeDtypeStruct((n_k, width + 128), jnp.float32),
        in_specs=[vmem] * (1 + n_slots) + [hbm] * len(chunks),
        out_specs=vmem,
        scratch_shapes=[pltpu.VMEM((n_rows, width), jnp.bfloat16), pltpu.SemaphoreType.DMA((len(chunks),))],
        compiler_params=pltpu.CompilerParams(vmem_limit_bytes=vmem_limit(*weights, *chunks)),
        cost_estimate=pl.CostEstimate(
            flops=2 * n_k * n_rows * width, bytes_accessed=2 * n_rows * width, transcendentals=0
        ),
        name="sums_pass",
    )(scale, *weights, *chunks)


def second_kernel(shard, n_slots, per_device, sums, previous, *refs):
    n_chunks = PLANE * n_slots
    row_sqs = refs[:n_slots]
    chunks = refs[n_slots : n_slots + n_chunks]
    updated_ref, stats_ref, rows_v, sems = refs[n_slots + n_chunks :]
    copies = load_chunks(chunks, rows_v, sems, shard)
    width = rows_v.shape[1]
    counts = sums[:, width : width + 1]
    renewed = (sums[:, :width] + prior_mass * previous[...]) / (counts + prior_mass)
    updated_ref[...] = renewed[:per_device, :]
    piece = renewed.astype(jnp.bfloat16)
    cent_sq = centroid_squares(piece)
    tile = 2 * shard
    for s in range(n_slots):
        for j in range(PLANE // 2):
            first = PLANE * s + 2 * j
            copies[first].wait()
            copies[first + 1].wait()
            rows = rows_v[first * shard : (first + 2) * shard, :]
            score = scores(piece, cent_sq, rows, row_sqs[s][:, j * tile : (j + 1) * tile])
            top = jnp.max(score, axis=0, keepdims=True)
            shifted = score - top
            weight = jnp.exp(shifted)
            total = jnp.sum(weight, axis=0, keepdims=True)
            spread = jnp.sum(weight * shifted, axis=0, keepdims=True)
            for i in range(2):
                span = slice(i * shard, (i + 1) * shard)
                row = slice(2 * j + i, 2 * j + i + 1)
                stats_ref[s, 0, row, :] = top[:, span]
                stats_ref[s, 1, row, :] = total[:, span]
                stats_ref[s, 2, row, :] = spread[:, span]


def second_pass(sums, previous, row_sqs, chunks, per_device):
    shard, width = chunks[0].shape
    n_slots = len(row_sqs)
    n_k = previous.shape[0]
    n_rows = len(chunks) * shard
    vmem = pl.BlockSpec(memory_space=pltpu.VMEM)
    hbm = pl.BlockSpec(memory_space=pl.ANY)
    return pl.pallas_call(
        functools.partial(second_kernel, shard, n_slots, per_device),
        out_shape=(
            jax.ShapeDtypeStruct((per_device, width), jnp.float32),
            jax.ShapeDtypeStruct((n_slots, 3, PLANE, shard), jnp.float32),
        ),
        in_specs=[vmem] * (2 + n_slots) + [hbm] * len(chunks),
        out_specs=(vmem, vmem),
        scratch_shapes=[pltpu.VMEM((n_rows, width), jnp.bfloat16), pltpu.SemaphoreType.DMA((len(chunks),))],
        compiler_params=pltpu.CompilerParams(vmem_limit_bytes=vmem_limit(sums, previous, *chunks)),
        cost_estimate=pl.CostEstimate(
            flops=2 * n_k * n_rows * width, bytes_accessed=2 * n_rows * width, transcendentals=n_k * n_rows
        ),
        name="second_pass",
    )(sums, previous, *row_sqs, *chunks)


def merge(parts, axis):
    tops = [jnp.take(p, 0, axis=axis) for p in parts]
    top = functools.reduce(jnp.maximum, tops)
    total = 0.0
    spread = 0.0
    for p, own in zip(parts, tops):
        drop = own - top
        factor = jnp.exp(drop)
        part_total = jnp.take(p, 1, axis=axis)
        total = total + factor * part_total
        if p.shape[axis] == 3:
            spread = spread + factor * (jnp.take(p, 2, axis=axis) + drop * part_total)
    return top, total, spread


def solution(mesh):
    n_dp = mesh.shape["dp"]
    n_cent = mesh.shape["cent"]
    n_slots = n_dp // PLANE

    def along_z(value, shift):
        return lax.ppermute(value, "dp", [(i, (i + PLANE * shift) % n_dp) for i in range(n_dp)])

    def in_plane(value, bits):
        return lax.ppermute(value, "dp", [(i, i ^ bits) for i in range(n_dp)])

    def across(value, bits):
        return lax.ppermute(value, "cent", [(i, i ^ bits) for i in range(n_cent)])

    def blocks_swapped(value, bits):
        blocks = jnp.split(value, n_cent, axis=0)
        return jnp.concatenate([blocks[i ^ bits] for i in range(n_cent)], axis=0)

    def on_device(embeddings, centroids):
        per_device = centroids.shape[0]
        own = embeddings.astype(jnp.bfloat16)
        order = [0] + sorted(range(1, n_slots), key=lambda s: (min(s, n_slots - s), s))
        slots = {0: own}
        for s in order[1:]:
            slots[s] = along_z(own, s)
        planes = {}
        for s in order:
            chunk = slots[s]
            early, late = (1, 2) if s % 2 == 0 else (2, 1)
            pieces = {0: chunk, early: in_plane(chunk, early), late: in_plane(chunk, late)}
            pieces[3] = in_plane(pieces[early], late)
            planes[s] = [pieces[b] for b in range(PLANE)]
        chunks = [c for s in range(n_slots) for c in planes[s]]

        previous = jnp.concatenate([centroids] + [across(centroids, b) for b in range(1, n_cent)], axis=0)
        piece = previous.astype(jnp.bfloat16)

        weights, local, row_sqs, plane_stats = [], [], [], []
        for s in range(n_slots):
            weight, stats, row_sq = first_pass(piece, planes[s])
            weights.append(weight)
            local.append(stats)
            row_sqs.append(row_sq)
            parts = [stats]
            for bits in range(1, PLANE):
                other = in_plane(stats, bits)
                parts.append(jnp.stack([other[:, b ^ bits] for b in range(PLANE)], axis=1))
            top, total, unused = merge(parts, 0)
            plane_stats.append(jnp.stack([top, total]))
        plane_stats = jnp.stack(plane_stats)
        parts = [plane_stats]
        for shift in range(1, n_slots):
            other = along_z(plane_stats, shift)
            parts.append(jnp.concatenate([other[n_slots - shift :], other[: n_slots - shift]], axis=0))
        top, total, unused = merge(parts, 1)
        scale = jnp.exp(jnp.stack([stats[0] for stats in local]) - top) / total
        scale = scale.reshape(n_slots, PLANE * own.shape[0])

        sums = sums_pass(scale, weights, chunks)
        bits = 1
        while bits < n_cent:
            sums = sums + blocks_swapped(across(sums, bits), bits)
            bits *= 2

        updated, stats = second_pass(sums, previous, row_sqs, chunks, per_device)
        parts = [stats[0]]
        for shift in range(1, n_slots):
            parts.append(along_z(stats[shift], -shift))
        stats = jnp.stack(merge(parts, 0))
        parts = [stats[:, 0]]
        for bits in range(1, PLANE):
            parts.append(in_plane(stats[:, bits], bits))
        top, total, spread = merge(parts, 0)
        entropy = jnp.log(total) - spread / total
        return (updated, entropy)

    in_specs = (P(("dp", "cent"), None), P(("dp", "cent"), None))
    out_specs = (P(("dp", "cent"), None), P(("dp", "cent")))
    return jax.shard_map(
        on_device, mesh=mesh, in_specs=in_specs, out_specs=out_specs, check_vma=False
    )
```

```python
import functools

import jax
import jax.numpy as jnp
from jax import lax
from jax.experimental import pallas as pl
from jax.experimental.pallas import tpu as pltpu
from jax.sharding import PartitionSpec as P

softness_level = 32.0
prior_mass = 4.0
CUBE = 8
GROUPS = ((0, 1, 2, 4), (3, 5), (6, 7))
VMEM = pl.BlockSpec(memory_space=pltpu.VMEM)
GRANT = 20 << 20


def params():
    return pltpu.CompilerParams(vmem_limit_bytes=GRANT)


def row_squares(rows):
    wide = rows.astype(jnp.float32)
    square = wide * wide
    part = square[:, :128]
    for j in range(128, square.shape[1], 128):
        part = part + square[:, j : j + 128]
    return jnp.sum(part.T, axis=0, keepdims=True)


def centroid_squares(piece):
    wide = piece.astype(jnp.float32)
    return jnp.sum(wide * wide, axis=1, keepdims=True)


def scores(piece, cent_sq, rows, row_sq):
    inner = lax.dot_general(piece, rows, (((1,), (1,)), ((), ())), preferred_element_type=jnp.float32)
    return -(row_sq - 2.0 * inner + cent_sq) * (0.5 / softness_level)


def first_kernel(n, shard, cents, *refs):
    chunks = refs[:n]
    weight_ref, stats_ref, row_sq_ref, rows_ref = refs[n:]
    for i in range(n):
        rows_ref[i * shard : (i + 1) * shard, :] = chunks[i][...]
    piece = cents[...]
    cent_sq = centroid_squares(piece)
    tile = 2 * shard
    for j in range(n // 2):
        span = slice(j * tile, (j + 1) * tile)
        rows = rows_ref[span, :]
        row_sq = row_squares(rows)
        score = scores(piece, cent_sq, rows, row_sq)
        top = jnp.max(score, axis=0, keepdims=True)
        weight = jnp.exp(score - top)
        total = jnp.sum(weight, axis=0, keepdims=True)
        weight_ref[:, span] = weight
        row_sq_ref[:, span] = row_sq
        for i in range(2):
            stats_ref[0, 2 * j + i : 2 * j + i + 1, :] = top[:, i * shard : (i + 1) * shard]
            stats_ref[1, 2 * j + i : 2 * j + i + 1, :] = total[:, i * shard : (i + 1) * shard]


def first_pass(cents, chunks):
    n = len(chunks)
    shard, width = chunks[0].shape
    n_k = cents.shape[0]
    n_rows = n * shard
    return pl.pallas_call(
        functools.partial(first_kernel, n, shard),
        out_shape=(
            jax.ShapeDtypeStruct((n_k, n_rows), jnp.float32),
            jax.ShapeDtypeStruct((2, n, shard), jnp.float32),
            jax.ShapeDtypeStruct((1, n_rows), jnp.float32),
            jax.ShapeDtypeStruct((n_rows, width), jnp.bfloat16),
        ),
        in_specs=[VMEM] * (1 + n),
        out_specs=(VMEM,) * 4,
        compiler_params=params(),
        cost_estimate=pl.CostEstimate(
            flops=2 * n_k * n_rows * width, bytes_accessed=2 * n_rows * width, transcendentals=n_k * n_rows
        ),
        name="first_pass",
    )(cents, *chunks)


def sums_kernel(first, last, n, *refs):
    scales, weights, rows = refs[:n], refs[n : 2 * n], refs[2 * n : 3 * n]
    out_ref = refs[3 * n]
    width = rows[0].shape[1]
    counts = 0.0
    for s in range(n):
        resp = (weights[s][first:last, :] * scales[s][...]).astype(jnp.bfloat16)
        counts = counts + jnp.sum(resp.astype(jnp.float32), axis=1, keepdims=True)
        part = jnp.dot(resp, rows[s][...], preferred_element_type=jnp.float32)
        if s:
            part = part + out_ref[:, :width]
        out_ref[:, :width] = part
    out_ref[:, width:] = jnp.broadcast_to(counts, (last - first, 128))


def sums_pass(scales, weights, rows, first, last):
    n = len(rows)
    width = rows[0].shape[1]
    n_rows = sum(r.shape[0] for r in rows)
    return pl.pallas_call(
        functools.partial(sums_kernel, first, last, n),
        out_shape=jax.ShapeDtypeStruct((last - first, width + 128), jnp.float32),
        in_specs=[VMEM] * (3 * n),
        out_specs=VMEM,
        compiler_params=params(),
        cost_estimate=pl.CostEstimate(
            flops=2 * (last - first) * n_rows * width, bytes_accessed=2 * n_rows * width, transcendentals=0
        ),
        name="sums_pass",
    )(*scales, *weights, *rows)


def second_kernel(shard, n, cents, *refs):
    row_sqs, rows, stats = refs[:n], refs[n : 2 * n], refs[2 * n :]
    piece = cents[...]
    cent_sq = centroid_squares(piece)
    tile = 2 * shard
    for s in range(n):
        for j in range(rows[s].shape[0] // tile):
            span = slice(j * tile, (j + 1) * tile)
            score = scores(piece, cent_sq, rows[s][span, :], row_sqs[s][:, span])
            top = jnp.max(score, axis=0, keepdims=True)
            shifted = score - top
            weight = jnp.exp(shifted)
            total = jnp.sum(weight, axis=0, keepdims=True)
            spread = jnp.sum(weight * shifted, axis=0, keepdims=True)
            for i in range(2):
                part = slice(i * shard, (i + 1) * shard)
                at = slice(2 * j + i, 2 * j + i + 1)
                stats[s][0, at, :] = top[:, part]
                stats[s][1, at, :] = total[:, part]
                stats[s][2, at, :] = spread[:, part]


def second_pass(cents, row_sqs, rows, shard):
    n = len(rows)
    n_k, width = cents.shape
    n_rows = sum(r.shape[0] for r in rows)
    return pl.pallas_call(
        functools.partial(second_kernel, shard, n),
        out_shape=tuple(jax.ShapeDtypeStruct((3, r.shape[0] // shard, shard), jnp.float32) for r in rows),
        in_specs=[VMEM] * (1 + 2 * n),
        out_specs=(VMEM,) * n,
        compiler_params=params(),
        cost_estimate=pl.CostEstimate(
            flops=2 * n_k * n_rows * width, bytes_accessed=2 * n_rows * width, transcendentals=n_k * n_rows
        ),
        name="second_pass",
    )(cents, *row_sqs, *rows)


def merge(a, b):
    top = jnp.maximum(a[0], b[0])
    drops = (a[0] - top, b[0] - top)
    factors = (jnp.exp(drops[0]), jnp.exp(drops[1]))
    out = [top, factors[0] * a[1] + factors[1] * b[1]]
    if a.shape[0] == 3:
        out.append(factors[0] * (a[2] + drops[0] * a[1]) + factors[1] * (b[2] + drops[1] * b[1]))
    return jnp.stack(out)


def by_chunk(groups):
    place = {b: (g, i) for g, bits in enumerate(GROUPS) for i, b in enumerate(bits)}
    return jnp.stack([groups[place[b][0]][:, place[b][1]] for b in range(CUBE)], axis=1)


def solution(mesh):
    n_dp = mesh.shape["dp"]
    n_cent = mesh.shape["cent"]
    top_bit = n_dp // 2

    def flip(value, bits):
        return lax.ppermute(value, "dp", [(i, i ^ bits) for i in range(n_dp)])

    def across(value, bits):
        return lax.ppermute(value, "cent", [(i, i ^ bits) for i in range(n_cent)])

    def gather_cent(value):
        bits = 1
        while bits < n_cent:
            value = jnp.concatenate([value, across(value, bits)], axis=0)
            bits *= 2
        return value

    def scatter_cent(value):
        bits = n_cent // 2
        while bits:
            half = value.shape[0] // 2
            value = value[:half] + across(value[half:], bits)
            bits //= 2
        return value

    def gather_near(value):
        bits = CUBE
        while bits < top_bit:
            value = jnp.concatenate([value, flip(value, bits)], axis=0)
            bits *= 2
        return value

    def scatter_near(value):
        bits = top_bit // 2
        while bits >= CUBE:
            half = value.shape[0] // 2
            value = value[:half] + flip(value[half:], bits)
            bits //= 2
        return value

    def on_device(embeddings, centroids):
        shard, width = embeddings.shape
        half = shard // 2
        chunk = {0: embeddings.astype(jnp.bfloat16)}
        for bit in (1, 2, 4):
            chunk[bit] = flip(chunk[0], bit)
        chunk[3] = flip(chunk[1], 2)
        chunk[6] = flip(chunk[2], 4)
        chunk[5] = flip(chunk[4], 1)
        chunk[7] = jnp.concatenate([flip(chunk[6][:half], 1), flip(chunk[5][half:], 2)], axis=0)

        near_own = gather_near(centroids.astype(jnp.bfloat16))
        far_own = flip(near_own, top_bit)
        piece = jnp.concatenate([gather_cent(near_own), gather_cent(far_own)], axis=0)
        n_near = piece.shape[0] // 2

        weights, local, row_sqs, rows = [], [], [], []
        for bits in GROUPS:
            weight, stats, row_sq, held = first_pass(piece, [chunk[b] for b in bits])
            weights.append(weight)
            local.append(stats)
            row_sqs.append(row_sq)
            rows.append(held)

        stats = by_chunk(local)
        for bit in (1, 2, 4):
            other = flip(stats, bit)
            stats = merge(stats, jnp.stack([other[:, b ^ bit] for b in range(CUBE)], axis=1))
        scales = []
        for g, bits in enumerate(GROUPS):
            scale = [jnp.exp(local[g][0, i] - stats[0, b]) / stats[1, b] for i, b in enumerate(bits)]
            scales.append(jnp.concatenate(scale)[None, :])

        far = scatter_cent(sums_pass(scales, weights, rows, n_near, 2 * n_near))
        count = far[:, width:]
        coarse = lax.reduce_precision(count, 8, 7)
        lane = lax.broadcasted_iota(jnp.int32, count.shape, 1)
        far = jnp.concatenate([far[:, :width], jnp.where(lane < 64, coarse, count - coarse)], axis=1)
        far = flip(far.astype(jnp.bfloat16), top_bit).astype(jnp.float32)
        near = scatter_cent(sums_pass(scales, weights, rows, 0, n_near))
        counts = near[:, width : width + 1] + (far[:, width : width + 1] + far[:, width + 64 : width + 65])
        sums = scatter_near(jnp.concatenate([near[:, :width] + far[:, :width], jnp.broadcast_to(counts, count.shape)], axis=1))
        updated = (sums[:, :width] + prior_mass * centroids) / (sums[:, width : width + 1] + prior_mass)

        near_own = gather_near(updated.astype(jnp.bfloat16))
        far_own = flip(near_own, top_bit)
        near = second_pass(gather_cent(near_own), row_sqs, rows, shard)
        far = second_pass(gather_cent(far_own), row_sqs, rows, shard)
        stats = merge(by_chunk(near), by_chunk(far))
        for bit in (4, 2, 1):
            stats = merge(stats[:, :bit], flip(stats[:, bit:], bit))
        entropy = (jnp.log(stats[1]) - stats[2] / stats[1]).reshape(shard)
        return (updated, entropy)

    in_specs = (P(("dp", "cent"), None), P(("dp", "cent"), None))
    out_specs = (P(("dp", "cent"), None), P(("dp", "cent")))
    return jax.shard_map(
        on_device, mesh=mesh, in_specs=in_specs, out_specs=out_specs, check_vma=False
    )
```

```python
import functools

import jax
import jax.numpy as jnp
from jax import lax
from jax.experimental import pallas as pl
from jax.experimental.pallas import tpu as pltpu
from jax.sharding import PartitionSpec as P

softness_level = 32.0
prior_mass = 4.0
CUBE = 8
GROUPS = ((0, 1, 2, 4), (3, 5), (6, 7))
VMEM = pl.BlockSpec(memory_space=pltpu.VMEM)
GRANT = 20 << 20


def params():
    return pltpu.CompilerParams(vmem_limit_bytes=GRANT)


def row_squares(rows):
    wide = rows.astype(jnp.float32)
    square = wide * wide
    part = square[:, :128]
    for j in range(128, square.shape[1], 128):
        part = part + square[:, j : j + 128]
    return jnp.sum(part.T, axis=0, keepdims=True)


def centroid_squares(piece):
    wide = piece.astype(jnp.float32)
    return jnp.sum(wide * wide, axis=1, keepdims=True)


def scores(piece, cent_sq, rows, row_sq):
    inner = lax.dot_general(piece, rows, (((1,), (1,)), ((), ())), preferred_element_type=jnp.float32)
    return -(row_sq - 2.0 * inner + cent_sq) * (0.5 / softness_level)


def first_kernel(n, shard, cents, *refs):
    chunks = refs[:n]
    stats_ref, row_sq_ref, rows_ref = refs[n:]
    for i in range(n):
        rows_ref[i * shard : (i + 1) * shard, :] = chunks[i][...]
    piece = cents[...]
    cent_sq = centroid_squares(piece)
    tile = 2 * shard
    for j in range(n // 2):
        span = slice(j * tile, (j + 1) * tile)
        rows = rows_ref[span, :]
        row_sq = row_squares(rows)
        score = scores(piece, cent_sq, rows, row_sq)
        top = jnp.max(score, axis=0, keepdims=True)
        total = jnp.sum(jnp.exp(score - top), axis=0, keepdims=True)
        row_sq_ref[:, span] = row_sq
        for i in range(2):
            stats_ref[0, 2 * j + i : 2 * j + i + 1, :] = top[:, i * shard : (i + 1) * shard]
            stats_ref[1, 2 * j + i : 2 * j + i + 1, :] = total[:, i * shard : (i + 1) * shard]


def first_pass(cents, chunks):
    n = len(chunks)
    shard, width = chunks[0].shape
    n_k = cents.shape[0]
    n_rows = n * shard
    return pl.pallas_call(
        functools.partial(first_kernel, n, shard),
        out_shape=(
            jax.ShapeDtypeStruct((2, n, shard), jnp.float32),
            jax.ShapeDtypeStruct((1, n_rows), jnp.float32),
            jax.ShapeDtypeStruct((n_rows, width), jnp.bfloat16),
        ),
        in_specs=[VMEM] * (1 + n),
        out_specs=(VMEM,) * 3,
        compiler_params=params(),
        cost_estimate=pl.CostEstimate(
            flops=2 * n_k * n_rows * width, bytes_accessed=2 * n_rows * width, transcendentals=n_k * n_rows
        ),
        name="first_pass",
    )(cents, *chunks)


def sums_kernel(first, last, n, cents, *refs):
    stats, row_sqs, rows = refs[:n], refs[n : 2 * n], refs[2 * n : 3 * n]
    out_ref = refs[3 * n]
    width = cents.shape[1]
    piece = cents[first:last, :]
    cent_sq = centroid_squares(piece)
    counts = 0.0
    for s in range(n):
        score = scores(piece, cent_sq, rows[s][...], row_sqs[s][...])
        resp = (jnp.exp(score - stats[s][0:1, :]) / stats[s][1:2, :]).astype(jnp.bfloat16)
        counts = counts + jnp.sum(resp.astype(jnp.float32), axis=1, keepdims=True)
        part = jnp.dot(resp, rows[s][...], preferred_element_type=jnp.float32)
        if s:
            part = part + out_ref[:, :width]
        out_ref[:, :width] = part
    out_ref[:, width:] = jnp.broadcast_to(counts, (last - first, 128))


def sums_pass(cents, stats, row_sqs, rows, first, last):
    n = len(rows)
    width = rows[0].shape[1]
    n_rows = sum(r.shape[0] for r in rows)
    return pl.pallas_call(
        functools.partial(sums_kernel, first, last, n),
        out_shape=jax.ShapeDtypeStruct((last - first, width + 128), jnp.float32),
        in_specs=[VMEM] * (1 + 3 * n),
        out_specs=VMEM,
        compiler_params=params(),
        cost_estimate=pl.CostEstimate(
            flops=4 * (last - first) * n_rows * width,
            bytes_accessed=2 * n_rows * width,
            transcendentals=(last - first) * n_rows,
        ),
        name="sums_pass",
    )(cents, *stats, *row_sqs, *rows)


def second_kernel(shard, n, cents, *refs):
    row_sqs, rows, stats = refs[:n], refs[n : 2 * n], refs[2 * n :]
    piece = cents[...]
    cent_sq = centroid_squares(piece)
    tile = 2 * shard
    for s in range(n):
        for j in range(rows[s].shape[0] // tile):
            span = slice(j * tile, (j + 1) * tile)
            score = scores(piece, cent_sq, rows[s][span, :], row_sqs[s][:, span])
            top = jnp.max(score, axis=0, keepdims=True)
            shifted = score - top
            weight = jnp.exp(shifted)
            total = jnp.sum(weight, axis=0, keepdims=True)
            spread = jnp.sum(weight * shifted, axis=0, keepdims=True)
            for i in range(2):
                part = slice(i * shard, (i + 1) * shard)
                at = slice(2 * j + i, 2 * j + i + 1)
                stats[s][0, at, :] = top[:, part]
                stats[s][1, at, :] = total[:, part]
                stats[s][2, at, :] = spread[:, part]


def second_pass(cents, row_sqs, rows, shard):
    n = len(rows)
    n_k, width = cents.shape
    n_rows = sum(r.shape[0] for r in rows)
    return pl.pallas_call(
        functools.partial(second_kernel, shard, n),
        out_shape=tuple(jax.ShapeDtypeStruct((3, r.shape[0] // shard, shard), jnp.float32) for r in rows),
        in_specs=[VMEM] * (1 + 2 * n),
        out_specs=(VMEM,) * n,
        compiler_params=params(),
        cost_estimate=pl.CostEstimate(
            flops=2 * n_k * n_rows * width, bytes_accessed=2 * n_rows * width, transcendentals=n_k * n_rows
        ),
        name="second_pass",
    )(cents, *row_sqs, *rows)


def hold(*values):
    return lax.optimization_barrier(values)


def merge(a, b):
    top = jnp.maximum(a[0], b[0])
    drops = (a[0] - top, b[0] - top)
    factors = (jnp.exp(drops[0]), jnp.exp(drops[1]))
    out = [top, factors[0] * a[1] + factors[1] * b[1]]
    if a.shape[0] == 3:
        out.append(factors[0] * (a[2] + drops[0] * a[1]) + factors[1] * (b[2] + drops[1] * b[1]))
    return jnp.stack(out)


def by_chunk(groups):
    place = {b: (g, i) for g, bits in enumerate(GROUPS) for i, b in enumerate(bits)}
    return jnp.stack([groups[place[b][0]][:, place[b][1]] for b in range(CUBE)], axis=1)


def solution(mesh):
    n_dp = mesh.shape["dp"]
    n_cent = mesh.shape["cent"]
    top_bit = n_dp // 2

    def flip(value, bits):
        return lax.ppermute(value, "dp", [(i, i ^ bits) for i in range(n_dp)])

    def across(value, bits):
        return lax.ppermute(value, "cent", [(i, i ^ bits) for i in range(n_cent)])

    def gather_cent(value):
        bits = 1
        while bits < n_cent:
            value = jnp.concatenate([value, across(value, bits)], axis=0)
            bits *= 2
        return value

    def scatter_cent(value):
        bits = n_cent // 2
        while bits:
            half = value.shape[0] // 2
            value = value[:half] + across(value[half:], bits)
            bits //= 2
        return value

    def gather_near(value):
        bits = CUBE
        while bits < top_bit:
            value = jnp.concatenate([value, flip(value, bits)], axis=0)
            bits *= 2
        return value

    def scatter_near(value):
        bits = top_bit // 2
        while bits >= CUBE:
            half = value.shape[0] // 2
            value = value[:half] + flip(value[half:], bits)
            bits //= 2
        return value

    def by_position(stats):
        place = lax.axis_index("dp") % CUBE
        for bit in (1, 2, 4):
            swapped = jnp.stack([stats[:, b ^ bit] for b in range(CUBE)], axis=1)
            stats = jnp.where((place & bit) != 0, swapped, stats)
        return stats

    def exchange(value):
        groups = [list(range(i, i + CUBE)) for i in range(0, n_dp, CUBE)]
        return lax.all_to_all(value, "dp", 0, 0, axis_index_groups=groups)

    def everywhere(stats):
        return exchange(jnp.broadcast_to(stats[None], (CUBE,) + stats.shape))

    def to_owner(stats):
        return exchange(stats.transpose(1, 0, 2))

    def on_device(embeddings, centroids):
        shard, width = embeddings.shape
        half = shard // 2
        chunk = {0: embeddings.astype(jnp.bfloat16)}
        for bit in (1, 2, 4):
            chunk[bit] = flip(chunk[0], bit)
        near_own = gather_near(centroids.astype(jnp.bfloat16))
        far_own = flip(near_own, top_bit)
        chunk[3] = flip(chunk[1], 2)
        chunk[6] = flip(chunk[2], 4)
        chunk[5] = flip(chunk[4], 1)
        parts = (flip(chunk[6][:half], 1), flip(chunk[5][half:], 2))
        near = gather_cent(near_own)
        n_near = near.shape[0]
        far_own = hold(far_own, chunk[3], chunk[5], chunk[6])[0]
        piece = jnp.concatenate([near, gather_cent(far_own)], axis=0)
        passes = [first_pass(piece, [chunk[b] for b in bits]) for bits in GROUPS[:2]]
        parts, passes = hold(parts, passes)
        chunk[7] = jnp.concatenate(parts, axis=0)
        passes.append(first_pass(piece, [chunk[b] for b in GROUPS[2]]))
        local, row_sqs, rows = zip(*passes)

        stats = by_position(by_chunk(local))
        stats = everywhere(stats)
        top = jnp.max(stats[:, 0], axis=0)
        total = jnp.sum(stats[:, 1] * jnp.exp(stats[:, 0] - top), axis=0)
        stats = by_position(jnp.stack([top, total]))
        final = [jnp.concatenate([stats[:, b] for b in bits], axis=1) for bits in GROUPS]

        far = scatter_cent(sums_pass(piece, final, row_sqs, rows, n_near, 2 * n_near))
        count = far[:, width:]
        coarse = lax.reduce_precision(count, 8, 7)
        lane = lax.broadcasted_iota(jnp.int32, count.shape, 1)
        far = jnp.concatenate([far[:, :width], jnp.where(lane < 64, coarse, count - coarse)], axis=1)
        far = flip(far.astype(jnp.bfloat16), top_bit).astype(jnp.float32)
        near = scatter_cent(sums_pass(piece, final, row_sqs, rows, 0, n_near))
        counts = near[:, width : width + 1] + (far[:, width : width + 1] + far[:, width + 64 : width + 65])
        sums = scatter_near(jnp.concatenate([near[:, :width] + far[:, :width], jnp.broadcast_to(counts, count.shape)], axis=1))
        updated = (sums[:, :width] + prior_mass * centroids) / (sums[:, width : width + 1] + prior_mass)

        near_own = gather_near(updated.astype(jnp.bfloat16))
        far_own = flip(near_own, top_bit)
        near = second_pass(gather_cent(near_own), row_sqs, rows, shard)
        far_own, near = hold(far_own, near)
        far = second_pass(gather_cent(far_own), row_sqs, rows, shard)
        stats = merge(by_chunk(near), by_chunk(far))
        stats = to_owner(by_position(stats))
        drop = stats[:, 0] - jnp.max(stats[:, 0], axis=0)
        factor = jnp.exp(drop)
        total = jnp.sum(factor * stats[:, 1], axis=0)
        spread = jnp.sum(factor * (stats[:, 2] + drop * stats[:, 1]), axis=0)
        entropy = jnp.log(total) - spread / total
        return (updated, entropy)

    in_specs = (P(("dp", "cent"), None), P(("dp", "cent"), None))
    out_specs = (P(("dp", "cent"), None), P(("dp", "cent")))
    return jax.shard_map(
        on_device, mesh=mesh, in_specs=in_specs, out_specs=out_specs, check_vma=False
    )
```

```python
import functools

import jax
import jax.numpy as jnp
from jax import lax
from jax.experimental import pallas as pl
from jax.experimental.pallas import tpu as pltpu
from jax.sharding import PartitionSpec as P

softness_level = 32.0
prior_mass = 4.0
CUBE = 8
GROUPS = ((0, 1, 2, 4), (3, 5), (6, 7))
VMEM = pl.BlockSpec(memory_space=pltpu.VMEM)
GRANT = 12 << 20


def params():
    return pltpu.CompilerParams(vmem_limit_bytes=GRANT)


def row_squares(rows):
    wide = rows.astype(jnp.float32)
    square = wide * wide
    part = square[:, :128]
    for j in range(128, square.shape[1], 128):
        part = part + square[:, j : j + 128]
    return jnp.sum(part.T, axis=0, keepdims=True)


def centroid_squares(piece):
    wide = piece.astype(jnp.float32)
    return jnp.sum(wide * wide, axis=1, keepdims=True)


def scores(piece, cent_sq, rows, row_sq):
    inner = lax.dot_general(piece, rows, (((1,), (1,)), ((), ())), preferred_element_type=jnp.float32)
    return -(row_sq - 2.0 * inner + cent_sq) * (0.5 / softness_level)


def first_kernel(n, shard, cents, *refs):
    chunks = refs[:n]
    stats_ref, row_sq_ref, rows_ref = refs[n:]
    for i in range(n):
        rows_ref[i * shard : (i + 1) * shard, :] = chunks[i][...]
    piece = cents[...]
    cent_sq = centroid_squares(piece)
    tile = 2 * shard
    for j in range(n // 2):
        span = slice(j * tile, (j + 1) * tile)
        rows = rows_ref[span, :]
        row_sq = row_squares(rows)
        score = scores(piece, cent_sq, rows, row_sq)
        top = jnp.max(score, axis=0, keepdims=True)
        total = jnp.sum(jnp.exp(score - top), axis=0, keepdims=True)
        row_sq_ref[:, span] = row_sq
        for i in range(2):
            stats_ref[0, 2 * j + i : 2 * j + i + 1, :] = top[:, i * shard : (i + 1) * shard]
            stats_ref[1, 2 * j + i : 2 * j + i + 1, :] = total[:, i * shard : (i + 1) * shard]


def first_pass(cents, chunks):
    n = len(chunks)
    shard, width = chunks[0].shape
    n_k = cents.shape[0]
    n_rows = n * shard
    return pl.pallas_call(
        functools.partial(first_kernel, n, shard),
        out_shape=(
            jax.ShapeDtypeStruct((2, n, shard), jnp.float32),
            jax.ShapeDtypeStruct((1, n_rows), jnp.float32),
            jax.ShapeDtypeStruct((n_rows, width), jnp.bfloat16),
        ),
        in_specs=[VMEM] * (1 + n),
        out_specs=(VMEM,) * 3,
        compiler_params=params(),
        cost_estimate=pl.CostEstimate(
            flops=2 * n_k * n_rows * width, bytes_accessed=2 * n_rows * width, transcendentals=n_k * n_rows
        ),
        name="first_pass",
    )(cents, *chunks)


def sums_kernel(first, last, n, cents, *refs):
    stats, row_sqs, rows = refs[:n], refs[n : 2 * n], refs[2 * n : 3 * n]
    out_ref = refs[3 * n]
    width = cents.shape[1]
    piece = cents[first:last, :]
    cent_sq = centroid_squares(piece)
    counts = 0.0
    for s in range(n):
        score = scores(piece, cent_sq, rows[s][...], row_sqs[s][...])
        resp = (jnp.exp(score - stats[s][0:1, :]) / stats[s][1:2, :]).astype(jnp.bfloat16)
        counts = counts + jnp.sum(resp.astype(jnp.float32), axis=1, keepdims=True)
        part = jnp.dot(resp, rows[s][...], preferred_element_type=jnp.float32)
        if s:
            part = part + out_ref[:, :width]
        out_ref[:, :width] = part
    out_ref[:, width:] = jnp.broadcast_to(counts, (last - first, 128))


def sums_pass(cents, stats, row_sqs, rows, first, last):
    n = len(rows)
    width = rows[0].shape[1]
    n_rows = sum(r.shape[0] for r in rows)
    return pl.pallas_call(
        functools.partial(sums_kernel, first, last, n),
        out_shape=jax.ShapeDtypeStruct((last - first, width + 128), jnp.float32),
        in_specs=[VMEM] * (1 + 3 * n),
        out_specs=VMEM,
        compiler_params=params(),
        cost_estimate=pl.CostEstimate(
            flops=4 * (last - first) * n_rows * width,
            bytes_accessed=2 * n_rows * width,
            transcendentals=(last - first) * n_rows,
        ),
        name="sums_pass",
    )(cents, *stats, *row_sqs, *rows)


def second_kernel(shard, n, cents, *refs):
    row_sqs, rows, stats = refs[:n], refs[n : 2 * n], refs[2 * n :]
    piece = cents[...]
    cent_sq = centroid_squares(piece)
    tile = 2 * shard
    for s in range(n):
        for j in range(rows[s].shape[0] // tile):
            span = slice(j * tile, (j + 1) * tile)
            score = scores(piece, cent_sq, rows[s][span, :], row_sqs[s][:, span])
            top = jnp.max(score, axis=0, keepdims=True)
            shifted = score - top
            weight = jnp.exp(shifted)
            total = jnp.sum(weight, axis=0, keepdims=True)
            spread = jnp.sum(weight * shifted, axis=0, keepdims=True)
            for i in range(2):
                part = slice(i * shard, (i + 1) * shard)
                at = slice(2 * j + i, 2 * j + i + 1)
                stats[s][0, at, :] = top[:, part]
                stats[s][1, at, :] = total[:, part]
                stats[s][2, at, :] = spread[:, part]


def second_pass(cents, row_sqs, rows, shard):
    n = len(rows)
    n_k, width = cents.shape
    n_rows = sum(r.shape[0] for r in rows)
    return pl.pallas_call(
        functools.partial(second_kernel, shard, n),
        out_shape=tuple(jax.ShapeDtypeStruct((3, r.shape[0] // shard, shard), jnp.float32) for r in rows),
        in_specs=[VMEM] * (1 + 2 * n),
        out_specs=(VMEM,) * n,
        compiler_params=params(),
        cost_estimate=pl.CostEstimate(
            flops=2 * n_k * n_rows * width, bytes_accessed=2 * n_rows * width, transcendentals=n_k * n_rows
        ),
        name="second_pass",
    )(cents, *row_sqs, *rows)


def hold(*values):
    return lax.optimization_barrier(values)


def merge(a, b):
    top = jnp.maximum(a[0], b[0])
    drops = (a[0] - top, b[0] - top)
    factors = (jnp.exp(drops[0]), jnp.exp(drops[1]))
    out = [top, factors[0] * a[1] + factors[1] * b[1]]
    if a.shape[0] == 3:
        out.append(factors[0] * (a[2] + drops[0] * a[1]) + factors[1] * (b[2] + drops[1] * b[1]))
    return jnp.stack(out)


def by_chunk(groups):
    place = {b: (g, i) for g, bits in enumerate(GROUPS) for i, b in enumerate(bits)}
    return jnp.stack([groups[place[b][0]][:, place[b][1]] for b in range(CUBE)], axis=1)


def solution(mesh):
    n_dp = mesh.shape["dp"]
    n_cent = mesh.shape["cent"]
    top_bit = n_dp // 2

    def flip(value, bits):
        return lax.ppermute(value, "dp", [(i, i ^ bits) for i in range(n_dp)])

    def across(value, bits):
        return lax.ppermute(value, "cent", [(i, i ^ bits) for i in range(n_cent)])

    def gather_cent(value):
        bits = 1
        while bits < n_cent:
            value = jnp.concatenate([value, across(value, bits)], axis=0)
            bits *= 2
        return value

    def scatter_cent(value):
        bits = n_cent // 2
        while bits:
            half = value.shape[0] // 2
            value = value[:half] + across(value[half:], bits)
            bits //= 2
        return value

    def gather_near(value):
        bits = CUBE
        while bits < top_bit:
            value = jnp.concatenate([value, flip(value, bits)], axis=0)
            bits *= 2
        return value

    def scatter_near(value):
        bits = top_bit // 2
        while bits >= CUBE:
            half = value.shape[0] // 2
            value = value[:half] + flip(value[half:], bits)
            bits //= 2
        return value

    def by_position(stats):
        place = lax.axis_index("dp") % CUBE
        for bit in (1, 2, 4):
            swapped = jnp.stack([stats[:, b ^ bit] for b in range(CUBE)], axis=1)
            stats = jnp.where((place & bit) != 0, swapped, stats)
        return stats

    def exchange(value):
        groups = [list(range(i, i + CUBE)) for i in range(0, n_dp, CUBE)]
        return lax.all_to_all(value, "dp", 0, 0, axis_index_groups=groups)

    def everywhere(stats):
        return exchange(jnp.broadcast_to(stats[None], (CUBE,) + stats.shape))

    def to_owner(stats):
        return exchange(stats.transpose(1, 0, 2))

    def on_device(embeddings, centroids):
        shard, width = embeddings.shape
        third = shard // 3
        chunk = {0: embeddings.astype(jnp.bfloat16)}
        for bit in (1, 2, 4):
            chunk[bit] = flip(chunk[0], bit)
        near_own = gather_near(centroids.astype(jnp.bfloat16))
        far_own = flip(near_own, top_bit)
        chunk[3] = flip(chunk[1], 2)
        chunk[6] = flip(chunk[2], 4)
        chunk[5] = flip(chunk[4], 1)
        parts = (
            flip(chunk[6][:third], 1),
            flip(chunk[5][third : 2 * third], 2),
            flip(chunk[3][2 * third :], 4),
        )
        near = gather_cent(near_own)
        n_near = near.shape[0]
        far_own = hold(far_own, chunk[1], chunk[2], chunk[4])[0]
        piece = jnp.concatenate([near, gather_cent(far_own)], axis=0)
        passes = [first_pass(piece, [chunk[b] for b in bits]) for bits in GROUPS[:2]]
        parts, passes = hold(parts, passes)
        chunk[7] = jnp.concatenate(parts, axis=0)
        passes.append(first_pass(piece, [chunk[b] for b in GROUPS[2]]))
        local, row_sqs, rows = zip(*passes)

        stats = by_position(by_chunk(local))
        stats = everywhere(stats)
        top = jnp.max(stats[:, 0], axis=0)
        total = jnp.sum(stats[:, 1] * jnp.exp(stats[:, 0] - top), axis=0)
        stats = by_position(jnp.stack([top, total]))
        final = [jnp.concatenate([stats[:, b] for b in bits], axis=1) for bits in GROUPS]

        far = scatter_cent(sums_pass(piece, final, row_sqs, rows, n_near, 2 * n_near))
        count = far[:, width:]
        coarse = lax.reduce_precision(count, 8, 7)
        lane = lax.broadcasted_iota(jnp.int32, count.shape, 1)
        far = jnp.concatenate([far[:, :width], jnp.where(lane < 64, coarse, count - coarse)], axis=1)
        far = flip(far.astype(jnp.bfloat16), top_bit).astype(jnp.float32)
        near = scatter_cent(sums_pass(piece, final, row_sqs, rows, 0, n_near))
        counts = near[:, width : width + 1] + (far[:, width : width + 1] + far[:, width + 64 : width + 65])
        sums = scatter_near(jnp.concatenate([near[:, :width] + far[:, :width], jnp.broadcast_to(counts, count.shape)], axis=1))
        updated = (sums[:, :width] + prior_mass * centroids) / (sums[:, width : width + 1] + prior_mass)

        near_own = gather_near(updated.astype(jnp.bfloat16))
        far_own = flip(near_own, top_bit)
        near = second_pass(gather_cent(near_own), row_sqs, rows, shard)
        far_own, near = hold(far_own, near)
        far = second_pass(gather_cent(far_own), row_sqs, rows, shard)
        stats = merge(by_chunk(near), by_chunk(far))
        stats = to_owner(by_position(stats))
        drop = stats[:, 0] - jnp.max(stats[:, 0], axis=0)
        factor = jnp.exp(drop)
        total = jnp.sum(factor * stats[:, 1], axis=0)
        spread = jnp.sum(factor * (stats[:, 2] + drop * stats[:, 1]), axis=0)
        entropy = jnp.log(total) - spread / total
        return (updated, entropy)

    in_specs = (P(("dp", "cent"), None), P(("dp", "cent"), None))
    out_specs = (P(("dp", "cent"), None), P(("dp", "cent")))
    return jax.shard_map(
        on_device, mesh=mesh, in_specs=in_specs, out_specs=out_specs, check_vma=False
    )
```

```python
import functools

import jax
import jax.numpy as jnp
from jax import lax
from jax.experimental import pallas as pl
from jax.experimental.pallas import tpu as pltpu
from jax.sharding import PartitionSpec as P

softness_level = 32.0
prior_mass = 4.0
CUBE = 8
GROUPS = ((0, 1, 2, 4), (3, 5, 6, 7))
VMEM = pl.BlockSpec(memory_space=pltpu.VMEM)
HBM = pl.BlockSpec(memory_space=pltpu.HBM)
GRANT = 12 << 20


def params():
    return pltpu.CompilerParams(vmem_limit_bytes=GRANT)


def row_squares(rows):
    wide = rows.astype(jnp.float32)
    square = wide * wide
    part = square[:, :128]
    for j in range(128, square.shape[1], 128):
        part = part + square[:, j : j + 128]
    return jnp.sum(part.T, axis=0, keepdims=True)


def centroid_squares(piece):
    wide = piece.astype(jnp.float32)
    return jnp.sum(wide * wide, axis=1, keepdims=True)


def scores(piece, cent_sq, rows, row_sq):
    inner = lax.dot_general(piece, rows, (((1,), (1,)), ((), ())), preferred_element_type=jnp.float32)
    return -(row_sq - 2.0 * inner + cent_sq) * (0.5 / softness_level)


def fetch(sources, target, sems):
    copies, at = [], 0
    for i, source in enumerate(sources):
        n = source.shape[0]
        copy = pltpu.make_async_copy(source, target.at[pl.ds(at, n)], sems.at[i])
        copy.start()
        copies.append(copy)
        at += n
    return copies


def first_kernel(n, n_blocks, shard, last, *refs):
    blocks, chunks, refs = refs[:n_blocks], refs[n_blocks : n_blocks + n], refs[n_blocks + n :]
    stats_ref, row_sq_ref, rows_ref = refs[:3]
    sems = refs[-1]
    cents, copies = blocks[0], []
    if n_blocks > 1:
        cents, at = refs[3], 0
        for block in blocks:
            cents[at : at + block.shape[0], :] = block[...]
            at += block.shape[0]
    if last:
        for i in range(n):
            rows_ref[i * shard : (i + 1) * shard, :] = chunks[i][...]
    else:
        copies = fetch(chunks, rows_ref, sems)
    piece = cents[...]
    cent_sq = centroid_squares(piece)
    tile = 2 * shard
    for j in range(n // 2):
        for copy in copies[2 * j : 2 * j + 2]:
            copy.wait()
        span = slice(j * tile, (j + 1) * tile)
        rows = rows_ref[span, :]
        row_sq = row_squares(rows)
        score = scores(piece, cent_sq, rows, row_sq)
        top = jnp.max(score, axis=0, keepdims=True)
        total = jnp.sum(jnp.exp(score - top), axis=0, keepdims=True)
        row_sq_ref[:, span] = row_sq
        for i in range(2):
            stats_ref[0, 2 * j + i : 2 * j + i + 1, :] = top[:, i * shard : (i + 1) * shard]
            stats_ref[1, 2 * j + i : 2 * j + i + 1, :] = total[:, i * shard : (i + 1) * shard]


def first_pass(blocks, chunks, last=False):
    n, n_blocks = len(chunks), len(blocks)
    shard, width = chunks[0].shape
    n_k = sum(b.shape[0] for b in blocks)
    n_rows = n * shard
    outs = [
        jax.ShapeDtypeStruct((2, n, shard), jnp.float32),
        jax.ShapeDtypeStruct((1, n_rows), jnp.float32),
        jax.ShapeDtypeStruct((n_rows, width), jnp.bfloat16),
    ]
    if n_blocks > 1:
        outs.append(jax.ShapeDtypeStruct((n_k, width), jnp.bfloat16))
    out = pl.pallas_call(
        functools.partial(first_kernel, n, n_blocks, shard, last),
        out_shape=tuple(outs),
        in_specs=[VMEM] * n_blocks + [VMEM if last else HBM] * n,
        out_specs=(VMEM,) * len(outs),
        scratch_shapes=[pltpu.SemaphoreType.DMA((n,))],
        compiler_params=params(),
        cost_estimate=pl.CostEstimate(
            flops=(16 if n_blocks > 1 else 2) * n_k * n_rows * width,
            bytes_accessed=2 * n_rows * width,
            transcendentals=n_k * n_rows,
        ),
        name="first_pass",
    )(*blocks, *chunks)
    return out[:3], (out[3] if n_blocks > 1 else blocks[0])


def sums_kernel(first, last, n, cents, *refs):
    stats, row_sqs, rows = refs[:n], refs[n : 2 * n], refs[2 * n : 3 * n]
    out_ref = refs[3 * n]
    width = cents.shape[1]
    piece = cents[first:last, :]
    cent_sq = centroid_squares(piece)
    counts = 0.0
    for s in range(n):
        score = scores(piece, cent_sq, rows[s][...], row_sqs[s][...])
        resp = (jnp.exp(score - stats[s][0:1, :]) / stats[s][1:2, :]).astype(jnp.bfloat16)
        counts = counts + jnp.sum(resp.astype(jnp.float32), axis=1, keepdims=True)
        part = jnp.dot(resp, rows[s][...], preferred_element_type=jnp.float32)
        if s:
            part = part + out_ref[:, :width]
        out_ref[:, :width] = part
    out_ref[:, width:] = jnp.broadcast_to(counts, (last - first, 128))


def sums_pass(cents, stats, row_sqs, rows, first, last):
    n = len(rows)
    width = rows[0].shape[1]
    n_rows = sum(r.shape[0] for r in rows)
    return pl.pallas_call(
        functools.partial(sums_kernel, first, last, n),
        out_shape=jax.ShapeDtypeStruct((last - first, width + 128), jnp.float32),
        in_specs=[VMEM] * (1 + 3 * n),
        out_specs=VMEM,
        compiler_params=params(),
        cost_estimate=pl.CostEstimate(
            flops=4 * (last - first) * n_rows * width,
            bytes_accessed=2 * n_rows * width,
            transcendentals=(last - first) * n_rows,
        ),
        name="sums_pass",
    )(cents, *stats, *row_sqs, *rows)


def second_kernel(shard, n, cents, *refs):
    row_sqs, rows, stats = refs[:n], refs[n : 2 * n], refs[2 * n :]
    piece = cents[...]
    cent_sq = centroid_squares(piece)
    tile = 2 * shard
    for s in range(n):
        for j in range(rows[s].shape[0] // tile):
            span = slice(j * tile, (j + 1) * tile)
            score = scores(piece, cent_sq, rows[s][span, :], row_sqs[s][:, span])
            top = jnp.max(score, axis=0, keepdims=True)
            shifted = score - top
            weight = jnp.exp(shifted)
            total = jnp.sum(weight, axis=0, keepdims=True)
            spread = jnp.sum(weight * shifted, axis=0, keepdims=True)
            for i in range(2):
                part = slice(i * shard, (i + 1) * shard)
                at = slice(2 * j + i, 2 * j + i + 1)
                stats[s][0, at, :] = top[:, part]
                stats[s][1, at, :] = total[:, part]
                stats[s][2, at, :] = spread[:, part]


def second_pass(cents, row_sqs, rows, shard):
    n = len(rows)
    n_k, width = cents.shape
    n_rows = sum(r.shape[0] for r in rows)
    out = pl.pallas_call(
        functools.partial(second_kernel, shard, n),
        out_shape=tuple(jax.ShapeDtypeStruct((3, r.shape[0] // shard, shard), jnp.float32) for r in rows),
        in_specs=[VMEM] * (1 + 2 * n),
        out_specs=(VMEM,) * n,
        compiler_params=params(),
        cost_estimate=pl.CostEstimate(
            flops=2 * n_k * n_rows * width, bytes_accessed=2 * n_rows * width, transcendentals=n_k * n_rows
        ),
        name="second_pass",
    )(cents, *row_sqs, *rows)
    return by_chunk(out)


def hold(*values):
    return lax.optimization_barrier(values)


def merge(a, b):
    top = jnp.maximum(a[0], b[0])
    drops = (a[0] - top, b[0] - top)
    factors = (jnp.exp(drops[0]), jnp.exp(drops[1]))
    out = [top, factors[0] * a[1] + factors[1] * b[1]]
    if a.shape[0] == 3:
        out.append(factors[0] * (a[2] + drops[0] * a[1]) + factors[1] * (b[2] + drops[1] * b[1]))
    return jnp.stack(out)


def by_chunk(groups):
    place = {b: (g, i) for g, bits in enumerate(GROUPS) for i, b in enumerate(bits)}
    return jnp.stack([groups[place[b][0]][:, place[b][1]] for b in range(CUBE)], axis=1)


def solution(mesh):
    n_dp = mesh.shape["dp"]
    n_cent = mesh.shape["cent"]
    top_bit = n_dp // 2

    def flip(value, bits):
        return lax.ppermute(value, "dp", [(i, i ^ bits) for i in range(n_dp)])

    def across(value, bits):
        return lax.ppermute(value, "cent", [(i, i ^ bits) for i in range(n_cent)])

    def gather_cent(value):
        blocks = [value]
        bits = 1
        while bits < n_cent:
            blocks = blocks + [across(b, bits) for b in blocks]
            bits *= 2
        return blocks

    def scatter_cent(value):
        bits = n_cent // 2
        while bits:
            half = value.shape[0] // 2
            value = value[:half] + across(value[half:], bits)
            bits //= 2
        return value

    def gather_near(value):
        bits = CUBE
        while bits < top_bit:
            value = jnp.concatenate([value, flip(value, bits)], axis=0)
            bits *= 2
        return value

    def scatter_near(value):
        bits = top_bit // 2
        while bits >= CUBE:
            half = value.shape[0] // 2
            value = value[:half] + flip(value[half:], bits)
            bits //= 2
        return value

    def by_position(stats):
        place = lax.axis_index("dp") % CUBE
        for bit in (1, 2, 4):
            swapped = jnp.stack([stats[:, b ^ bit] for b in range(CUBE)], axis=1)
            stats = jnp.where((place & bit) != 0, swapped, stats)
        return stats

    def exchange(value):
        groups = [list(range(i, i + CUBE)) for i in range(0, n_dp, CUBE)]
        return lax.all_to_all(value, "dp", 0, 0, axis_index_groups=groups)

    def everywhere(stats):
        return exchange(jnp.broadcast_to(stats[None], (CUBE,) + stats.shape))

    def to_owner(stats):
        return exchange(stats.transpose(1, 0, 2))

    def on_device(embeddings, centroids):
        shard, width = embeddings.shape
        per_device = centroids.shape[0]
        cuts = [per_device * 3 // 8] if top_bit == CUBE and per_device % 64 == 0 else []
        half = shard // 2
        chunk = {0: embeddings.astype(jnp.bfloat16)}
        for bit in (1, 2, 4):
            chunk[bit] = flip(chunk[0], bit)
        near_own = gather_near(centroids.astype(jnp.bfloat16))
        far_own = flip(near_own, top_bit)
        chunk[3] = jnp.concatenate([flip(chunk[2][:half], 1), flip(chunk[1][half:], 2)], axis=0)
        chunk[5] = flip(chunk[4], 1)
        chunk[6] = flip(chunk[4], 2)
        chunk[7] = flip(chunk[3], 4)
        near = gather_cent(near_own)
        n_near = len(near) * near_own.shape[0]
        far_own = hold(far_own, chunk[1], chunk[2], chunk[4])[0]
        done, piece = first_pass(near + gather_cent(far_own), [chunk[b] for b in GROUPS[0]])
        chunk[7], done = hold(chunk[7], done)
        passes = [done]
        for bits in GROUPS[1:]:
            passes.append(first_pass([piece], [chunk[b] for b in bits], bits == GROUPS[-1])[0])
        local, row_sqs, rows = zip(*passes)

        stats = by_position(by_chunk(local))
        stats = everywhere(stats)
        top = jnp.max(stats[:, 0], axis=0)
        total = jnp.sum(stats[:, 1] * jnp.exp(stats[:, 0] - top), axis=0)
        stats = by_position(jnp.stack([top, total]))
        final = [jnp.concatenate([stats[:, b] for b in bits], axis=1) for bits in GROUPS]

        far = scatter_cent(sums_pass(piece, final, row_sqs, rows, n_near, 2 * n_near))
        count = far[:, width:]
        coarse = lax.reduce_precision(count, 8, 7)
        lane = lax.broadcasted_iota(jnp.int32, count.shape, 1)
        far = jnp.concatenate([far[:, :width], jnp.where(lane < 64, coarse, count - coarse)], axis=1)
        far = [flip(p, top_bit) for p in jnp.split(far.astype(jnp.bfloat16), cuts, axis=0)]
        near = scatter_cent(sums_pass(piece, final, row_sqs, rows, 0, n_near))
        updated, near_own = [], []
        for p, (here, there) in enumerate(zip(jnp.split(near, cuts, axis=0), far)):
            if p:
                there = hold(there, near_own[-1])[0]
            there = there.astype(jnp.float32)
            counts = there[:, width : width + 1] + there[:, width + 64 : width + 65]
            there = jnp.concatenate([there[:, :width], jnp.broadcast_to(counts, (there.shape[0], 128))], axis=1)
            sums = scatter_near(here + there)
            at = cuts[0] if p else 0
            prior = prior_mass * centroids[at : at + sums.shape[0]]
            updated.append((sums[:, :width] + prior) / (sums[:, width : width + 1] + prior_mass))
            near_own.append(gather_near(updated[-1].astype(jnp.bfloat16)))
        far_own = [flip(p, top_bit) for p in near_own]
        near = [b for p in near_own for b in gather_cent(p)]
        stats = [second_pass(jnp.concatenate(near, axis=0), row_sqs, rows, shard)]
        for p in far_own:
            p, stats[-1] = hold(p, stats[-1]) if p is far_own[-1] else (p, stats[-1])
            stats.append(second_pass(jnp.concatenate(gather_cent(p), axis=0), row_sqs, rows, shard))
        stats = functools.reduce(merge, stats)
        updated = jnp.concatenate(updated, axis=0)
        stats = to_owner(by_position(stats))
        drop = stats[:, 0] - jnp.max(stats[:, 0], axis=0)
        factor = jnp.exp(drop)
        total = jnp.sum(factor * stats[:, 1], axis=0)
        spread = jnp.sum(factor * (stats[:, 2] + drop * stats[:, 1]), axis=0)
        entropy = jnp.log(total) - spread / total
        return (updated, entropy)

    in_specs = (P(("dp", "cent"), None), P(("dp", "cent"), None))
    out_specs = (P(("dp", "cent"), None), P(("dp", "cent")))
    return jax.shard_map(
        on_device, mesh=mesh, in_specs=in_specs, out_specs=out_specs, check_vma=False
    )
```

```python
import functools

import jax
import jax.numpy as jnp
from jax import lax
from jax.experimental import pallas as pl
from jax.experimental.pallas import tpu as pltpu
from jax.sharding import PartitionSpec as P

softness_level = 32.0
prior_mass = 4.0
CUBE = 8
GROUPS = ((0, 1, 2, 4), (3, 5, 6, 7))
VMEM = pl.BlockSpec(memory_space=pltpu.VMEM)
HBM = pl.BlockSpec(memory_space=pltpu.HBM)
GRANT = 12 << 20


def params():
    return pltpu.CompilerParams(vmem_limit_bytes=GRANT)


def row_squares(rows):
    wide = rows.astype(jnp.float32)
    square = wide * wide
    part = square[:, :128]
    for j in range(128, square.shape[1], 128):
        part = part + square[:, j : j + 128]
    return jnp.sum(part.T, axis=0, keepdims=True)


def centroid_squares(piece):
    wide = piece.astype(jnp.float32)
    return jnp.sum(wide * wide, axis=1, keepdims=True)


def scores(piece, cent_sq, rows, row_sq):
    inner = lax.dot_general(piece, rows, (((1,), (1,)), ((), ())), preferred_element_type=jnp.float32)
    return -(row_sq - 2.0 * inner + cent_sq) * (0.5 / softness_level)


def fetch(sources, target, sems):
    copies, at = [], 0
    for i, source in enumerate(sources):
        n = source.shape[0]
        copy = pltpu.make_async_copy(source, target.at[pl.ds(at, n)], sems.at[i])
        copy.start()
        copies.append(copy)
        at += n
    return copies


def first_kernel(n, n_blocks, shard, last, *refs):
    blocks, chunks, refs = refs[:n_blocks], refs[n_blocks : n_blocks + n], refs[n_blocks + n :]
    stats_ref, row_sq_ref, rows_ref = refs[:3]
    sems = refs[-1]
    cents, copies = blocks[0], []
    if n_blocks > 1:
        cents, at = refs[3], 0
        for block in blocks:
            cents[at : at + block.shape[0], :] = block[...]
            at += block.shape[0]
    if last:
        for i in range(n):
            rows_ref[i * shard : (i + 1) * shard, :] = chunks[i][...]
    else:
        copies = fetch(chunks, rows_ref, sems)
    piece = cents[...]
    cent_sq = centroid_squares(piece)
    tile = 2 * shard
    for j in range(n // 2):
        for copy in copies[2 * j : 2 * j + 2]:
            copy.wait()
        span = slice(j * tile, (j + 1) * tile)
        rows = rows_ref[span, :]
        row_sq = row_squares(rows)
        score = scores(piece, cent_sq, rows, row_sq)
        top = jnp.max(score, axis=0, keepdims=True)
        total = jnp.sum(jnp.exp(score - top), axis=0, keepdims=True)
        row_sq_ref[:, span] = row_sq
        for i in range(2):
            stats_ref[0, 2 * j + i : 2 * j + i + 1, :] = top[:, i * shard : (i + 1) * shard]
            stats_ref[1, 2 * j + i : 2 * j + i + 1, :] = total[:, i * shard : (i + 1) * shard]


def first_pass(blocks, chunks, last=False):
    n, n_blocks = len(chunks), len(blocks)
    shard, width = chunks[0].shape
    n_k = sum(b.shape[0] for b in blocks)
    n_rows = n * shard
    outs = [
        jax.ShapeDtypeStruct((2, n, shard), jnp.float32),
        jax.ShapeDtypeStruct((1, n_rows), jnp.float32),
        jax.ShapeDtypeStruct((n_rows, width), jnp.bfloat16),
    ]
    if n_blocks > 1:
        outs.append(jax.ShapeDtypeStruct((n_k, width), jnp.bfloat16))
    out = pl.pallas_call(
        functools.partial(first_kernel, n, n_blocks, shard, last),
        out_shape=tuple(outs),
        in_specs=[VMEM] * n_blocks + [VMEM if last else HBM] * n,
        out_specs=(VMEM,) * len(outs),
        scratch_shapes=[pltpu.SemaphoreType.DMA((n,))],
        compiler_params=params(),
        cost_estimate=pl.CostEstimate(
            flops=(16 if n_blocks > 1 else 2) * n_k * n_rows * width,
            bytes_accessed=2 * n_rows * width,
            transcendentals=n_k * n_rows,
        ),
        name="first_pass",
    )(*blocks, *chunks)
    return out[:3], (out[3] if n_blocks > 1 else blocks[0])


def sums_kernel(first, last, n, cents, *refs):
    stats, row_sqs, rows = refs[:n], refs[n : 2 * n], refs[2 * n : 3 * n]
    out_ref = refs[3 * n]
    width = cents.shape[1]
    piece = cents[first:last, :]
    cent_sq = centroid_squares(piece)
    counts = 0.0
    for s in range(n):
        score = scores(piece, cent_sq, rows[s][...], row_sqs[s][...])
        resp = (jnp.exp(score - stats[s][0:1, :]) / stats[s][1:2, :]).astype(jnp.bfloat16)
        counts = counts + jnp.sum(resp.astype(jnp.float32), axis=1, keepdims=True)
        part = jnp.dot(resp, rows[s][...], preferred_element_type=jnp.float32)
        if s:
            part = part + out_ref[:, :width]
        out_ref[:, :width] = part
    out_ref[:, width:] = jnp.broadcast_to(counts, (last - first, 128))


def sums_pass(cents, stats, row_sqs, rows, first, last):
    n = len(rows)
    width = rows[0].shape[1]
    n_rows = sum(r.shape[0] for r in rows)
    return pl.pallas_call(
        functools.partial(sums_kernel, first, last, n),
        out_shape=jax.ShapeDtypeStruct((last - first, width + 128), jnp.float32),
        in_specs=[VMEM] * (1 + 3 * n),
        out_specs=VMEM,
        compiler_params=params(),
        cost_estimate=pl.CostEstimate(
            flops=4 * (last - first) * n_rows * width,
            bytes_accessed=2 * n_rows * width,
            transcendentals=(last - first) * n_rows,
        ),
        name="sums_pass",
    )(cents, *stats, *row_sqs, *rows)


def second_kernel(shard, n, cents, *refs):
    row_sqs, rows, stats = refs[:n], refs[n : 2 * n], refs[2 * n :]
    piece = cents[...]
    cent_sq = centroid_squares(piece)
    tile = 2 * shard
    for s in range(n):
        for j in range(rows[s].shape[0] // tile):
            span = slice(j * tile, (j + 1) * tile)
            score = scores(piece, cent_sq, rows[s][span, :], row_sqs[s][:, span])
            top = jnp.max(score, axis=0, keepdims=True)
            shifted = score - top
            weight = jnp.exp(shifted)
            total = jnp.sum(weight, axis=0, keepdims=True)
            spread = jnp.sum(weight * shifted, axis=0, keepdims=True)
            for i in range(2):
                part = slice(i * shard, (i + 1) * shard)
                at = slice(2 * j + i, 2 * j + i + 1)
                stats[s][0, at, :] = top[:, part]
                stats[s][1, at, :] = total[:, part]
                stats[s][2, at, :] = spread[:, part]


def second_pass(cents, row_sqs, rows, shard):
    n = len(rows)
    n_k, width = cents.shape
    n_rows = sum(r.shape[0] for r in rows)
    out = pl.pallas_call(
        functools.partial(second_kernel, shard, n),
        out_shape=tuple(jax.ShapeDtypeStruct((3, r.shape[0] // shard, shard), jnp.float32) for r in rows),
        in_specs=[VMEM] * (1 + 2 * n),
        out_specs=(VMEM,) * n,
        compiler_params=params(),
        cost_estimate=pl.CostEstimate(
            flops=2 * n_k * n_rows * width, bytes_accessed=2 * n_rows * width, transcendentals=n_k * n_rows
        ),
        name="second_pass",
    )(cents, *row_sqs, *rows)
    return by_chunk(out)


def hold(*values):
    return lax.optimization_barrier(values)


def merge(a, b):
    top = jnp.maximum(a[0], b[0])
    drops = (a[0] - top, b[0] - top)
    factors = (jnp.exp(drops[0]), jnp.exp(drops[1]))
    out = [top, factors[0] * a[1] + factors[1] * b[1]]
    if a.shape[0] == 3:
        out.append(factors[0] * (a[2] + drops[0] * a[1]) + factors[1] * (b[2] + drops[1] * b[1]))
    return jnp.stack(out)


def by_chunk(groups):
    place = {b: (g, i) for g, bits in enumerate(GROUPS) for i, b in enumerate(bits)}
    return jnp.stack([groups[place[b][0]][:, place[b][1]] for b in range(CUBE)], axis=1)


def solution(mesh):
    n_dp = mesh.shape["dp"]
    n_cent = mesh.shape["cent"]
    top_bit = n_dp // 2

    def flip(value, bits):
        return lax.ppermute(value, "dp", [(i, i ^ bits) for i in range(n_dp)])

    def across(value, bits):
        return lax.ppermute(value, "cent", [(i, i ^ bits) for i in range(n_cent)])

    def gather_cent(value):
        blocks = [value]
        bits = 1
        while bits < n_cent:
            blocks = blocks + [across(b, bits) for b in blocks]
            bits *= 2
        return blocks

    def scatter_cent(value):
        bits = n_cent // 2
        while bits:
            half = value.shape[0] // 2
            value = value[:half] + across(value[half:], bits)
            bits //= 2
        return value

    def gather_near(value):
        bits = CUBE
        while bits < top_bit:
            value = jnp.concatenate([value, flip(value, bits)], axis=0)
            bits *= 2
        return value

    def scatter_near(value):
        bits = top_bit // 2
        while bits >= CUBE:
            half = value.shape[0] // 2
            value = value[:half] + flip(value[half:], bits)
            bits //= 2
        return value

    def by_position(stats):
        place = lax.axis_index("dp") % CUBE
        for bit in (1, 2, 4):
            swapped = jnp.stack([stats[:, b ^ bit] for b in range(CUBE)], axis=1)
            stats = jnp.where((place & bit) != 0, swapped, stats)
        return stats

    def exchange(value):
        groups = [list(range(i, i + CUBE)) for i in range(0, n_dp, CUBE)]
        return lax.all_to_all(value, "dp", 0, 0, axis_index_groups=groups)

    def everywhere(stats):
        return exchange(jnp.broadcast_to(stats[None], (CUBE,) + stats.shape))

    def to_owner(stats):
        return exchange(stats.transpose(1, 0, 2))

    def on_device(embeddings, centroids):
        shard, width = embeddings.shape
        per_device = centroids.shape[0]
        cuts = [per_device * 3 // 8] if top_bit == CUBE and per_device % 64 == 0 else []
        half = shard // 2
        chunk = {0: embeddings.astype(jnp.bfloat16)}
        for bit in (1, 2, 4):
            chunk[bit] = flip(chunk[0], bit)
        near_own = gather_near(centroids.astype(jnp.bfloat16))
        far_own = flip(near_own, top_bit)
        chunk[3] = jnp.concatenate([flip(chunk[2][:half], 1), flip(chunk[1][half:], 2)], axis=0)
        chunk[5] = flip(chunk[4], 1)
        chunk[6] = flip(chunk[4], 2)
        chunk[7] = flip(chunk[3], 4)
        near = gather_cent(near_own)
        n_near = len(near) * near_own.shape[0]
        far_own = hold(far_own, chunk[1], chunk[2], chunk[4])[0]
        done, piece = first_pass(near + gather_cent(far_own), [chunk[b] for b in GROUPS[0]])
        chunk[7], done = hold(chunk[7], done)
        passes = [done]
        for bits in GROUPS[1:]:
            passes.append(first_pass([piece], [chunk[b] for b in bits], bits == GROUPS[-1])[0])
        local, row_sqs, rows = zip(*passes)

        stats = by_position(by_chunk(local))
        stats = everywhere(stats)
        top = jnp.max(stats[:, 0], axis=0)
        total = jnp.sum(stats[:, 1] * jnp.exp(stats[:, 0] - top), axis=0)
        stats = by_position(jnp.stack([top, total]))
        final = [jnp.concatenate([stats[:, b] for b in bits], axis=1) for bits in GROUPS]

        far = scatter_cent(sums_pass(piece, final, row_sqs, rows, n_near, 2 * n_near))
        count = far[:, width:]
        coarse = lax.reduce_precision(count, 8, 7)
        lane = lax.broadcasted_iota(jnp.int32, count.shape, 1)
        far = jnp.concatenate([far[:, :width], jnp.where(lane < 64, coarse, count - coarse)], axis=1)
        far = [flip(p, top_bit) for p in jnp.split(far.astype(jnp.bfloat16), cuts, axis=0)]
        near = scatter_cent(sums_pass(piece, final, row_sqs, rows, 0, n_near))
        updated, near_own = [], []
        for p, (here, there) in enumerate(zip(jnp.split(near, cuts, axis=0), far)):
            if p:
                there = hold(there, near_own[-1])[0]
            there = there.astype(jnp.float32)
            counts = there[:, width : width + 1] + there[:, width + 64 : width + 65]
            there = jnp.concatenate([there[:, :width], jnp.broadcast_to(counts, (there.shape[0], 128))], axis=1)
            sums = scatter_near(here + there)
            at = cuts[0] if p else 0
            prior = prior_mass * centroids[at : at + sums.shape[0]]
            updated.append((sums[:, :width] + prior) / (sums[:, width : width + 1] + prior_mass))
            near_own.append(gather_near(updated[-1].astype(jnp.bfloat16)))
        far_own = [flip(p, top_bit) for p in near_own]
        far_own[0] = hold(far_own[0], near_own[-1])[0]
        near = [b for p in near_own for b in gather_cent(p)]
        stats = [second_pass(jnp.concatenate(near, axis=0), row_sqs, rows, shard)]
        for p in far_own:
            p, stats[-1] = hold(p, stats[-1]) if p is far_own[-1] else (p, stats[-1])
            stats.append(second_pass(jnp.concatenate(gather_cent(p), axis=0), row_sqs, rows, shard))
        stats = functools.reduce(merge, stats)
        updated = jnp.concatenate(updated, axis=0)
        stats = to_owner(by_position(stats))
        drop = stats[:, 0] - jnp.max(stats[:, 0], axis=0)
        factor = jnp.exp(drop)
        total = jnp.sum(factor * stats[:, 1], axis=0)
        spread = jnp.sum(factor * (stats[:, 2] + drop * stats[:, 1]), axis=0)
        entropy = jnp.log(total) - spread / total
        return (updated, entropy)

    in_specs = (P(("dp", "cent"), None), P(("dp", "cent"), None))
    out_specs = (P(("dp", "cent"), None), P(("dp", "cent")))
    return jax.shard_map(
        on_device, mesh=mesh, in_specs=in_specs, out_specs=out_specs, check_vma=False
    )
```

```python
import functools

import jax
import jax.numpy as jnp
from jax import lax
from jax.experimental import pallas as pl
from jax.experimental.pallas import tpu as pltpu
from jax.sharding import PartitionSpec as P

softness_level = 32.0
prior_mass = 4.0
CUBE = 8
GROUPS = ((0, 1, 2, 3), (4, 5), (6, 7))
VMEM = pl.BlockSpec(memory_space=pltpu.VMEM)
HBM = pl.BlockSpec(memory_space=pltpu.HBM)
GRANT = 12 << 20


def params():
    return pltpu.CompilerParams(vmem_limit_bytes=GRANT)


def row_squares(rows):
    wide = rows.astype(jnp.float32)
    square = wide * wide
    part = square[:, :128]
    for j in range(128, square.shape[1], 128):
        part = part + square[:, j : j + 128]
    return jnp.sum(part.T, axis=0, keepdims=True)


def centroid_squares(piece):
    wide = piece.astype(jnp.float32)
    return jnp.sum(wide * wide, axis=1, keepdims=True)


def scores(piece, cent_sq, rows, row_sq):
    inner = lax.dot_general(piece, rows, (((1,), (1,)), ((), ())), preferred_element_type=jnp.float32)
    return -(row_sq - 2.0 * inner + cent_sq) * (0.5 / softness_level)


def fetch(sources, target, sems):
    copies, at = [], 0
    for i, source in enumerate(sources):
        n = source.shape[0]
        copy = pltpu.make_async_copy(source, target.at[pl.ds(at, n)], sems.at[i])
        copy.start()
        copies.append(copy)
        at += n
    return copies


def first_kernel(n, n_blocks, shard, last, *refs):
    blocks, chunks, refs = refs[:n_blocks], refs[n_blocks : n_blocks + n], refs[n_blocks + n :]
    stats_ref, row_sq_ref, rows_ref = refs[:3]
    sems = refs[-1]
    cents, copies = blocks[0], []
    if n_blocks > 1:
        cents, at = refs[3], 0
        for block in blocks:
            cents[at : at + block.shape[0], :] = block[...]
            at += block.shape[0]
    if last:
        for i in range(n):
            rows_ref[i * shard : (i + 1) * shard, :] = chunks[i][...]
    else:
        copies = fetch(chunks, rows_ref, sems)
    piece = cents[...]
    cent_sq = centroid_squares(piece)
    tile = 2 * shard
    for j in range(n // 2):
        for copy in copies[2 * j : 2 * j + 2]:
            copy.wait()
        span = slice(j * tile, (j + 1) * tile)
        rows = rows_ref[span, :]
        row_sq = row_squares(rows)
        score = scores(piece, cent_sq, rows, row_sq)
        top = jnp.max(score, axis=0, keepdims=True)
        total = jnp.sum(jnp.exp(score - top), axis=0, keepdims=True)
        row_sq_ref[:, span] = row_sq
        for i in range(2):
            stats_ref[0, 2 * j + i : 2 * j + i + 1, :] = top[:, i * shard : (i + 1) * shard]
            stats_ref[1, 2 * j + i : 2 * j + i + 1, :] = total[:, i * shard : (i + 1) * shard]


def first_pass(blocks, chunks, last=False):
    n, n_blocks = len(chunks), len(blocks)
    shard, width = chunks[0].shape
    n_k = sum(b.shape[0] for b in blocks)
    n_rows = n * shard
    outs = [
        jax.ShapeDtypeStruct((2, n, shard), jnp.float32),
        jax.ShapeDtypeStruct((1, n_rows), jnp.float32),
        jax.ShapeDtypeStruct((n_rows, width), jnp.bfloat16),
    ]
    if n_blocks > 1:
        outs.append(jax.ShapeDtypeStruct((n_k, width), jnp.bfloat16))
    out = pl.pallas_call(
        functools.partial(first_kernel, n, n_blocks, shard, last),
        out_shape=tuple(outs),
        in_specs=[VMEM] * n_blocks + [VMEM if last else HBM] * n,
        out_specs=(VMEM,) * len(outs),
        scratch_shapes=[pltpu.SemaphoreType.DMA((n,))],
        compiler_params=params(),
        cost_estimate=pl.CostEstimate(
            flops=(16 if n_blocks > 1 else 2) * n_k * n_rows * width,
            bytes_accessed=2 * n_rows * width,
            transcendentals=n_k * n_rows,
        ),
        name="first_pass",
    )(*blocks, *chunks)
    return out[:3], (out[3] if n_blocks > 1 else blocks[0])


def sums_kernel(first, last, n, cents, *refs):
    stats, row_sqs, rows = refs[:n], refs[n : 2 * n], refs[2 * n : 3 * n]
    out_ref = refs[3 * n]
    width = cents.shape[1]
    piece = cents[first:last, :]
    cent_sq = centroid_squares(piece)
    counts = 0.0
    for s in range(n):
        score = scores(piece, cent_sq, rows[s][...], row_sqs[s][...])
        resp = (jnp.exp(score - stats[s][0:1, :]) / stats[s][1:2, :]).astype(jnp.bfloat16)
        counts = counts + jnp.sum(resp.astype(jnp.float32), axis=1, keepdims=True)
        part = jnp.dot(resp, rows[s][...], preferred_element_type=jnp.float32)
        if s:
            part = part + out_ref[:, :width]
        out_ref[:, :width] = part
    out_ref[:, width:] = jnp.broadcast_to(counts, (last - first, 128))


def sums_pass(cents, stats, row_sqs, rows, first, last):
    n = len(rows)
    width = rows[0].shape[1]
    n_rows = sum(r.shape[0] for r in rows)
    return pl.pallas_call(
        functools.partial(sums_kernel, first, last, n),
        out_shape=jax.ShapeDtypeStruct((last - first, width + 128), jnp.float32),
        in_specs=[VMEM] * (1 + 3 * n),
        out_specs=VMEM,
        compiler_params=params(),
        cost_estimate=pl.CostEstimate(
            flops=4 * (last - first) * n_rows * width,
            bytes_accessed=2 * n_rows * width,
            transcendentals=(last - first) * n_rows,
        ),
        name="sums_pass",
    )(cents, *stats, *row_sqs, *rows)


def second_kernel(shard, n, cents, *refs):
    row_sqs, rows, stats = refs[:n], refs[n : 2 * n], refs[2 * n :]
    piece = cents[...]
    cent_sq = centroid_squares(piece)
    tile = 2 * shard
    for s in range(n):
        for j in range(rows[s].shape[0] // tile):
            span = slice(j * tile, (j + 1) * tile)
            score = scores(piece, cent_sq, rows[s][span, :], row_sqs[s][:, span])
            top = jnp.max(score, axis=0, keepdims=True)
            shifted = score - top
            weight = jnp.exp(shifted)
            total = jnp.sum(weight, axis=0, keepdims=True)
            spread = jnp.sum(weight * shifted, axis=0, keepdims=True)
            for i in range(2):
                part = slice(i * shard, (i + 1) * shard)
                at = slice(2 * j + i, 2 * j + i + 1)
                stats[s][0, at, :] = top[:, part]
                stats[s][1, at, :] = total[:, part]
                stats[s][2, at, :] = spread[:, part]


def second_pass(cents, row_sqs, rows, shard):
    n = len(rows)
    n_k, width = cents.shape
    n_rows = sum(r.shape[0] for r in rows)
    out = pl.pallas_call(
        functools.partial(second_kernel, shard, n),
        out_shape=tuple(jax.ShapeDtypeStruct((3, r.shape[0] // shard, shard), jnp.float32) for r in rows),
        in_specs=[VMEM] * (1 + 2 * n),
        out_specs=(VMEM,) * n,
        compiler_params=params(),
        cost_estimate=pl.CostEstimate(
            flops=2 * n_k * n_rows * width, bytes_accessed=2 * n_rows * width, transcendentals=n_k * n_rows
        ),
        name="second_pass",
    )(cents, *row_sqs, *rows)
    return by_chunk(out)


def hold(*values):
    return lax.optimization_barrier(values)


def merge(a, b):
    top = jnp.maximum(a[0], b[0])
    drops = (a[0] - top, b[0] - top)
    factors = (jnp.exp(drops[0]), jnp.exp(drops[1]))
    out = [top, factors[0] * a[1] + factors[1] * b[1]]
    if a.shape[0] == 3:
        out.append(factors[0] * (a[2] + drops[0] * a[1]) + factors[1] * (b[2] + drops[1] * b[1]))
    return jnp.stack(out)


def by_chunk(groups):
    place = {b: (g, i) for g, bits in enumerate(GROUPS) for i, b in enumerate(bits)}
    return jnp.stack([groups[place[b][0]][:, place[b][1]] for b in range(CUBE)], axis=1)


def solution(mesh):
    n_dp = mesh.shape["dp"]
    n_cent = mesh.shape["cent"]
    high = n_dp // 2
    top_bit = n_dp // 4

    def flip(value, bits):
        return lax.ppermute(value, "dp", [(i, i ^ bits) for i in range(n_dp)])

    def member(place):
        return (place & 3) | (high if place & 4 else 0)

    def rows_from(value, place):
        return flip(value, member(place))

    def across(value, bits):
        return lax.ppermute(value, "cent", [(i, i ^ bits) for i in range(n_cent)])

    def gather_cent(value):
        blocks = [value]
        bits = 1
        while bits < n_cent:
            blocks = blocks + [across(b, bits) for b in blocks]
            bits *= 2
        return blocks

    def scatter_cent(value):
        bits = n_cent // 2
        while bits:
            half = value.shape[0] // 2
            value = value[:half] + across(value[half:], bits)
            bits //= 2
        return value

    def gather_near(value):
        bits = 4
        while bits < top_bit:
            value = jnp.concatenate([value, flip(value, bits)], axis=0)
            bits *= 2
        return value

    def scatter_near(value):
        bits = top_bit // 2
        while bits >= 4:
            half = value.shape[0] // 2
            value = value[:half] + flip(value[half:], bits)
            bits //= 2
        return value

    def by_position(stats):
        place = lax.axis_index("dp")
        for bit in (1, 2, 4):
            swapped = jnp.stack([stats[:, b ^ bit] for b in range(CUBE)], axis=1)
            stats = jnp.where((place & member(bit)) != 0, swapped, stats)
        return stats

    def exchange(value):
        groups = [[i + member(place) for place in range(CUBE)] for i in range(0, high, 4)]
        return lax.all_to_all(value, "dp", 0, 0, axis_index_groups=groups)

    def everywhere(stats):
        return exchange(jnp.broadcast_to(stats[None], (CUBE,) + stats.shape))

    def to_owner(stats):
        return exchange(stats.transpose(1, 0, 2))

    def on_device(embeddings, centroids):
        shard, width = embeddings.shape
        half = shard // 2
        chunk = {0: embeddings.astype(jnp.bfloat16)}
        for bit in (4, 1, 2):
            chunk[bit] = rows_from(chunk[0], bit)
        near_own = gather_near(centroids.astype(jnp.bfloat16))
        far_own = flip(near_own, top_bit)
        chunk[3] = rows_from(chunk[1], 2)
        chunk[4], chunk[3], chunk[2], far_own = hold(chunk[4], chunk[3], chunk[2], far_own)
        chunk[5] = rows_from(chunk[4], 1)
        chunk[6] = rows_from(chunk[4], 2)
        near = gather_cent(near_own)
        n_near = len(near) * near_own.shape[0]
        done, piece = first_pass(near + gather_cent(far_own), [chunk[b] for b in GROUPS[0]])
        chunk[5], chunk[6], done = hold(chunk[5], chunk[6], done)
        parts = (rows_from(chunk[6][:half], 1), rows_from(chunk[5][half:], 2))
        passes = [done, first_pass([piece], [chunk[b] for b in GROUPS[1]])[0]]
        parts, passes = hold(parts, passes)
        chunk[7] = jnp.concatenate(parts, axis=0)
        passes.append(first_pass([piece], [chunk[b] for b in GROUPS[2]], True)[0])
        local, row_sqs, rows = zip(*passes)

        stats = by_position(by_chunk(local))
        stats = everywhere(stats)
        top = jnp.max(stats[:, 0], axis=0)
        total = jnp.sum(stats[:, 1] * jnp.exp(stats[:, 0] - top), axis=0)
        stats = by_position(jnp.stack([top, total]))
        final = [jnp.concatenate([stats[:, b] for b in bits], axis=1) for bits in GROUPS]

        far = scatter_cent(sums_pass(piece, final, row_sqs, rows, n_near, 2 * n_near))
        count = far[:, width:]
        coarse = lax.reduce_precision(count, 8, 7)
        lane = lax.broadcasted_iota(jnp.int32, count.shape, 1)
        far = jnp.concatenate([far[:, :width], jnp.where(lane < 64, coarse, count - coarse)], axis=1)
        far = flip(far.astype(jnp.bfloat16), top_bit).astype(jnp.float32)
        near = scatter_cent(sums_pass(piece, final, row_sqs, rows, 0, n_near))
        counts = far[:, width : width + 1] + far[:, width + 64 : width + 65]
        far = jnp.concatenate([far[:, :width], jnp.broadcast_to(counts, count.shape)], axis=1)
        sums = scatter_near(near + far)
        updated = (sums[:, :width] + prior_mass * centroids) / (sums[:, width : width + 1] + prior_mass)
        near_own = gather_near(updated.astype(jnp.bfloat16))
        far_own = flip(near_own, top_bit)
        stats = second_pass(jnp.concatenate(gather_cent(near_own), axis=0), row_sqs, rows, shard)
        far_own, stats = hold(far_own, stats)
        far = gather_cent(far_own)
        stats = merge(stats, second_pass(far_own, row_sqs, rows, shard))
        stats = merge(stats, second_pass(jnp.concatenate(far[1:], axis=0), row_sqs, rows, shard))
        stats = to_owner(by_position(stats))
        drop = stats[:, 0] - jnp.max(stats[:, 0], axis=0)
        factor = jnp.exp(drop)
        total = jnp.sum(factor * stats[:, 1], axis=0)
        spread = jnp.sum(factor * (stats[:, 2] + drop * stats[:, 1]), axis=0)
        entropy = jnp.log(total) - spread / total
        return (updated, entropy)

    in_specs = (P(("dp", "cent"), None), P(("dp", "cent"), None))
    out_specs = (P(("dp", "cent"), None), P(("dp", "cent")))
    return jax.shard_map(
        on_device, mesh=mesh, in_specs=in_specs, out_specs=out_specs, check_vma=False
    )
```

```python
import functools

import jax
import jax.numpy as jnp
from jax import lax
from jax.experimental import pallas as pl
from jax.experimental.pallas import tpu as pltpu
from jax.sharding import PartitionSpec as P

softness_level = 32.0
prior_mass = 4.0
CUBE = 8
GROUPS = ((0, 1, 2, 3), (4, 5), (6, 7))
VMEM = pl.BlockSpec(memory_space=pltpu.VMEM)
HBM = pl.BlockSpec(memory_space=pltpu.HBM)
GRANT = 12 << 20


def params():
    return pltpu.CompilerParams(vmem_limit_bytes=GRANT)


def row_squares(rows):
    wide = rows.astype(jnp.float32)
    square = wide * wide
    part = square[:, :128]
    for j in range(128, square.shape[1], 128):
        part = part + square[:, j : j + 128]
    return jnp.sum(part.T, axis=0, keepdims=True)


def centroid_squares(piece):
    wide = piece.astype(jnp.float32)
    return jnp.sum(wide * wide, axis=1, keepdims=True)


def scores(piece, cent_sq, rows, row_sq):
    inner = lax.dot_general(piece, rows, (((1,), (1,)), ((), ())), preferred_element_type=jnp.float32)
    return -(row_sq - 2.0 * inner + cent_sq) * (0.5 / softness_level)


def fetch(sources, target, sems):
    copies, at = [], 0
    for i, source in enumerate(sources):
        n = source.shape[0]
        copy = pltpu.make_async_copy(source, target.at[pl.ds(at, n)], sems.at[i])
        copy.start()
        copies.append(copy)
        at += n
    return copies


def first_kernel(n, n_blocks, shard, last, *refs):
    blocks, chunks, refs = refs[:n_blocks], refs[n_blocks : n_blocks + n], refs[n_blocks + n :]
    stats_ref, row_sq_ref, rows_ref = refs[:3]
    sems = refs[-1]
    cents, copies = blocks[0], []
    if n_blocks > 1:
        cents, at = refs[3], 0
        for block in blocks:
            cents[at : at + block.shape[0], :] = block[...]
            at += block.shape[0]
    if last:
        for i in range(n):
            rows_ref[i * shard : (i + 1) * shard, :] = chunks[i][...]
    else:
        copies = fetch(chunks, rows_ref, sems)
    piece = cents[...]
    cent_sq = centroid_squares(piece)
    tile = 2 * shard
    for j in range(n // 2):
        for copy in copies[2 * j : 2 * j + 2]:
            copy.wait()
        span = slice(j * tile, (j + 1) * tile)
        rows = rows_ref[span, :]
        row_sq = row_squares(rows)
        score = scores(piece, cent_sq, rows, row_sq)
        top = jnp.max(score, axis=0, keepdims=True)
        total = jnp.sum(jnp.exp(score - top), axis=0, keepdims=True)
        row_sq_ref[:, span] = row_sq
        for i in range(2):
            stats_ref[0, 2 * j + i : 2 * j + i + 1, :] = top[:, i * shard : (i + 1) * shard]
            stats_ref[1, 2 * j + i : 2 * j + i + 1, :] = total[:, i * shard : (i + 1) * shard]


def first_pass(blocks, chunks, last=False):
    n, n_blocks = len(chunks), len(blocks)
    shard, width = chunks[0].shape
    n_k = sum(b.shape[0] for b in blocks)
    n_rows = n * shard
    outs = [
        jax.ShapeDtypeStruct((2, n, shard), jnp.float32),
        jax.ShapeDtypeStruct((1, n_rows), jnp.float32),
        jax.ShapeDtypeStruct((n_rows, width), jnp.bfloat16),
    ]
    if n_blocks > 1:
        outs.append(jax.ShapeDtypeStruct((n_k, width), jnp.bfloat16))
    out = pl.pallas_call(
        functools.partial(first_kernel, n, n_blocks, shard, last),
        out_shape=tuple(outs),
        in_specs=[VMEM] * n_blocks + [VMEM if last else HBM] * n,
        out_specs=(VMEM,) * len(outs),
        scratch_shapes=[pltpu.SemaphoreType.DMA((n,))],
        compiler_params=params(),
        cost_estimate=pl.CostEstimate(
            flops=2 * n_k * n_rows * width,
            bytes_accessed=2 * n_rows * width,
            transcendentals=n_k * n_rows,
        ),
        name="first_pass",
    )(*blocks, *chunks)
    return out[:3], (out[3] if n_blocks > 1 else blocks[0])


def sums_kernel(first, last, n, cents, *refs):
    stats, row_sqs, rows = refs[:n], refs[n : 2 * n], refs[2 * n : 3 * n]
    out_ref = refs[3 * n]
    width = cents.shape[1]
    piece = cents[first:last, :]
    cent_sq = centroid_squares(piece)
    counts = 0.0
    for s in range(n):
        score = scores(piece, cent_sq, rows[s][...], row_sqs[s][...])
        resp = (jnp.exp(score - stats[s][0:1, :]) / stats[s][1:2, :]).astype(jnp.bfloat16)
        counts = counts + jnp.sum(resp.astype(jnp.float32), axis=1, keepdims=True)
        part = jnp.dot(resp, rows[s][...], preferred_element_type=jnp.float32)
        if s:
            part = part + out_ref[:, :width]
        out_ref[:, :width] = part
    out_ref[:, width:] = jnp.broadcast_to(counts, (last - first, 128))


def sums_pass(cents, stats, row_sqs, rows, first, last):
    n = len(rows)
    width = rows[0].shape[1]
    n_rows = sum(r.shape[0] for r in rows)
    return pl.pallas_call(
        functools.partial(sums_kernel, first, last, n),
        out_shape=jax.ShapeDtypeStruct((last - first, width + 128), jnp.float32),
        in_specs=[VMEM] * (1 + 3 * n),
        out_specs=VMEM,
        compiler_params=params(),
        cost_estimate=pl.CostEstimate(
            flops=4 * (last - first) * n_rows * width,
            bytes_accessed=2 * n_rows * width,
            transcendentals=(last - first) * n_rows,
        ),
        name="sums_pass",
    )(cents, *stats, *row_sqs, *rows)


def second_kernel(shard, n, cents, *refs):
    row_sqs, rows, stats = refs[:n], refs[n : 2 * n], refs[2 * n :]
    piece = cents[...]
    cent_sq = centroid_squares(piece)
    tile = 2 * shard
    for s in range(n):
        for j in range(rows[s].shape[0] // tile):
            span = slice(j * tile, (j + 1) * tile)
            score = scores(piece, cent_sq, rows[s][span, :], row_sqs[s][:, span])
            top = jnp.max(score, axis=0, keepdims=True)
            shifted = score - top
            weight = jnp.exp(shifted)
            total = jnp.sum(weight, axis=0, keepdims=True)
            spread = jnp.sum(weight * shifted, axis=0, keepdims=True)
            for i in range(2):
                part = slice(i * shard, (i + 1) * shard)
                at = slice(2 * j + i, 2 * j + i + 1)
                stats[s][0, at, :] = top[:, part]
                stats[s][1, at, :] = total[:, part]
                stats[s][2, at, :] = spread[:, part]


def second_pass(cents, row_sqs, rows, shard):
    n = len(rows)
    n_k, width = cents.shape
    n_rows = sum(r.shape[0] for r in rows)
    out = pl.pallas_call(
        functools.partial(second_kernel, shard, n),
        out_shape=tuple(jax.ShapeDtypeStruct((3, r.shape[0] // shard, shard), jnp.float32) for r in rows),
        in_specs=[VMEM] * (1 + 2 * n),
        out_specs=(VMEM,) * n,
        compiler_params=params(),
        cost_estimate=pl.CostEstimate(
            flops=2 * n_k * n_rows * width, bytes_accessed=2 * n_rows * width, transcendentals=n_k * n_rows
        ),
        name="second_pass",
    )(cents, *row_sqs, *rows)
    return by_chunk(out)


def hold(*values):
    return lax.optimization_barrier(values)


def merge(a, b):
    top = jnp.maximum(a[0], b[0])
    drops = (a[0] - top, b[0] - top)
    factors = (jnp.exp(drops[0]), jnp.exp(drops[1]))
    out = [top, factors[0] * a[1] + factors[1] * b[1]]
    if a.shape[0] == 3:
        out.append(factors[0] * (a[2] + drops[0] * a[1]) + factors[1] * (b[2] + drops[1] * b[1]))
    return jnp.stack(out)


def by_chunk(groups):
    place = {b: (g, i) for g, bits in enumerate(GROUPS) for i, b in enumerate(bits)}
    return jnp.stack([groups[place[b][0]][:, place[b][1]] for b in range(CUBE)], axis=1)


def solution(mesh):
    n_dp = mesh.shape["dp"]
    n_cent = mesh.shape["cent"]
    high = n_dp // 2
    top_bit = n_dp // 4

    def flip(value, bits):
        return lax.ppermute(value, "dp", [(i, i ^ bits) for i in range(n_dp)])

    def member(place):
        return (place & 3) | (high if place & 4 else 0)

    def rows_from(value, place):
        return flip(value, member(place))

    def across(value, bits):
        return lax.ppermute(value, "cent", [(i, i ^ bits) for i in range(n_cent)])

    def gather_cent(value):
        blocks = [value]
        bits = 1
        while bits < n_cent:
            blocks = blocks + [across(b, bits) for b in blocks]
            bits *= 2
        return blocks

    def scatter_cent(value):
        bits = n_cent // 2
        while bits:
            half = value.shape[0] // 2
            value = value[:half] + across(value[half:], bits)
            bits //= 2
        return value

    def gather_near(value):
        bits = 4
        while bits < top_bit:
            value = jnp.concatenate([value, flip(value, bits)], axis=0)
            bits *= 2
        return value

    def scatter_near(value):
        bits = top_bit // 2
        while bits >= 4:
            half = value.shape[0] // 2
            value = value[:half] + flip(value[half:], bits)
            bits //= 2
        return value

    def by_position(stats):
        place = lax.axis_index("dp")
        for bit in (1, 2, 4):
            swapped = jnp.stack([stats[:, b ^ bit] for b in range(CUBE)], axis=1)
            stats = jnp.where((place & member(bit)) != 0, swapped, stats)
        return stats

    def exchange(value):
        groups = [[i + member(place) for place in range(CUBE)] for i in range(0, high, 4)]
        return lax.all_to_all(value, "dp", 0, 0, axis_index_groups=groups)

    def everywhere(stats):
        return exchange(jnp.broadcast_to(stats[None], (CUBE,) + stats.shape))

    def to_owner(stats):
        return exchange(stats.transpose(1, 0, 2))

    def on_device(embeddings, centroids):
        shard, width = embeddings.shape
        half = shard // 2
        chunk = {0: embeddings.astype(jnp.bfloat16)}
        for bit in (4, 1, 2):
            chunk[bit] = rows_from(chunk[0], bit)
        chunk[3] = rows_from(chunk[1], 2)
        near_own = gather_near(centroids.astype(jnp.bfloat16))
        far_own = flip(near_own, top_bit)
        chunk[4], chunk[3], chunk[2] = hold(chunk[4], chunk[3], chunk[2])
        chunk[5] = rows_from(chunk[4], 1)
        chunk[6] = rows_from(chunk[4], 2)
        parts = (rows_from(chunk[3][:half], 4), rows_from(chunk[4][half:], 3))
        near = gather_cent(near_own)
        n_near = len(near) * near_own.shape[0]
        done, piece = first_pass(near + gather_cent(far_own), [chunk[b] for b in GROUPS[0]])
        passes = [done, first_pass([piece], [chunk[b] for b in GROUPS[1]])[0]]
        parts, passes = hold(parts, passes)
        chunk[7] = jnp.concatenate(parts, axis=0)
        passes.append(first_pass([piece], [chunk[b] for b in GROUPS[2]], True)[0])
        local, row_sqs, rows = zip(*passes)

        stats = by_position(by_chunk(local))
        stats = everywhere(stats)
        top = jnp.max(stats[:, 0], axis=0)
        total = jnp.sum(stats[:, 1] * jnp.exp(stats[:, 0] - top), axis=0)
        stats = by_position(jnp.stack([top, total]))
        final = [jnp.concatenate([stats[:, b] for b in bits], axis=1) for bits in GROUPS]

        far = scatter_cent(sums_pass(piece, final, row_sqs, rows, n_near, 2 * n_near))
        count = far[:, width:]
        coarse = lax.reduce_precision(count, 8, 7)
        lane = lax.broadcasted_iota(jnp.int32, count.shape, 1)
        far = jnp.concatenate([far[:, :width], jnp.where(lane < 64, coarse, count - coarse)], axis=1)
        far = flip(far.astype(jnp.bfloat16), top_bit).astype(jnp.float32)
        near = scatter_cent(sums_pass(piece, final, row_sqs, rows, 0, n_near))
        counts = far[:, width : width + 1] + far[:, width + 64 : width + 65]
        far = jnp.concatenate([far[:, :width], jnp.broadcast_to(counts, count.shape)], axis=1)
        sums = scatter_near(near + far)
        updated = (sums[:, :width] + prior_mass * centroids) / (sums[:, width : width + 1] + prior_mass)
        near_own = gather_near(updated.astype(jnp.bfloat16))
        far_own = flip(near_own, top_bit)
        stats = second_pass(jnp.concatenate(gather_cent(near_own), axis=0), row_sqs, rows, shard)
        far_own, stats = hold(far_own, stats)
        far = gather_cent(far_own)
        stats = merge(stats, second_pass(far_own, row_sqs, rows, shard))
        stats = merge(stats, second_pass(jnp.concatenate(far[1:], axis=0), row_sqs, rows, shard))
        stats = to_owner(by_position(stats))
        drop = stats[:, 0] - jnp.max(stats[:, 0], axis=0)
        factor = jnp.exp(drop)
        total = jnp.sum(factor * stats[:, 1], axis=0)
        spread = jnp.sum(factor * (stats[:, 2] + drop * stats[:, 1]), axis=0)
        entropy = jnp.log(total) - spread / total
        return (updated, entropy)

    in_specs = (P(("dp", "cent"), None), P(("dp", "cent"), None))
    out_specs = (P(("dp", "cent"), None), P(("dp", "cent")))
    return jax.shard_map(
        on_device, mesh=mesh, in_specs=in_specs, out_specs=out_specs, check_vma=False
    )
```

```python
import functools

import jax
import jax.numpy as jnp
from jax import lax
from jax.experimental import pallas as pl
from jax.experimental.pallas import tpu as pltpu
from jax.sharding import PartitionSpec as P

softness_level = 32.0
prior_mass = 4.0
CUBE = 8
GROUPS = ((0, 1, 2, 3), (4, 5), (6, 7))
VMEM = pl.BlockSpec(memory_space=pltpu.VMEM)
HBM = pl.BlockSpec(memory_space=pltpu.HBM)
GRANT = 12 << 20


def params():
    return pltpu.CompilerParams(vmem_limit_bytes=GRANT)


def row_squares(rows):
    wide = rows.astype(jnp.float32)
    square = wide * wide
    part = square[:, :128]
    for j in range(128, square.shape[1], 128):
        part = part + square[:, j : j + 128]
    return jnp.sum(part.T, axis=0, keepdims=True)


def centroid_squares(piece):
    wide = piece.astype(jnp.float32)
    return jnp.sum(wide * wide, axis=1, keepdims=True)


def scores(piece, cent_sq, rows, row_sq):
    inner = lax.dot_general(piece, rows, (((1,), (1,)), ((), ())), preferred_element_type=jnp.float32)
    return -(row_sq - 2.0 * inner + cent_sq) * (0.5 / softness_level)


def fetch(sources, target, sems):
    copies, at = [], 0
    for i, source in enumerate(sources):
        n = source.shape[0]
        copy = pltpu.make_async_copy(source, target.at[pl.ds(at, n)], sems.at[i])
        copy.start()
        copies.append(copy)
        at += n
    return copies


def first_kernel(n, n_blocks, n_chunks, shard, last, *refs):
    blocks, chunks, refs = refs[:n_blocks], refs[n_blocks : n_blocks + n_chunks], refs[n_blocks + n_chunks :]
    stats_ref, row_sq_ref, rows_ref = refs[:3]
    sems = refs[-1]
    cents, copies = blocks[0], []
    if n_blocks > 1:
        cents, at = refs[3], 0
        for block in blocks:
            cents[at : at + block.shape[0], :] = block[...]
            at += block.shape[0]
    if last:
        at = 0
        for chunk in chunks:
            rows_ref[at : at + chunk.shape[0], :] = chunk[...]
            at += chunk.shape[0]
    else:
        copies = fetch(chunks, rows_ref, sems)
    piece = cents[...]
    cent_sq = centroid_squares(piece)
    tile = 2 * shard
    for j in range(n // 2):
        for copy in copies[2 * j : 2 * j + 2]:
            copy.wait()
        span = slice(j * tile, (j + 1) * tile)
        rows = rows_ref[span, :]
        row_sq = row_squares(rows)
        score = scores(piece, cent_sq, rows, row_sq)
        top = jnp.max(score, axis=0, keepdims=True)
        total = jnp.sum(jnp.exp(score - top), axis=0, keepdims=True)
        row_sq_ref[:, span] = row_sq
        for i in range(2):
            stats_ref[0, 2 * j + i : 2 * j + i + 1, :] = top[:, i * shard : (i + 1) * shard]
            stats_ref[1, 2 * j + i : 2 * j + i + 1, :] = total[:, i * shard : (i + 1) * shard]


def first_pass(blocks, chunks, last=False):
    n_blocks, n_chunks = len(blocks), len(chunks)
    shard, width = chunks[0].shape
    n_k = sum(b.shape[0] for b in blocks)
    n_rows = sum(c.shape[0] for c in chunks)
    n = n_rows // shard
    outs = [
        jax.ShapeDtypeStruct((2, n, shard), jnp.float32),
        jax.ShapeDtypeStruct((1, n_rows), jnp.float32),
        jax.ShapeDtypeStruct((n_rows, width), jnp.bfloat16),
    ]
    if n_blocks > 1:
        outs.append(jax.ShapeDtypeStruct((n_k, width), jnp.bfloat16))
    out = pl.pallas_call(
        functools.partial(first_kernel, n, n_blocks, n_chunks, shard, last),
        out_shape=tuple(outs),
        in_specs=[VMEM] * n_blocks + [VMEM if last else HBM] * n_chunks,
        out_specs=(VMEM,) * len(outs),
        scratch_shapes=[pltpu.SemaphoreType.DMA((n_chunks,))],
        compiler_params=params(),
        cost_estimate=pl.CostEstimate(
            flops=2 * n_k * n_rows * width,
            bytes_accessed=2 * n_rows * width,
            transcendentals=n_k * n_rows,
        ),
        name="first_pass",
    )(*blocks, *chunks)
    return out[:3], (out[3] if n_blocks > 1 else blocks[0])


def sums_kernel(first, last, n, cents, *refs):
    stats, row_sqs, rows = refs[:n], refs[n : 2 * n], refs[2 * n : 3 * n]
    out_ref = refs[3 * n]
    width = cents.shape[1]
    piece = cents[first:last, :]
    cent_sq = centroid_squares(piece)
    counts = 0.0
    for s in range(n):
        score = scores(piece, cent_sq, rows[s][...], row_sqs[s][...])
        resp = (jnp.exp(score - stats[s][0:1, :]) / stats[s][1:2, :]).astype(jnp.bfloat16)
        counts = counts + jnp.sum(resp.astype(jnp.float32), axis=1, keepdims=True)
        part = jnp.dot(resp, rows[s][...], preferred_element_type=jnp.float32)
        if s:
            part = part + out_ref[:, :width]
        out_ref[:, :width] = part
    out_ref[:, width:] = jnp.broadcast_to(counts, (last - first, 128))


def sums_pass(cents, stats, row_sqs, rows, first, last):
    n = len(rows)
    width = rows[0].shape[1]
    n_rows = sum(r.shape[0] for r in rows)
    return pl.pallas_call(
        functools.partial(sums_kernel, first, last, n),
        out_shape=jax.ShapeDtypeStruct((last - first, width + 128), jnp.float32),
        in_specs=[VMEM] * (1 + 3 * n),
        out_specs=VMEM,
        compiler_params=params(),
        cost_estimate=pl.CostEstimate(
            flops=4 * (last - first) * n_rows * width,
            bytes_accessed=2 * n_rows * width,
            transcendentals=(last - first) * n_rows,
        ),
        name="sums_pass",
    )(cents, *stats, *row_sqs, *rows)


def second_kernel(shard, n, cents, *refs):
    row_sqs, rows, stats = refs[:n], refs[n : 2 * n], refs[2 * n :]
    piece = cents[...]
    cent_sq = centroid_squares(piece)
    tile = 2 * shard
    for s in range(n):
        for j in range(rows[s].shape[0] // tile):
            span = slice(j * tile, (j + 1) * tile)
            score = scores(piece, cent_sq, rows[s][span, :], row_sqs[s][:, span])
            top = jnp.max(score, axis=0, keepdims=True)
            shifted = score - top
            weight = jnp.exp(shifted)
            total = jnp.sum(weight, axis=0, keepdims=True)
            spread = jnp.sum(weight * shifted, axis=0, keepdims=True)
            for i in range(2):
                part = slice(i * shard, (i + 1) * shard)
                at = slice(2 * j + i, 2 * j + i + 1)
                stats[s][0, at, :] = top[:, part]
                stats[s][1, at, :] = total[:, part]
                stats[s][2, at, :] = spread[:, part]


def second_pass(cents, row_sqs, rows, shard):
    n = len(rows)
    n_k, width = cents.shape
    n_rows = sum(r.shape[0] for r in rows)
    out = pl.pallas_call(
        functools.partial(second_kernel, shard, n),
        out_shape=tuple(jax.ShapeDtypeStruct((3, r.shape[0] // shard, shard), jnp.float32) for r in rows),
        in_specs=[VMEM] * (1 + 2 * n),
        out_specs=(VMEM,) * n,
        compiler_params=params(),
        cost_estimate=pl.CostEstimate(
            flops=2 * n_k * n_rows * width, bytes_accessed=2 * n_rows * width, transcendentals=n_k * n_rows
        ),
        name="second_pass",
    )(cents, *row_sqs, *rows)
    return by_chunk(out)


def hold(*values):
    return lax.optimization_barrier(values)


def merge(a, b):
    top = jnp.maximum(a[0], b[0])
    drops = (a[0] - top, b[0] - top)
    factors = (jnp.exp(drops[0]), jnp.exp(drops[1]))
    out = [top, factors[0] * a[1] + factors[1] * b[1]]
    if a.shape[0] == 3:
        out.append(factors[0] * (a[2] + drops[0] * a[1]) + factors[1] * (b[2] + drops[1] * b[1]))
    return jnp.stack(out)


def by_chunk(groups):
    place = {b: (g, i) for g, bits in enumerate(GROUPS) for i, b in enumerate(bits)}
    return jnp.stack([groups[place[b][0]][:, place[b][1]] for b in range(CUBE)], axis=1)


def solution(mesh):
    n_dp = mesh.shape["dp"]
    n_cent = mesh.shape["cent"]
    high = n_dp // 2
    top_bit = n_dp // 4

    def flip(value, bits):
        return lax.ppermute(value, "dp", [(i, i ^ bits) for i in range(n_dp)])

    def member(place):
        return (place & 3) | (high if place & 4 else 0)

    def rows_from(value, place):
        return flip(value, member(place))

    def across(value, bits):
        return lax.ppermute(value, "cent", [(i, i ^ bits) for i in range(n_cent)])

    def gather_cent(value):
        blocks = [value]
        bits = 1
        while bits < n_cent:
            blocks = blocks + [across(b, bits) for b in blocks]
            bits *= 2
        return blocks

    def scatter_cent(value):
        bits = n_cent // 2
        while bits:
            half = value.shape[0] // 2
            value = value[:half] + across(value[half:], bits)
            bits //= 2
        return value

    def gather_near(value):
        bits = 4
        while bits < top_bit:
            value = jnp.concatenate([value, flip(value, bits)], axis=0)
            bits *= 2
        return value

    def scatter_near(value):
        bits = top_bit // 2
        while bits >= 4:
            half = value.shape[0] // 2
            value = value[:half] + flip(value[half:], bits)
            bits //= 2
        return value

    def by_position(stats):
        place = lax.axis_index("dp")
        for bit in (1, 2, 4):
            swapped = jnp.stack([stats[:, b ^ bit] for b in range(CUBE)], axis=1)
            stats = jnp.where((place & member(bit)) != 0, swapped, stats)
        return stats

    def exchange(value):
        groups = [[i + member(place) for place in range(CUBE)] for i in range(0, high, 4)]
        return lax.all_to_all(value, "dp", 0, 0, axis_index_groups=groups)

    def everywhere(stats):
        return exchange(jnp.broadcast_to(stats[None], (CUBE,) + stats.shape))

    def to_owner(stats):
        return exchange(stats.transpose(1, 0, 2))

    def on_device(embeddings, centroids):
        shard, width = embeddings.shape
        half = shard // 2
        chunk = {0: embeddings.astype(jnp.bfloat16)}
        for bit in (4, 1, 2):
            chunk[bit] = rows_from(chunk[0], bit)
        chunk[3] = rows_from(chunk[1], 2)
        near_own = gather_near(centroids.astype(jnp.bfloat16))
        far_own = flip(near_own, top_bit)
        near = gather_cent(near_own)
        n_near = len(near) * near_own.shape[0]
        far = gather_cent(far_own)
        chunk[4], chunk[3], chunk[2], far = hold(chunk[4], chunk[3], chunk[2], far)
        chunk[5] = rows_from(chunk[4], 1)
        chunk[6] = rows_from(chunk[4], 2)
        parts = (rows_from(chunk[3][:half], 4), rows_from(chunk[4][half:], 3))
        done, piece = first_pass(near + far, [chunk[b] for b in GROUPS[0]])
        passes = [done, first_pass([piece], [chunk[b] for b in GROUPS[1]])[0]]
        parts, passes = hold(parts, passes)
        passes.append(first_pass([piece], [chunk[GROUPS[2][0]], *parts], True)[0])
        local, row_sqs, rows = zip(*passes)

        stats = by_position(by_chunk(local))
        stats = everywhere(stats)
        top = jnp.max(stats[:, 0], axis=0)
        total = jnp.sum(stats[:, 1] * jnp.exp(stats[:, 0] - top), axis=0)
        stats = by_position(jnp.stack([top, total]))
        final = [jnp.concatenate([stats[:, b] for b in bits], axis=1) for bits in GROUPS]

        far = scatter_cent(sums_pass(piece, final, row_sqs, rows, n_near, 2 * n_near))
        count = far[:, width:]
        coarse = lax.reduce_precision(count, 8, 7)
        lane = lax.broadcasted_iota(jnp.int32, count.shape, 1)
        far = jnp.concatenate([far[:, :width], jnp.where(lane < 64, coarse, count - coarse)], axis=1)
        far = flip(far.astype(jnp.bfloat16), top_bit).astype(jnp.float32)
        near = scatter_cent(sums_pass(piece, final, row_sqs, rows, 0, n_near))
        counts = far[:, width : width + 1] + far[:, width + 64 : width + 65]
        far = jnp.concatenate([far[:, :width], jnp.broadcast_to(counts, count.shape)], axis=1)
        sums = scatter_near(near + far)
        updated = (sums[:, :width] + prior_mass * centroids) / (sums[:, width : width + 1] + prior_mass)
        near_own = gather_near(updated.astype(jnp.bfloat16))
        far_own = flip(near_own, top_bit)
        stats = second_pass(jnp.concatenate(gather_cent(near_own), axis=0), row_sqs, rows, shard)
        far_own, stats = hold(far_own, stats)
        far = gather_cent(far_own)
        stats = merge(stats, second_pass(far_own, row_sqs, rows, shard))
        stats = merge(stats, second_pass(jnp.concatenate(far[1:], axis=0), row_sqs, rows, shard))
        stats = to_owner(by_position(stats))
        drop = stats[:, 0] - jnp.max(stats[:, 0], axis=0)
        factor = jnp.exp(drop)
        total = jnp.sum(factor * stats[:, 1], axis=0)
        spread = jnp.sum(factor * (stats[:, 2] + drop * stats[:, 1]), axis=0)
        entropy = jnp.log(total) - spread / total
        return (updated, entropy)

    in_specs = (P(("dp", "cent"), None), P(("dp", "cent"), None))
    out_specs = (P(("dp", "cent"), None), P(("dp", "cent")))
    return jax.shard_map(
        on_device, mesh=mesh, in_specs=in_specs, out_specs=out_specs, check_vma=False
    )
```

```python
import functools

import jax
import jax.numpy as jnp
from jax import lax
from jax.experimental import pallas as pl
from jax.experimental.pallas import tpu as pltpu
from jax.sharding import PartitionSpec as P

softness_level = 32.0
prior_mass = 4.0
CUBE = 8
GROUPS = ((0, 1, 2, 3), (4, 5), (6, 7))
VMEM = pl.BlockSpec(memory_space=pltpu.VMEM)
HBM = pl.BlockSpec(memory_space=pltpu.HBM)
GRANT = 12 << 20


def params():
    return pltpu.CompilerParams(vmem_limit_bytes=GRANT)


def row_squares(rows):
    wide = rows.astype(jnp.float32)
    square = wide * wide
    part = square[:, :128]
    for j in range(128, square.shape[1], 128):
        part = part + square[:, j : j + 128]
    return jnp.sum(part.T, axis=0, keepdims=True)


def centroid_squares(piece):
    wide = piece.astype(jnp.float32)
    return jnp.sum(wide * wide, axis=1, keepdims=True)


def scores(piece, cent_sq, rows, row_sq):
    inner = lax.dot_general(piece, rows, (((1,), (1,)), ((), ())), preferred_element_type=jnp.float32)
    scale = 0.5 / softness_level
    return (2.0 * scale) * inner - scale * row_sq - scale * cent_sq


def fetch(sources, target, sems):
    copies, at = [], 0
    for i, source in enumerate(sources):
        n = source.shape[0]
        copy = pltpu.make_async_copy(source, target.at[pl.ds(at, n)], sems.at[i])
        copy.start()
        copies.append(copy)
        at += n
    return copies


def first_kernel(n, n_blocks, n_chunks, shard, last, *refs):
    blocks, chunks, refs = refs[:n_blocks], refs[n_blocks : n_blocks + n_chunks], refs[n_blocks + n_chunks :]
    stats_ref, row_sq_ref, rows_ref = refs[:3]
    sems = refs[-1]
    cents, copies = blocks[0], []
    if n_blocks > 1:
        cents, at = refs[3], 0
        for block in blocks:
            cents[at : at + block.shape[0], :] = block[...]
            at += block.shape[0]
    if last:
        at = 0
        for chunk in chunks:
            rows_ref[at : at + chunk.shape[0], :] = chunk[...]
            at += chunk.shape[0]
    else:
        copies = fetch(chunks, rows_ref, sems)
    piece = cents[...]
    cent_sq = centroid_squares(piece)
    tile = 2 * shard
    for j in range(n // 2):
        for copy in copies[2 * j : 2 * j + 2]:
            copy.wait()
        span = slice(j * tile, (j + 1) * tile)
        rows = rows_ref[span, :]
        row_sq = row_squares(rows)
        score = scores(piece, cent_sq, rows, row_sq)
        top = jnp.max(score, axis=0, keepdims=True)
        total = jnp.sum(jnp.exp(score - top), axis=0, keepdims=True)
        row_sq_ref[:, span] = row_sq
        for i in range(2):
            stats_ref[0, 2 * j + i : 2 * j + i + 1, :] = top[:, i * shard : (i + 1) * shard]
            stats_ref[1, 2 * j + i : 2 * j + i + 1, :] = total[:, i * shard : (i + 1) * shard]


def first_pass(blocks, chunks, last=False):
    n_blocks, n_chunks = len(blocks), len(chunks)
    shard, width = chunks[0].shape
    n_k = sum(b.shape[0] for b in blocks)
    n_rows = sum(c.shape[0] for c in chunks)
    n = n_rows // shard
    outs = [
        jax.ShapeDtypeStruct((2, n, shard), jnp.float32),
        jax.ShapeDtypeStruct((1, n_rows), jnp.float32),
        jax.ShapeDtypeStruct((n_rows, width), jnp.bfloat16),
    ]
    if n_blocks > 1:
        outs.append(jax.ShapeDtypeStruct((n_k, width), jnp.bfloat16))
    out = pl.pallas_call(
        functools.partial(first_kernel, n, n_blocks, n_chunks, shard, last),
        out_shape=tuple(outs),
        in_specs=[VMEM] * n_blocks + [VMEM if last else HBM] * n_chunks,
        out_specs=(VMEM,) * len(outs),
        scratch_shapes=[pltpu.SemaphoreType.DMA((n_chunks,))],
        compiler_params=params(),
        cost_estimate=pl.CostEstimate(
            flops=2 * n_k * n_rows * width,
            bytes_accessed=2 * n_rows * width,
            transcendentals=n_k * n_rows,
        ),
        name="first_pass",
    )(*blocks, *chunks)
    return out[:3], (out[3] if n_blocks > 1 else blocks[0])


def sums_kernel(first, last, n, cents, *refs):
    stats, row_sqs, rows, priors = refs[:n], refs[n : 2 * n], refs[2 * n : 3 * n], refs[3 * n : -1]
    out_ref = refs[-1]
    width = cents.shape[1]
    piece = cents[first:last, :]
    cent_sq = centroid_squares(piece)
    counts = 0.0
    for s in range(n):
        score = scores(piece, cent_sq, rows[s][...], row_sqs[s][...])
        resp = (jnp.exp(score - stats[s][0:1, :]) * (1.0 / stats[s][1:2, :])).astype(jnp.bfloat16)
        counts = counts + jnp.sum(resp.astype(jnp.float32), axis=1, keepdims=True)
        part = jnp.dot(resp, rows[s][...], preferred_element_type=jnp.float32)
        if s:
            part = part + out_ref[:, :width]
        out_ref[:, :width] = part
    out_ref[:, width:] = jnp.broadcast_to(counts, (last - first, 128))
    for prior in priors:
        held = prior.shape[0]
        out_ref[:held, :width] += prior_mass * prior[...]
        out_ref[:held, width:] += prior_mass


def sums_pass(cents, stats, row_sqs, rows, first, last, priors=()):
    n = len(rows)
    width = rows[0].shape[1]
    n_rows = sum(r.shape[0] for r in rows)
    return pl.pallas_call(
        functools.partial(sums_kernel, first, last, n),
        out_shape=jax.ShapeDtypeStruct((last - first, width + 128), jnp.float32),
        in_specs=[VMEM] * (1 + 3 * n + len(priors)),
        out_specs=VMEM,
        compiler_params=params(),
        cost_estimate=pl.CostEstimate(
            flops=4 * (last - first) * n_rows * width,
            bytes_accessed=2 * n_rows * width,
            transcendentals=(last - first) * n_rows,
        ),
        name="sums_pass",
    )(cents, *stats, *row_sqs, *rows, *priors)


def second_kernel(shard, n, cents, *refs):
    row_sqs, rows, stats = refs[:n], refs[n : 2 * n], refs[2 * n :]
    piece = cents[...]
    cent_sq = centroid_squares(piece)
    tile = 2 * shard
    for s in range(n):
        for j in range(rows[s].shape[0] // tile):
            span = slice(j * tile, (j + 1) * tile)
            score = scores(piece, cent_sq, rows[s][span, :], row_sqs[s][:, span])
            top = jnp.max(score, axis=0, keepdims=True)
            shifted = score - top
            weight = jnp.exp(shifted)
            total = jnp.sum(weight, axis=0, keepdims=True)
            spread = jnp.sum(weight * shifted, axis=0, keepdims=True)
            for i in range(2):
                part = slice(i * shard, (i + 1) * shard)
                at = slice(2 * j + i, 2 * j + i + 1)
                stats[s][0, at, :] = top[:, part]
                stats[s][1, at, :] = total[:, part]
                stats[s][2, at, :] = spread[:, part]


def second_pass(cents, row_sqs, rows, shard):
    n = len(rows)
    n_k, width = cents.shape
    n_rows = sum(r.shape[0] for r in rows)
    out = pl.pallas_call(
        functools.partial(second_kernel, shard, n),
        out_shape=tuple(jax.ShapeDtypeStruct((3, r.shape[0] // shard, shard), jnp.float32) for r in rows),
        in_specs=[VMEM] * (1 + 2 * n),
        out_specs=(VMEM,) * n,
        compiler_params=params(),
        cost_estimate=pl.CostEstimate(
            flops=2 * n_k * n_rows * width, bytes_accessed=2 * n_rows * width, transcendentals=n_k * n_rows
        ),
        name="second_pass",
    )(cents, *row_sqs, *rows)
    return by_chunk(out)


def hold(*values):
    return lax.optimization_barrier(values)


def merge(a, b):
    top = jnp.maximum(a[0], b[0])
    drops = (a[0] - top, b[0] - top)
    factors = (jnp.exp(drops[0]), jnp.exp(drops[1]))
    out = [top, factors[0] * a[1] + factors[1] * b[1]]
    if a.shape[0] == 3:
        out.append(factors[0] * (a[2] + drops[0] * a[1]) + factors[1] * (b[2] + drops[1] * b[1]))
    return jnp.stack(out)


def by_chunk(groups):
    place = {b: (g, i) for g, bits in enumerate(GROUPS) for i, b in enumerate(bits)}
    return jnp.stack([groups[place[b][0]][:, place[b][1]] for b in range(CUBE)], axis=1)


def solution(mesh):
    n_dp = mesh.shape["dp"]
    n_cent = mesh.shape["cent"]
    high = n_dp // 2
    top_bit = n_dp // 4

    def flip(value, bits):
        return lax.ppermute(value, "dp", [(i, i ^ bits) for i in range(n_dp)])

    def member(place):
        return (place & 3) | (high if place & 4 else 0)

    def rows_from(value, place):
        return flip(value, member(place))

    def across(value, bits):
        return lax.ppermute(value, "cent", [(i, i ^ bits) for i in range(n_cent)])

    def gather_cent(value):
        blocks = [value]
        bits = 1
        while bits < n_cent:
            blocks = blocks + [across(b, bits) for b in blocks]
            bits *= 2
        return blocks

    def scatter_cent(value):
        bits = n_cent // 2
        while bits:
            half = value.shape[0] // 2
            value = value[:half] + across(value[half:], bits)
            bits //= 2
        return value

    def gather_near(value):
        bits = 4
        while bits < top_bit:
            value = jnp.concatenate([value, flip(value, bits)], axis=0)
            bits *= 2
        return value

    def scatter_near(value):
        bits = top_bit // 2
        while bits >= 4:
            half = value.shape[0] // 2
            value = value[:half] + flip(value[half:], bits)
            bits //= 2
        return value

    def by_position(stats):
        place = lax.axis_index("dp")
        for bit in (1, 2, 4):
            swapped = jnp.stack([stats[:, b ^ bit] for b in range(CUBE)], axis=1)
            stats = jnp.where((place & member(bit)) != 0, swapped, stats)
        return stats

    def exchange(value):
        groups = [[i + member(place) for place in range(CUBE)] for i in range(0, high, 4)]
        return lax.all_to_all(value, "dp", 0, 0, axis_index_groups=groups)

    def everywhere(stats):
        return exchange(jnp.broadcast_to(stats[None], (CUBE,) + stats.shape))

    def to_owner(stats):
        return exchange(stats.transpose(1, 0, 2))

    def on_device(embeddings, centroids):
        shard, width = embeddings.shape
        half = shard // 2
        chunk = {0: embeddings.astype(jnp.bfloat16)}
        for bit in (4, 1, 2):
            chunk[bit] = rows_from(chunk[0], bit)
        chunk[3] = rows_from(chunk[1], 2)
        near_own = gather_near(centroids.astype(jnp.bfloat16))
        far_own = flip(near_own, top_bit)
        near = gather_cent(near_own)
        n_near = len(near) * near_own.shape[0]
        far = gather_cent(far_own)
        chunk[4], chunk[3], chunk[2], far = hold(chunk[4], chunk[3], chunk[2], far)
        chunk[5] = rows_from(chunk[4], 1)
        chunk[6] = rows_from(chunk[4], 2)
        parts = (rows_from(chunk[3][:half], 4), rows_from(chunk[4][half:], 3))
        done, piece = first_pass(near + far, [chunk[b] for b in GROUPS[0]])
        passes = [done, first_pass([piece], [chunk[b] for b in GROUPS[1]])[0]]
        parts, passes = hold(parts, passes)
        passes.append(first_pass([piece], [chunk[GROUPS[2][0]], *parts], True)[0])
        local, row_sqs, rows = zip(*passes)

        stats = by_position(by_chunk(local))
        stats = everywhere(stats)
        top = jnp.max(stats[:, 0], axis=0)
        total = jnp.sum(stats[:, 1] * jnp.exp(stats[:, 0] - top), axis=0)
        stats = by_position(jnp.stack([top, total]))
        final = [jnp.concatenate([stats[:, b] for b in bits], axis=1) for bits in GROUPS]

        far = scatter_cent(sums_pass(piece, final, row_sqs, rows, n_near, 2 * n_near))
        count = far[:, width:]
        coarse = lax.reduce_precision(count, 8, 7)
        lane = lax.broadcasted_iota(jnp.int32, count.shape, 1)
        far = jnp.concatenate([far[:, :width], jnp.where(lane < 64, coarse, count - coarse)], axis=1)
        far = flip(far.astype(jnp.bfloat16), top_bit).astype(jnp.float32)
        near = scatter_cent(sums_pass(piece, final, row_sqs, rows, 0, n_near, [centroids]))
        counts = far[:, width : width + 1] + far[:, width + 64 : width + 65]
        far = jnp.concatenate([far[:, :width], jnp.broadcast_to(counts, count.shape)], axis=1)
        sums = scatter_near(near + far)
        updated = sums[:, :width] / sums[:, width : width + 1]
        near_own = gather_near(updated.astype(jnp.bfloat16))
        far_own = flip(near_own, top_bit)
        stats = second_pass(jnp.concatenate(gather_cent(near_own), axis=0), row_sqs, rows, shard)
        far_own, stats = hold(far_own, stats)
        far = gather_cent(far_own)
        stats = merge(stats, second_pass(far_own, row_sqs, rows, shard))
        stats = merge(stats, second_pass(jnp.concatenate(far[1:], axis=0), row_sqs, rows, shard))
        stats = to_owner(by_position(stats))
        drop = stats[:, 0] - jnp.max(stats[:, 0], axis=0)
        factor = jnp.exp(drop)
        total = jnp.sum(factor * stats[:, 1], axis=0)
        spread = jnp.sum(factor * (stats[:, 2] + drop * stats[:, 1]), axis=0)
        entropy = jnp.log(total) - spread / total
        return (updated, entropy)

    in_specs = (P(("dp", "cent"), None), P(("dp", "cent"), None))
    out_specs = (P(("dp", "cent"), None), P(("dp", "cent")))
    return jax.shard_map(
        on_device, mesh=mesh, in_specs=in_specs, out_specs=out_specs, check_vma=False
    )
```

```python
import functools

import jax
import jax.numpy as jnp
from jax import lax
from jax.experimental import pallas as pl
from jax.experimental.pallas import tpu as pltpu
from jax.sharding import PartitionSpec as P

softness_level = 32.0
prior_mass = 4.0
CUBE = 8
GROUPS = ((0, 1, 2, 3), (4, 5), (6, 7))
VMEM = pl.BlockSpec(memory_space=pltpu.VMEM)
GRANT = 12 << 20


def params():
    return pltpu.CompilerParams(vmem_limit_bytes=GRANT)


def row_squares(rows):
    wide = rows.astype(jnp.float32)
    square = wide * wide
    part = square[:, :128]
    for j in range(128, square.shape[1], 128):
        part = part + square[:, j : j + 128]
    return jnp.sum(part.T, axis=0, keepdims=True)


def centroid_squares(piece):
    wide = piece.astype(jnp.float32)
    return jnp.sum(wide * wide, axis=1, keepdims=True)


def scores(piece, cent_sq, rows, row_sq):
    inner = lax.dot_general(piece, rows, (((1,), (1,)), ((), ())), preferred_element_type=jnp.float32)
    scale = 0.5 / softness_level
    return (2.0 * scale) * inner - scale * row_sq - scale * cent_sq


def first_kernel(n_chunks, shard, cents, *refs):
    chunks = refs[:n_chunks]
    stats_ref, row_sq_ref, rows_ref = refs[n_chunks:]
    at = 0
    for chunk in chunks:
        rows_ref[at : at + chunk.shape[0], :] = chunk[...]
        at += chunk.shape[0]
    piece = cents[...]
    cent_sq = centroid_squares(piece)
    tile = 2 * shard
    for j in range(at // tile):
        span = slice(j * tile, (j + 1) * tile)
        rows = rows_ref[span, :]
        row_sq = row_squares(rows)
        score = scores(piece, cent_sq, rows, row_sq)
        top = jnp.max(score, axis=0, keepdims=True)
        total = jnp.sum(jnp.exp(score - top), axis=0, keepdims=True)
        row_sq_ref[:, span] = row_sq
        for i in range(2):
            stats_ref[0, 2 * j + i : 2 * j + i + 1, :] = top[:, i * shard : (i + 1) * shard]
            stats_ref[1, 2 * j + i : 2 * j + i + 1, :] = total[:, i * shard : (i + 1) * shard]


def first_pass(cents, chunks):
    shard, width = chunks[0].shape
    n_k = cents.shape[0]
    n_rows = sum(c.shape[0] for c in chunks)
    return pl.pallas_call(
        functools.partial(first_kernel, len(chunks), shard),
        out_shape=(
            jax.ShapeDtypeStruct((2, n_rows // shard, shard), jnp.float32),
            jax.ShapeDtypeStruct((1, n_rows), jnp.float32),
            jax.ShapeDtypeStruct((n_rows, width), jnp.bfloat16),
        ),
        in_specs=[VMEM] * (1 + len(chunks)),
        out_specs=(VMEM,) * 3,
        compiler_params=params(),
        cost_estimate=pl.CostEstimate(
            flops=2 * n_k * n_rows * width, bytes_accessed=2 * n_rows * width, transcendentals=n_k * n_rows
        ),
        name="first_pass",
    )(cents, *chunks)


def sums_kernel(first, last, n, cents, *refs):
    stats, row_sqs, rows, priors = refs[:n], refs[n : 2 * n], refs[2 * n : 3 * n], refs[3 * n : -1]
    out_ref = refs[-1]
    width = cents.shape[1]
    piece = cents[first:last, :]
    cent_sq = centroid_squares(piece)
    counts = 0.0
    for s in range(n):
        score = scores(piece, cent_sq, rows[s][...], row_sqs[s][...])
        resp = (jnp.exp(score - stats[s][0:1, :]) * (1.0 / stats[s][1:2, :])).astype(jnp.bfloat16)
        counts = counts + jnp.sum(resp.astype(jnp.float32), axis=1, keepdims=True)
        part = jnp.dot(resp, rows[s][...], preferred_element_type=jnp.float32)
        if s:
            part = part + out_ref[:, :width]
        out_ref[:, :width] = part
    out_ref[:, width:] = jnp.broadcast_to(counts, (last - first, 128))
    for prior in priors:
        held = prior.shape[0]
        out_ref[:held, :width] += prior_mass * prior[...]
        out_ref[:held, width:] += prior_mass


def sums_pass(cents, stats, row_sqs, rows, first, last, priors=()):
    n = len(rows)
    width = rows[0].shape[1]
    n_rows = sum(r.shape[0] for r in rows)
    return pl.pallas_call(
        functools.partial(sums_kernel, first, last, n),
        out_shape=jax.ShapeDtypeStruct((last - first, width + 128), jnp.float32),
        in_specs=[VMEM] * (1 + 3 * n + len(priors)),
        out_specs=VMEM,
        compiler_params=params(),
        cost_estimate=pl.CostEstimate(
            flops=4 * (last - first) * n_rows * width,
            bytes_accessed=2 * n_rows * width,
            transcendentals=(last - first) * n_rows,
        ),
        name="sums_pass",
    )(cents, *stats, *row_sqs, *rows, *priors)


def second_kernel(shard, n, cents, *refs):
    row_sqs, rows, stats = refs[:n], refs[n : 2 * n], refs[2 * n :]
    piece = cents[...]
    cent_sq = centroid_squares(piece)
    tile = 2 * shard
    for s in range(n):
        for j in range(rows[s].shape[0] // tile):
            span = slice(j * tile, (j + 1) * tile)
            score = scores(piece, cent_sq, rows[s][span, :], row_sqs[s][:, span])
            top = jnp.max(score, axis=0, keepdims=True)
            shifted = score - top
            weight = jnp.exp(shifted)
            total = jnp.sum(weight, axis=0, keepdims=True)
            spread = jnp.sum(weight * shifted, axis=0, keepdims=True)
            for i in range(2):
                part = slice(i * shard, (i + 1) * shard)
                at = slice(2 * j + i, 2 * j + i + 1)
                stats[s][0, at, :] = top[:, part]
                stats[s][1, at, :] = total[:, part]
                stats[s][2, at, :] = spread[:, part]


def second_pass(cents, row_sqs, rows, shard):
    n = len(rows)
    n_k, width = cents.shape
    n_rows = sum(r.shape[0] for r in rows)
    out = pl.pallas_call(
        functools.partial(second_kernel, shard, n),
        out_shape=tuple(jax.ShapeDtypeStruct((3, r.shape[0] // shard, shard), jnp.float32) for r in rows),
        in_specs=[VMEM] * (1 + 2 * n),
        out_specs=(VMEM,) * n,
        compiler_params=params(),
        cost_estimate=pl.CostEstimate(
            flops=2 * n_k * n_rows * width, bytes_accessed=2 * n_rows * width, transcendentals=n_k * n_rows
        ),
        name="second_pass",
    )(cents, *row_sqs, *rows)
    return by_chunk(out)


def hold(*values):
    return lax.optimization_barrier(values)


def merge(a, b):
    top = jnp.maximum(a[0], b[0])
    drops = (a[0] - top, b[0] - top)
    factors = (jnp.exp(drops[0]), jnp.exp(drops[1]))
    out = [top, factors[0] * a[1] + factors[1] * b[1]]
    if a.shape[0] == 3:
        out.append(factors[0] * (a[2] + drops[0] * a[1]) + factors[1] * (b[2] + drops[1] * b[1]))
    return jnp.stack(out)


def by_chunk(groups):
    place = {b: (g, i) for g, bits in enumerate(GROUPS) for i, b in enumerate(bits)}
    return jnp.stack([groups[place[b][0]][:, place[b][1]] for b in range(CUBE)], axis=1)


def solution(mesh):
    n_dp = mesh.shape["dp"]
    n_cent = mesh.shape["cent"]
    high = n_dp // 2
    top_bit = n_dp // 4

    def flip(value, bits):
        return lax.ppermute(value, "dp", [(i, i ^ bits) for i in range(n_dp)])

    def member(place):
        return (place & 3) | (high if place & 4 else 0)

    def rows_from(value, place):
        return flip(value, member(place))

    def across(value, bits):
        return lax.ppermute(value, "cent", [(i, i ^ bits) for i in range(n_cent)])

    def gather_cent(value):
        blocks = [value]
        bits = 1
        while bits < n_cent:
            blocks = blocks + [across(b, bits) for b in blocks]
            bits *= 2
        return blocks

    def scatter_cent(value):
        bits = n_cent // 2
        while bits:
            half = value.shape[0] // 2
            value = value[:half] + across(value[half:], bits)
            bits //= 2
        return value

    def gather_near(value):
        bits = 4
        while bits < top_bit:
            value = jnp.concatenate([value, flip(value, bits)], axis=0)
            bits *= 2
        return value

    def scatter_near(value):
        bits = top_bit // 2
        while bits >= 4:
            half = value.shape[0] // 2
            value = value[:half] + flip(value[half:], bits)
            bits //= 2
        return value

    def by_position(stats):
        place = lax.axis_index("dp")
        for bit in (1, 2, 4):
            swapped = jnp.stack([stats[:, b ^ bit] for b in range(CUBE)], axis=1)
            stats = jnp.where((place & member(bit)) != 0, swapped, stats)
        return stats

    def exchange(value):
        groups = [[i + member(place) for place in range(CUBE)] for i in range(0, high, 4)]
        return lax.all_to_all(value, "dp", 0, 0, axis_index_groups=groups)

    def everywhere(stats):
        return exchange(jnp.broadcast_to(stats[None], (CUBE,) + stats.shape))

    def to_owner(stats):
        return exchange(stats.transpose(1, 0, 2))

    def on_device(embeddings, centroids):
        shard, width = embeddings.shape
        half = shard // 2
        chunk = {0: embeddings.astype(jnp.bfloat16)}
        for bit in (4, 1, 2):
            chunk[bit] = rows_from(chunk[0], bit)
        chunk[3] = rows_from(chunk[1], 2)
        near_own = gather_near(centroids.astype(jnp.bfloat16))
        far_own = flip(near_own, top_bit)
        near = gather_cent(near_own)
        n_near = len(near) * near_own.shape[0]
        far = gather_cent(far_own)
        chunk[4], chunk[3], chunk[2], far = hold(chunk[4], chunk[3], chunk[2], far)
        chunk[5] = rows_from(chunk[4], 1)
        chunk[6] = rows_from(chunk[4], 2)
        parts = (rows_from(chunk[3][:half], 4), rows_from(chunk[4][half:], 3))
        piece = jnp.concatenate(near + far, axis=0)
        passes = [first_pass(piece, [chunk[b] for b in bits]) for bits in GROUPS[:2]]
        parts, passes = hold(parts, passes)
        passes.append(first_pass(piece, [chunk[GROUPS[2][0]], *parts]))
        local, row_sqs, rows = zip(*passes)

        stats = by_position(by_chunk(local))
        stats = everywhere(stats)
        top = jnp.max(stats[:, 0], axis=0)
        total = jnp.sum(stats[:, 1] * jnp.exp(stats[:, 0] - top), axis=0)
        stats = by_position(jnp.stack([top, total]))
        final = [jnp.concatenate([stats[:, b] for b in bits], axis=1) for bits in GROUPS]

        far = scatter_cent(sums_pass(piece, final, row_sqs, rows, n_near, 2 * n_near))
        count = far[:, width:]
        coarse = lax.reduce_precision(count, 8, 7)
        lane = lax.broadcasted_iota(jnp.int32, count.shape, 1)
        far = jnp.concatenate([far[:, :width], jnp.where(lane < 64, coarse, count - coarse)], axis=1)
        far = flip(far.astype(jnp.bfloat16), top_bit).astype(jnp.float32)
        near = scatter_cent(sums_pass(piece, final, row_sqs, rows, 0, n_near, [centroids]))
        counts = far[:, width : width + 1] + far[:, width + 64 : width + 65]
        far = jnp.concatenate([far[:, :width], jnp.broadcast_to(counts, count.shape)], axis=1)
        sums = scatter_near(near + far)
        updated = sums[:, :width] / sums[:, width : width + 1]
        near_own = gather_near(updated.astype(jnp.bfloat16))
        far_own = flip(near_own, top_bit)
        stats = second_pass(jnp.concatenate(gather_cent(near_own), axis=0), row_sqs, rows, shard)
        far_own, stats = hold(far_own, stats)
        far = gather_cent(far_own)
        stats = merge(stats, second_pass(far_own, row_sqs, rows, shard))
        stats = merge(stats, second_pass(jnp.concatenate(far[1:], axis=0), row_sqs, rows, shard))
        stats = to_owner(by_position(stats))
        drop = stats[:, 0] - jnp.max(stats[:, 0], axis=0)
        factor = jnp.exp(drop)
        total = jnp.sum(factor * stats[:, 1], axis=0)
        spread = jnp.sum(factor * (stats[:, 2] + drop * stats[:, 1]), axis=0)
        entropy = jnp.log(total) - spread / total
        return (updated, entropy)

    in_specs = (P(("dp", "cent"), None), P(("dp", "cent"), None))
    out_specs = (P(("dp", "cent"), None), P(("dp", "cent")))
    return jax.shard_map(
        on_device, mesh=mesh, in_specs=in_specs, out_specs=out_specs, check_vma=False
    )
```

```python
import functools

import jax
import jax.numpy as jnp
from jax import lax
from jax.experimental import pallas as pl
from jax.experimental.pallas import tpu as pltpu
from jax.sharding import PartitionSpec as P

softness_level = 32.0
prior_mass = 4.0
CUBE = 8
VMEM = pl.BlockSpec(memory_space=pltpu.VMEM)
GRANT = 12 << 20


def params():
    return pltpu.CompilerParams(vmem_limit_bytes=GRANT)


def row_squares(rows):
    wide = rows.astype(jnp.float32)
    square = wide * wide
    part = square[:, :128]
    for j in range(128, square.shape[1], 128):
        part = part + square[:, j : j + 128]
    return jnp.sum(part.T, axis=0, keepdims=True)


def centroid_squares(piece):
    wide = piece.astype(jnp.float32)
    return jnp.sum(wide * wide, axis=1, keepdims=True)


def scores(piece, cent_sq, rows, row_sq):
    inner = lax.dot_general(piece, rows, (((1,), (1,)), ((), ())), preferred_element_type=jnp.float32)
    scale = 0.5 / softness_level
    return (2.0 * scale) * inner - scale * row_sq - scale * cent_sq


def cast_kernel(source, target):
    target[...] = source[...].astype(target.dtype)


def rounded(value):
    return pl.pallas_call(
        cast_kernel,
        out_shape=jax.ShapeDtypeStruct(value.shape, jnp.bfloat16),
        in_specs=[VMEM],
        out_specs=VMEM,
        compiler_params=params(),
        name="rounded",
    )(value)


def first_kernel(n_chunks, shard, start, cents, *refs):
    chunks = refs[:n_chunks]
    stats_ref, row_sq_ref, rows_ref = refs[-3:]
    at = start
    for chunk in chunks:
        rows_ref[at : at + chunk.shape[0], :] = chunk[...]
        at += chunk.shape[0]
    piece = cents[...]
    cent_sq = centroid_squares(piece)
    tile = 2 * shard
    for j in range((at - start) // tile):
        span = slice(j * tile, (j + 1) * tile)
        rows = rows_ref[start + j * tile : start + (j + 1) * tile, :]
        row_sq = row_squares(rows)
        score = scores(piece, cent_sq, rows, row_sq)
        top = jnp.max(score, axis=0, keepdims=True)
        total = jnp.sum(jnp.exp(score - top), axis=0, keepdims=True)
        row_sq_ref[:, span] = row_sq
        for i in range(2):
            stats_ref[0, 2 * j + i : 2 * j + i + 1, :] = top[:, i * shard : (i + 1) * shard]
            stats_ref[1, 2 * j + i : 2 * j + i + 1, :] = total[:, i * shard : (i + 1) * shard]


def first_pass(cents, chunks, start, held=None):
    shard, width = chunks[0].shape
    n_k = cents.shape[0]
    n_rows = sum(c.shape[0] for c in chunks)
    before = [] if held is None else [held]
    return pl.pallas_call(
        functools.partial(first_kernel, len(chunks), shard, start),
        out_shape=(
            jax.ShapeDtypeStruct((2, n_rows // shard, shard), jnp.float32),
            jax.ShapeDtypeStruct((1, n_rows), jnp.float32),
            jax.ShapeDtypeStruct((CUBE * shard, width), jnp.bfloat16),
        ),
        in_specs=[VMEM] * (1 + len(chunks) + len(before)),
        out_specs=(VMEM,) * 3,
        input_output_aliases={1 + len(chunks): 2} if before else {},
        compiler_params=params(),
        cost_estimate=pl.CostEstimate(
            flops=2 * n_k * n_rows * width, bytes_accessed=2 * n_rows * width, transcendentals=n_k * n_rows
        ),
        name="first_pass",
    )(cents, *chunks, *before)


def sums_kernel(first, last, cents, stats, row_sq, rows, *refs):
    priors, out_ref = refs[:-1], refs[-1]
    width = cents.shape[1]
    piece = cents[first:last, :]
    score = scores(piece, centroid_squares(piece), rows[...], row_sq[...])
    resp = (jnp.exp(score - stats[0:1, :]) * (1.0 / stats[1:2, :])).astype(jnp.bfloat16)
    counts = jnp.sum(resp.astype(jnp.float32), axis=1, keepdims=True)
    out_ref[:, :width] = jnp.dot(resp, rows[...], preferred_element_type=jnp.float32)
    out_ref[:, width:] = jnp.broadcast_to(counts, (last - first, 128))
    for prior in priors:
        held = prior.shape[0]
        out_ref[:held, :width] += prior_mass * prior[...]
        out_ref[:held, width:] += prior_mass


def sums_pass(cents, stats, row_sq, rows, first, last, priors=()):
    n_rows, width = rows.shape
    return pl.pallas_call(
        functools.partial(sums_kernel, first, last),
        out_shape=jax.ShapeDtypeStruct((last - first, width + 128), jnp.float32),
        in_specs=[VMEM] * (4 + len(priors)),
        out_specs=VMEM,
        compiler_params=params(),
        cost_estimate=pl.CostEstimate(
            flops=4 * (last - first) * n_rows * width,
            bytes_accessed=2 * n_rows * width,
            transcendentals=(last - first) * n_rows,
        ),
        name="sums_pass",
    )(cents, stats, row_sq, rows, *priors)


def second_kernel(shard, cents, row_sqs, rows, stats):
    piece = cents[...]
    cent_sq = centroid_squares(piece)
    tile = 2 * shard
    for j in range(rows.shape[0] // tile):
        span = slice(j * tile, (j + 1) * tile)
        score = scores(piece, cent_sq, rows[span, :], row_sqs[:, span])
        top = jnp.max(score, axis=0, keepdims=True)
        shifted = score - top
        weight = jnp.exp(shifted)
        total = jnp.sum(weight, axis=0, keepdims=True)
        spread = jnp.sum(weight * shifted, axis=0, keepdims=True)
        for i in range(2):
            part = slice(i * shard, (i + 1) * shard)
            at = slice(2 * j + i, 2 * j + i + 1)
            stats[0, at, :] = top[:, part]
            stats[1, at, :] = total[:, part]
            stats[2, at, :] = spread[:, part]


def second_pass(cents, row_sq, rows, shard):
    n_k, width = cents.shape
    n_rows = rows.shape[0]
    return pl.pallas_call(
        functools.partial(second_kernel, shard),
        out_shape=jax.ShapeDtypeStruct((3, n_rows // shard, shard), jnp.float32),
        in_specs=[VMEM] * 3,
        out_specs=VMEM,
        compiler_params=params(),
        cost_estimate=pl.CostEstimate(
            flops=2 * n_k * n_rows * width, bytes_accessed=2 * n_rows * width, transcendentals=n_k * n_rows
        ),
        name="second_pass",
    )(cents, row_sq, rows)


def hold(*values):
    return lax.optimization_barrier(values)


def merge(a, b):
    top = jnp.maximum(a[0], b[0])
    drops = (a[0] - top, b[0] - top)
    factors = (jnp.exp(drops[0]), jnp.exp(drops[1]))
    out = [top, factors[0] * a[1] + factors[1] * b[1]]
    if a.shape[0] == 3:
        out.append(factors[0] * (a[2] + drops[0] * a[1]) + factors[1] * (b[2] + drops[1] * b[1]))
    return jnp.stack(out)


def solution(mesh):
    n_dp = mesh.shape["dp"]
    n_cent = mesh.shape["cent"]
    high = n_dp // 2
    top_bit = n_dp // 4

    def flip(value, bits):
        return lax.ppermute(value, "dp", [(i, i ^ bits) for i in range(n_dp)])

    def member(place):
        return (place & 3) | (high if place & 4 else 0)

    def rows_from(value, place):
        return flip(value, member(place))

    def across(value, bits):
        return lax.ppermute(value, "cent", [(i, i ^ bits) for i in range(n_cent)])

    def gather_cent(value):
        blocks = [value]
        bits = 1
        while bits < n_cent:
            blocks = blocks + [across(b, bits) for b in blocks]
            bits *= 2
        return blocks

    def scatter_cent(value):
        bits = n_cent // 2
        while bits:
            half = value.shape[0] // 2
            value = value[:half] + across(value[half:], bits)
            bits //= 2
        return value

    def gather_near(value):
        bits = 4
        while bits < top_bit:
            value = jnp.concatenate([value, flip(value, bits)], axis=0)
            bits *= 2
        return value

    def scatter_near(value):
        bits = top_bit // 2
        while bits >= 4:
            half = value.shape[0] // 2
            value = value[:half] + flip(value[half:], bits)
            bits //= 2
        return value

    def by_position(stats):
        place = lax.axis_index("dp")
        for bit in (1, 2, 4):
            swapped = jnp.stack([stats[:, b ^ bit] for b in range(CUBE)], axis=1)
            stats = jnp.where((place & member(bit)) != 0, swapped, stats)
        return stats

    def exchange(value):
        groups = [[i + member(place) for place in range(CUBE)] for i in range(0, high, 4)]
        return lax.all_to_all(value, "dp", 0, 0, axis_index_groups=groups)

    def everywhere(stats):
        return exchange(jnp.broadcast_to(stats[None], (CUBE,) + stats.shape))

    def to_owner(stats):
        return exchange(stats.transpose(1, 0, 2))

    def on_device(embeddings, centroids):
        shard, width = embeddings.shape
        half = shard // 2
        chunk = {0: embeddings.astype(jnp.bfloat16)}
        for bit in (4, 1, 2):
            chunk[bit] = rows_from(chunk[0], bit)
        chunk[3] = rows_from(chunk[1], 2)
        near_own = gather_near(rounded(centroids))
        far_own = flip(near_own, top_bit)
        near = gather_cent(near_own)
        n_near = len(near) * near_own.shape[0]
        far = gather_cent(far_own)
        chunk[4], chunk[2], far = hold(chunk[4], chunk[2], far)
        chunk[5] = rows_from(chunk[4], 1)
        chunk[6] = rows_from(chunk[4], 2)
        parts = (rows_from(chunk[3][:half], 4), rows_from(chunk[4][half:], 3))
        piece = jnp.concatenate(near + far, axis=0)
        passes = [first_pass(piece, [chunk[b] for b in range(4)], 0)]
        passes.append(first_pass(piece, [chunk[4], chunk[5]], 4 * shard, passes[0][2]))
        parts, passes = hold(parts, passes)
        passes.append(first_pass(piece, [chunk[6], *parts], 6 * shard, passes[1][2]))
        rows = passes[2][2]
        row_sq = jnp.concatenate([p[1] for p in passes], axis=1)

        stats = by_position(jnp.concatenate([p[0] for p in passes], axis=1))
        stats = everywhere(stats)
        top = jnp.max(stats[:, 0], axis=0)
        total = jnp.sum(stats[:, 1] * jnp.exp(stats[:, 0] - top), axis=0)
        stats = by_position(jnp.stack([top, total]))
        final = stats.reshape(2, CUBE * shard)

        far = scatter_cent(sums_pass(piece, final, row_sq, rows, n_near, 2 * n_near))
        count = far[:, width:]
        coarse = lax.reduce_precision(count, 8, 7)
        lane = lax.broadcasted_iota(jnp.int32, count.shape, 1)
        far = jnp.concatenate([far[:, :width], jnp.where(lane < 64, coarse, count - coarse)], axis=1)
        far = flip(far.astype(jnp.bfloat16), top_bit).astype(jnp.float32)
        near = scatter_cent(sums_pass(piece, final, row_sq, rows, 0, n_near, [centroids]))
        counts = far[:, width : width + 1] + far[:, width + 64 : width + 65]
        far = jnp.concatenate([far[:, :width], jnp.broadcast_to(counts, count.shape)], axis=1)
        sums = scatter_near(near + far)
        updated = sums[:, :width] / sums[:, width : width + 1]
        near_own = gather_near(updated.astype(jnp.bfloat16))
        far_own = flip(near_own, top_bit)
        stats = second_pass(jnp.concatenate(gather_cent(near_own), axis=0), row_sq, rows, shard)
        far_own, stats = hold(far_own, stats)
        far = gather_cent(far_own)
        stats = merge(stats, second_pass(far_own, row_sq, rows, shard))
        stats = merge(stats, second_pass(jnp.concatenate(far[1:], axis=0), row_sq, rows, shard))
        stats = to_owner(by_position(stats))
        drop = stats[:, 0] - jnp.max(stats[:, 0], axis=0)
        factor = jnp.exp(drop)
        total = jnp.sum(factor * stats[:, 1], axis=0)
        spread = jnp.sum(factor * (stats[:, 2] + drop * stats[:, 1]), axis=0)
        entropy = jnp.log(total) - spread / total
        return (updated, entropy)

    in_specs = (P(("dp", "cent"), None), P(("dp", "cent"), None))
    out_specs = (P(("dp", "cent"), None), P(("dp", "cent")))
    return jax.shard_map(
        on_device, mesh=mesh, in_specs=in_specs, out_specs=out_specs, check_vma=False
    )
```

```python
import functools

import jax
import jax.numpy as jnp
from jax import lax
from jax.experimental import pallas as pl
from jax.experimental.pallas import tpu as pltpu
from jax.sharding import PartitionSpec as P

softness_level = 32.0
prior_mass = 4.0
CUBE = 8
GROUPS = ((0, 1, 2, 3), (4, 5), (6, 7))
VMEM = pl.BlockSpec(memory_space=pltpu.VMEM)
GRANT = 12 << 20


def params(grant=GRANT):
    return pltpu.CompilerParams(vmem_limit_bytes=grant)


def row_squares(rows):
    wide = rows.astype(jnp.float32)
    square = wide * wide
    part = square[:, :128]
    for j in range(128, square.shape[1], 128):
        part = part + square[:, j : j + 128]
    return jnp.sum(part.T, axis=0, keepdims=True)


def centroid_squares(piece):
    wide = piece.astype(jnp.float32)
    return jnp.sum(wide * wide, axis=1, keepdims=True)


def scores(piece, cent_sq, rows, row_sq):
    inner = lax.dot_general(piece, rows, (((1,), (1,)), ((), ())), preferred_element_type=jnp.float32)
    scale = 0.5 / softness_level
    return (2.0 * scale) * inner - scale * row_sq - scale * cent_sq


def cast_kernel(n, *refs):
    sources, targets, held, sems = refs[:n], refs[n : 2 * n], refs[2 * n : 3 * n], refs[3 * n]
    copies = [pltpu.make_async_copy(sources[i], held[i], sems.at[i]) for i in range(n)]
    for copy in copies:
        copy.start()
    for copy, target, value in zip(copies, targets, held):
        copy.wait()
        target[...] = value[...].astype(target.dtype)


def rounded(*values):
    n = len(values)
    return pl.pallas_call(
        functools.partial(cast_kernel, n),
        out_shape=tuple(jax.ShapeDtypeStruct(v.shape, jnp.bfloat16) for v in values),
        in_specs=[pl.BlockSpec(memory_space=pltpu.HBM)] * n,
        out_specs=(VMEM,) * n,
        scratch_shapes=[pltpu.VMEM(v.shape, v.dtype) for v in values] + [pltpu.SemaphoreType.DMA((n,))],
        compiler_params=params(60 << 20),
        name="rounded",
    )(*values)


def first_kernel(n_chunks, n_before, shard, cents, *refs):
    chunks = refs[:n_chunks]
    stats_ref, row_sq_ref, rows_ref = refs[-3:]
    start = 0
    if n_before:
        start = n_before
        row_sq_ref[:, :start] = refs[n_chunks][...]
        rows_ref[:start, :] = refs[n_chunks + 1][...]
    at = start
    for chunk in chunks:
        rows_ref[at : at + chunk.shape[0], :] = chunk[...]
        at += chunk.shape[0]
    piece = cents[...]
    cent_sq = centroid_squares(piece)
    tile = 2 * shard
    for j in range((at - start) // tile):
        span = slice(start + j * tile, start + (j + 1) * tile)
        rows = rows_ref[span, :]
        row_sq = row_squares(rows)
        score = scores(piece, cent_sq, rows, row_sq)
        top = jnp.max(score, axis=0, keepdims=True)
        total = jnp.sum(jnp.exp(score - top), axis=0, keepdims=True)
        row_sq_ref[:, span] = row_sq
        for i in range(2):
            stats_ref[0, 2 * j + i : 2 * j + i + 1, :] = top[:, i * shard : (i + 1) * shard]
            stats_ref[1, 2 * j + i : 2 * j + i + 1, :] = total[:, i * shard : (i + 1) * shard]


def first_pass(cents, chunks, before=()):
    shard, width = chunks[0].shape
    n_k = cents.shape[0]
    n_rows = sum(c.shape[0] for c in chunks)
    n_before = before[1].shape[0] if before else 0
    return pl.pallas_call(
        functools.partial(first_kernel, len(chunks), n_before, shard),
        out_shape=(
            jax.ShapeDtypeStruct((2, n_rows // shard, shard), jnp.float32),
            jax.ShapeDtypeStruct((1, n_before + n_rows), jnp.float32),
            jax.ShapeDtypeStruct((n_before + n_rows, width), jnp.bfloat16),
        ),
        in_specs=[VMEM] * (1 + len(chunks) + len(before)),
        out_specs=(VMEM,) * 3,
        compiler_params=params(),
        cost_estimate=pl.CostEstimate(
            flops=2 * n_k * n_rows * width, bytes_accessed=2 * n_rows * width, transcendentals=n_k * n_rows
        ),
        name="first_pass",
    )(cents, *chunks, *before)


def sums_kernel(first, last, n, cents, *refs):
    stats, row_sqs, rows, priors = refs[:n], refs[n : 2 * n], refs[2 * n : 3 * n], refs[3 * n : -1]
    out_ref = refs[-1]
    width = cents.shape[1]
    piece = cents[first:last, :]
    cent_sq = centroid_squares(piece)
    counts = 0.0
    for s in range(n):
        score = scores(piece, cent_sq, rows[s][...], row_sqs[s][...])
        resp = (jnp.exp(score - stats[s][0:1, :]) * (1.0 / stats[s][1:2, :])).astype(jnp.bfloat16)
        counts = counts + jnp.sum(resp.astype(jnp.float32), axis=1, keepdims=True)
        part = jnp.dot(resp, rows[s][...], preferred_element_type=jnp.float32)
        if s:
            part = part + out_ref[:, :width]
        out_ref[:, :width] = part
    out_ref[:, width:] = jnp.broadcast_to(counts, (last - first, 128))
    for prior in priors:
        held = prior.shape[0]
        out_ref[:held, :width] += prior_mass * prior[...]
        out_ref[:held, width:] += prior_mass


def sums_pass(cents, stats, row_sqs, rows, first, last, priors=()):
    n = len(rows)
    width = rows[0].shape[1]
    n_rows = sum(r.shape[0] for r in rows)
    return pl.pallas_call(
        functools.partial(sums_kernel, first, last, n),
        out_shape=jax.ShapeDtypeStruct((last - first, width + 128), jnp.float32),
        in_specs=[VMEM] * (1 + 3 * n + len(priors)),
        out_specs=VMEM,
        compiler_params=params(),
        cost_estimate=pl.CostEstimate(
            flops=4 * (last - first) * n_rows * width,
            bytes_accessed=2 * n_rows * width,
            transcendentals=(last - first) * n_rows,
        ),
        name="sums_pass",
    )(cents, *stats, *row_sqs, *rows, *priors)


def second_kernel(shard, n, cents, *refs):
    row_sqs, rows, stats = refs[:n], refs[n : 2 * n], refs[2 * n :]
    piece = cents[...]
    cent_sq = centroid_squares(piece)
    tile = 2 * shard
    for s in range(n):
        for j in range(rows[s].shape[0] // tile):
            span = slice(j * tile, (j + 1) * tile)
            score = scores(piece, cent_sq, rows[s][span, :], row_sqs[s][:, span])
            top = jnp.max(score, axis=0, keepdims=True)
            shifted = score - top
            weight = jnp.exp(shifted)
            total = jnp.sum(weight, axis=0, keepdims=True)
            spread = jnp.sum(weight * shifted, axis=0, keepdims=True)
            for i in range(2):
                part = slice(i * shard, (i + 1) * shard)
                at = slice(2 * j + i, 2 * j + i + 1)
                stats[s][0, at, :] = top[:, part]
                stats[s][1, at, :] = total[:, part]
                stats[s][2, at, :] = spread[:, part]


def second_pass(cents, row_sqs, rows, shard):
    n = len(rows)
    n_k, width = cents.shape
    n_rows = sum(r.shape[0] for r in rows)
    out = pl.pallas_call(
        functools.partial(second_kernel, shard, n),
        out_shape=tuple(jax.ShapeDtypeStruct((3, r.shape[0] // shard, shard), jnp.float32) for r in rows),
        in_specs=[VMEM] * (1 + 2 * n),
        out_specs=(VMEM,) * n,
        compiler_params=params(),
        cost_estimate=pl.CostEstimate(
            flops=2 * n_k * n_rows * width, bytes_accessed=2 * n_rows * width, transcendentals=n_k * n_rows
        ),
        name="second_pass",
    )(cents, *row_sqs, *rows)
    return jnp.concatenate(out, axis=1)


def hold(*values):
    return lax.optimization_barrier(values)


def merge(a, b):
    top = jnp.maximum(a[0], b[0])
    drops = (a[0] - top, b[0] - top)
    factors = (jnp.exp(drops[0]), jnp.exp(drops[1]))
    out = [top, factors[0] * a[1] + factors[1] * b[1]]
    if a.shape[0] == 3:
        out.append(factors[0] * (a[2] + drops[0] * a[1]) + factors[1] * (b[2] + drops[1] * b[1]))
    return jnp.stack(out)


def solution(mesh):
    n_dp = mesh.shape["dp"]
    n_cent = mesh.shape["cent"]
    high = n_dp // 2
    top_bit = n_dp // 4

    def flip(value, bits):
        return lax.ppermute(value, "dp", [(i, i ^ bits) for i in range(n_dp)])

    def member(place):
        return (place & 3) | (high if place & 4 else 0)

    def rows_from(value, place):
        return flip(value, member(place))

    def across(value, bits):
        return lax.ppermute(value, "cent", [(i, i ^ bits) for i in range(n_cent)])

    def gather_cent(value):
        blocks = [value]
        bits = 1
        while bits < n_cent:
            blocks = blocks + [across(b, bits) for b in blocks]
            bits *= 2
        return blocks

    def scatter_cent(value):
        bits = n_cent // 2
        while bits:
            half = value.shape[0] // 2
            value = value[:half] + across(value[half:], bits)
            bits //= 2
        return value

    def gather_near(value):
        bits = 4
        while bits < top_bit:
            value = jnp.concatenate([value, flip(value, bits)], axis=0)
            bits *= 2
        return value

    def scatter_near(value):
        bits = top_bit // 2
        while bits >= 4:
            half = value.shape[0] // 2
            value = value[:half] + flip(value[half:], bits)
            bits //= 2
        return value

    def by_position(stats):
        place = lax.axis_index("dp")
        for bit in (1, 2, 4):
            swapped = jnp.stack([stats[:, b ^ bit] for b in range(CUBE)], axis=1)
            stats = jnp.where((place & member(bit)) != 0, swapped, stats)
        return stats

    def exchange(value):
        groups = [[i + member(place) for place in range(CUBE)] for i in range(0, high, 4)]
        return lax.all_to_all(value, "dp", 0, 0, axis_index_groups=groups)

    def everywhere(stats):
        return exchange(jnp.broadcast_to(stats[None], (CUBE,) + stats.shape))

    def to_owner(stats):
        return exchange(stats.transpose(1, 0, 2))

    def on_device(embeddings, centroids):
        shard, width = embeddings.shape
        half = shard // 2
        own, own_cents = rounded(embeddings, centroids)
        chunk = {0: own}
        for bit in (4, 1, 2):
            chunk[bit] = rows_from(chunk[0], bit)
        chunk[3] = rows_from(chunk[1], 2)
        near_own = gather_near(own_cents)
        far_own = flip(near_own, top_bit)
        near = gather_cent(near_own)
        n_near = len(near) * near_own.shape[0]
        far = gather_cent(far_own)
        chunk[4], chunk[3], chunk[2], far = hold(chunk[4], chunk[3], chunk[2], far)
        chunk[5] = rows_from(chunk[4], 1)
        chunk[6] = rows_from(chunk[4], 2)
        parts = (rows_from(chunk[3][:half], 4), rows_from(chunk[4][half:], 3))
        piece = jnp.concatenate(near + far, axis=0)
        passes = [first_pass(piece, [chunk[b] for b in bits]) for bits in GROUPS[:2]]
        parts, passes = hold(parts, passes)
        passes.append(first_pass(piece, [chunk[GROUPS[2][0]], *parts], passes[1][1:]))
        row_sqs, rows = zip(passes[0][1:], passes[2][1:])

        stats = by_position(jnp.concatenate([p[0] for p in passes], axis=1))
        stats = everywhere(stats)
        top = jnp.max(stats[:, 0], axis=0)
        total = jnp.sum(stats[:, 1] * jnp.exp(stats[:, 0] - top), axis=0)
        stats = by_position(jnp.stack([top, total]))
        final = [stats[:, i : i + 4].reshape(2, 4 * shard) for i in (0, 4)]

        far = scatter_cent(sums_pass(piece, final, row_sqs, rows, n_near, 2 * n_near))
        count = far[:, width:]
        coarse = lax.reduce_precision(count, 8, 7)
        lane = lax.broadcasted_iota(jnp.int32, count.shape, 1)
        far = jnp.concatenate([far[:, :width], jnp.where(lane < 64, coarse, count - coarse)], axis=1)
        far = flip(far.astype(jnp.bfloat16), top_bit).astype(jnp.float32)
        near = scatter_cent(sums_pass(piece, final, row_sqs, rows, 0, n_near, [centroids]))
        counts = far[:, width : width + 1] + far[:, width + 64 : width + 65]
        far = jnp.concatenate([far[:, :width], jnp.broadcast_to(counts, count.shape)], axis=1)
        sums = scatter_near(near + far)
        updated = sums[:, :width] / sums[:, width : width + 1]
        near_own = gather_near(updated.astype(jnp.bfloat16))
        far_own = flip(near_own, top_bit)
        stats = second_pass(jnp.concatenate(gather_cent(near_own), axis=0), row_sqs, rows, shard)
        far_own, stats = hold(far_own, stats)
        far = gather_cent(far_own)
        stats = merge(stats, second_pass(far_own, row_sqs, rows, shard))
        stats = merge(stats, second_pass(jnp.concatenate(far[1:], axis=0), row_sqs, rows, shard))
        stats = to_owner(by_position(stats))
        drop = stats[:, 0] - jnp.max(stats[:, 0], axis=0)
        factor = jnp.exp(drop)
        total = jnp.sum(factor * stats[:, 1], axis=0)
        spread = jnp.sum(factor * (stats[:, 2] + drop * stats[:, 1]), axis=0)
        entropy = jnp.log(total) - spread / total
        return (updated, entropy)

    in_specs = (P(("dp", "cent"), None), P(("dp", "cent"), None))
    out_specs = (P(("dp", "cent"), None), P(("dp", "cent")))
    return jax.shard_map(
        on_device, mesh=mesh, in_specs=in_specs, out_specs=out_specs, check_vma=False
    )
```

```python
import functools

import jax
import jax.numpy as jnp
from jax import lax
from jax.experimental import pallas as pl
from jax.experimental.pallas import tpu as pltpu
from jax.sharding import PartitionSpec as P

softness_level = 32.0
prior_mass = 4.0
CUBE = 8
GROUPS = ((0, 1, 2, 3), (4, 5), (6, 7))
VMEM = pl.BlockSpec(memory_space=pltpu.VMEM)
GRANT = 12 << 20


def params():
    return pltpu.CompilerParams(vmem_limit_bytes=GRANT)


def row_squares(rows):
    wide = rows.astype(jnp.float32)
    square = wide * wide
    part = square[:, :128]
    for j in range(128, square.shape[1], 128):
        part = part + square[:, j : j + 128]
    return jnp.sum(part.T, axis=0, keepdims=True)


def centroid_squares(piece):
    wide = piece.astype(jnp.float32)
    return jnp.sum(wide * wide, axis=1, keepdims=True)


def scores(piece, cent_sq, rows, row_sq):
    inner = lax.dot_general(piece, rows, (((1,), (1,)), ((), ())), preferred_element_type=jnp.float32)
    scale = 0.5 / softness_level
    return (2.0 * scale) * inner - scale * row_sq - scale * cent_sq


def first_kernel(n_chunks, shard, cents, *refs):
    chunks = refs[:n_chunks]
    stats_ref, row_sq_ref, rows_ref = refs[n_chunks:]
    at = 0
    for chunk in chunks:
        rows_ref[at : at + chunk.shape[0], :] = chunk[...]
        at += chunk.shape[0]
    piece = cents[...]
    cent_sq = centroid_squares(piece)
    tile = 2 * shard
    for j in range(at // tile):
        span = slice(j * tile, (j + 1) * tile)
        rows = rows_ref[span, :]
        row_sq = row_squares(rows)
        score = scores(piece, cent_sq, rows, row_sq)
        top = jnp.max(score, axis=0, keepdims=True)
        total = jnp.sum(jnp.exp(score - top), axis=0, keepdims=True)
        row_sq_ref[:, span] = row_sq
        for i in range(2):
            stats_ref[0, 2 * j + i : 2 * j + i + 1, :] = top[:, i * shard : (i + 1) * shard]
            stats_ref[1, 2 * j + i : 2 * j + i + 1, :] = total[:, i * shard : (i + 1) * shard]


def first_pass(cents, chunks):
    shard, width = chunks[0].shape
    n_k = cents.shape[0]
    n_rows = sum(c.shape[0] for c in chunks)
    return pl.pallas_call(
        functools.partial(first_kernel, len(chunks), shard),
        out_shape=(
            jax.ShapeDtypeStruct((2, n_rows // shard, shard), jnp.float32),
            jax.ShapeDtypeStruct((1, n_rows), jnp.float32),
            jax.ShapeDtypeStruct((n_rows, width), jnp.bfloat16),
        ),
        in_specs=[VMEM] * (1 + len(chunks)),
        out_specs=(VMEM,) * 3,
        compiler_params=params(),
        cost_estimate=pl.CostEstimate(
            flops=2 * n_k * n_rows * width, bytes_accessed=2 * n_rows * width, transcendentals=n_k * n_rows
        ),
        name="first_pass",
    )(cents, *chunks)


def sums_kernel(first, last, n, cents, *refs):
    stats, row_sqs, rows, priors = refs[:n], refs[n : 2 * n], refs[2 * n : 3 * n], refs[3 * n : -1]
    out_ref = refs[-1]
    width = cents.shape[1]
    piece = cents[first:last, :]
    cent_sq = centroid_squares(piece)
    counts = 0.0
    for s in range(n):
        score = scores(piece, cent_sq, rows[s][...], row_sqs[s][...])
        resp = (jnp.exp(score - stats[s][0:1, :]) * (1.0 / stats[s][1:2, :])).astype(jnp.bfloat16)
        counts = counts + jnp.sum(resp.astype(jnp.float32), axis=1, keepdims=True)
        part = jnp.dot(resp, rows[s][...], preferred_element_type=jnp.float32)
        if s:
            part = part + out_ref[:, :width]
        out_ref[:, :width] = part
    out_ref[:, width:] = jnp.broadcast_to(counts, (last - first, 128))
    for prior in priors:
        held = prior.shape[0]
        out_ref[:held, :width] += prior_mass * prior[...]
        out_ref[:held, width:] += prior_mass


def sums_pass(cents, stats, row_sqs, rows, first, last, priors=()):
    n = len(rows)
    width = rows[0].shape[1]
    n_rows = sum(r.shape[0] for r in rows)
    return pl.pallas_call(
        functools.partial(sums_kernel, first, last, n),
        out_shape=jax.ShapeDtypeStruct((last - first, width + 128), jnp.float32),
        in_specs=[VMEM] * (1 + 3 * n + len(priors)),
        out_specs=VMEM,
        compiler_params=params(),
        cost_estimate=pl.CostEstimate(
            flops=4 * (last - first) * n_rows * width,
            bytes_accessed=2 * n_rows * width,
            transcendentals=(last - first) * n_rows,
        ),
        name="sums_pass",
    )(cents, *stats, *row_sqs, *rows, *priors)


def second_kernel(shard, n, cents, *refs):
    row_sqs, rows, stats = refs[:n], refs[n : 2 * n], refs[2 * n :]
    piece = cents[...]
    cent_sq = centroid_squares(piece)
    tile = 2 * shard
    for s in range(n):
        for j in range(rows[s].shape[0] // tile):
            span = slice(j * tile, (j + 1) * tile)
            score = scores(piece, cent_sq, rows[s][span, :], row_sqs[s][:, span])
            top = jnp.max(score, axis=0, keepdims=True)
            shifted = score - top
            weight = jnp.exp(shifted)
            total = jnp.sum(weight, axis=0, keepdims=True)
            spread = jnp.sum(weight * shifted, axis=0, keepdims=True)
            for i in range(2):
                part = slice(i * shard, (i + 1) * shard)
                at = slice(2 * j + i, 2 * j + i + 1)
                stats[s][0, at, :] = top[:, part]
                stats[s][1, at, :] = total[:, part]
                stats[s][2, at, :] = spread[:, part]


def second_pass(cents, row_sqs, rows, shard):
    n = len(rows)
    n_k, width = cents.shape
    n_rows = sum(r.shape[0] for r in rows)
    out = pl.pallas_call(
        functools.partial(second_kernel, shard, n),
        out_shape=tuple(jax.ShapeDtypeStruct((3, r.shape[0] // shard, shard), jnp.float32) for r in rows),
        in_specs=[VMEM] * (1 + 2 * n),
        out_specs=(VMEM,) * n,
        compiler_params=params(),
        cost_estimate=pl.CostEstimate(
            flops=2 * n_k * n_rows * width, bytes_accessed=2 * n_rows * width, transcendentals=n_k * n_rows
        ),
        name="second_pass",
    )(cents, *row_sqs, *rows)
    return by_chunk(out)


def hold(*values):
    return lax.optimization_barrier(values)


def merge(a, b):
    top = jnp.maximum(a[0], b[0])
    drops = (a[0] - top, b[0] - top)
    factors = (jnp.exp(drops[0]), jnp.exp(drops[1]))
    out = [top, factors[0] * a[1] + factors[1] * b[1]]
    if a.shape[0] == 3:
        out.append(factors[0] * (a[2] + drops[0] * a[1]) + factors[1] * (b[2] + drops[1] * b[1]))
    return jnp.stack(out)


def by_chunk(groups):
    place = {b: (g, i) for g, bits in enumerate(GROUPS) for i, b in enumerate(bits)}
    return jnp.stack([groups[place[b][0]][:, place[b][1]] for b in range(CUBE)], axis=1)


def solution(mesh):
    n_dp = mesh.shape["dp"]
    n_cent = mesh.shape["cent"]
    high = n_dp // 2
    top_bit = n_dp // 4

    def flip(value, bits):
        return lax.ppermute(value, "dp", [(i, i ^ bits) for i in range(n_dp)])

    def member(place):
        return (place & 3) | (high if place & 4 else 0)

    def rows_from(value, place):
        return flip(value, member(place))

    def across(value, bits):
        return lax.ppermute(value, "cent", [(i, i ^ bits) for i in range(n_cent)])

    def gather_cent(value, cuts=1):
        cuts = cuts if value.shape[0] % (16 * cuts) == 0 else 1
        blocks = jnp.split(value, cuts, axis=0)
        bits = 1
        while bits < n_cent:
            blocks = blocks + [across(b, bits) for b in blocks]
            bits *= 2
        return blocks

    def scatter_cent(value):
        bits = n_cent // 2
        while bits:
            half = value.shape[0] // 2
            value = value[:half] + across(value[half:], bits)
            bits //= 2
        return value

    def gather_near(value):
        bits = 4
        while bits < top_bit:
            value = jnp.concatenate([value, flip(value, bits)], axis=0)
            bits *= 2
        return value

    def scatter_near(value):
        bits = top_bit // 2
        while bits >= 4:
            half = value.shape[0] // 2
            value = value[:half] + flip(value[half:], bits)
            bits //= 2
        return value

    def by_position(stats):
        place = lax.axis_index("dp")
        for bit in (1, 2, 4):
            swapped = jnp.stack([stats[:, b ^ bit] for b in range(CUBE)], axis=1)
            stats = jnp.where((place & member(bit)) != 0, swapped, stats)
        return stats

    def exchange(value):
        groups = [[i + member(place) for place in range(CUBE)] for i in range(0, high, 4)]
        return lax.all_to_all(value, "dp", 0, 0, axis_index_groups=groups)

    def everywhere(stats):
        return exchange(jnp.broadcast_to(stats[None], (CUBE,) + stats.shape))

    def to_owner(stats):
        return exchange(stats.transpose(1, 0, 2))

    def on_device(embeddings, centroids):
        shard, width = embeddings.shape
        half = shard // 2
        chunk = {0: embeddings.astype(jnp.bfloat16)}
        for bit in (4, 1, 2):
            chunk[bit] = rows_from(chunk[0], bit)
        chunk[3] = rows_from(chunk[1], 2)
        near_own = gather_near(centroids.astype(jnp.bfloat16))
        far_own = flip(near_own, top_bit)
        near = gather_cent(near_own)
        n_near = len(near) * near_own.shape[0]
        far = gather_cent(far_own, 2)
        chunk[4], chunk[3], chunk[2], far = hold(chunk[4], chunk[3], chunk[2], far)
        chunk[5] = rows_from(chunk[4], 1)
        chunk[6] = rows_from(chunk[4], 2)
        parts = (rows_from(chunk[3][:half], 4), rows_from(chunk[4][half:], 3))
        piece = jnp.concatenate(near + far, axis=0)
        passes = [first_pass(piece, [chunk[b] for b in bits]) for bits in GROUPS[:2]]
        parts, passes = hold(parts, passes)
        passes.append(first_pass(piece, [chunk[GROUPS[2][0]], *parts]))
        local, row_sqs, rows = zip(*passes)

        stats = by_position(by_chunk(local))
        stats = everywhere(stats)
        top = jnp.max(stats[:, 0], axis=0)
        total = jnp.sum(stats[:, 1] * jnp.exp(stats[:, 0] - top), axis=0)
        stats = by_position(jnp.stack([top, total]))
        final = [jnp.concatenate([stats[:, b] for b in bits], axis=1) for bits in GROUPS]

        far = scatter_cent(sums_pass(piece, final, row_sqs, rows, n_near, 2 * n_near))
        count = far[:, width:]
        coarse = lax.reduce_precision(count, 8, 7)
        lane = lax.broadcasted_iota(jnp.int32, count.shape, 1)
        far = jnp.concatenate([far[:, :width], jnp.where(lane < 64, coarse, count - coarse)], axis=1)
        far = flip(far.astype(jnp.bfloat16), top_bit).astype(jnp.float32)
        near = scatter_cent(sums_pass(piece, final, row_sqs, rows, 0, n_near, [centroids]))
        counts = far[:, width : width + 1] + far[:, width + 64 : width + 65]
        far = jnp.concatenate([far[:, :width], jnp.broadcast_to(counts, count.shape)], axis=1)
        sums = scatter_near(near + far)
        updated = sums[:, :width] / sums[:, width : width + 1]
        near_own = gather_near(updated.astype(jnp.bfloat16))
        far_own = flip(near_own, top_bit)
        stats = second_pass(jnp.concatenate(gather_cent(near_own), axis=0), row_sqs, rows, shard)
        far_own, stats = hold(far_own, stats)
        far = gather_cent(far_own)
        stats = merge(stats, second_pass(far_own, row_sqs, rows, shard))
        stats = merge(stats, second_pass(jnp.concatenate(far[1:], axis=0), row_sqs, rows, shard))
        stats = to_owner(by_position(stats))
        drop = stats[:, 0] - jnp.max(stats[:, 0], axis=0)
        factor = jnp.exp(drop)
        total = jnp.sum(factor * stats[:, 1], axis=0)
        spread = jnp.sum(factor * (stats[:, 2] + drop * stats[:, 1]), axis=0)
        entropy = jnp.log(total) - spread / total
        return (updated, entropy)

    in_specs = (P(("dp", "cent"), None), P(("dp", "cent"), None))
    out_specs = (P(("dp", "cent"), None), P(("dp", "cent")))
    return jax.shard_map(
        on_device, mesh=mesh, in_specs=in_specs, out_specs=out_specs, check_vma=False
    )
```

```python
import functools

import jax
import jax.numpy as jnp
from jax import lax
from jax.experimental import pallas as pl
from jax.experimental.pallas import tpu as pltpu
from jax.sharding import PartitionSpec as P

softness_level = 32.0
prior_mass = 4.0
CUBE = 8
GROUPS = ((0, 1, 2, 3), (4, 5), (6, 7))
VMEM = pl.BlockSpec(memory_space=pltpu.VMEM)
GRANT = 12 << 20


def params():
    return pltpu.CompilerParams(vmem_limit_bytes=GRANT)


def row_squares(rows):
    wide = rows.astype(jnp.float32)
    square = wide * wide
    part = square[:, :128]
    for j in range(128, square.shape[1], 128):
        part = part + square[:, j : j + 128]
    return jnp.sum(part.T, axis=0, keepdims=True)


def centroid_squares(piece):
    wide = piece.astype(jnp.float32)
    return jnp.sum(wide * wide, axis=1, keepdims=True)


def scores(piece, cent_sq, rows, row_sq):
    inner = lax.dot_general(piece, rows, (((1,), (1,)), ((), ())), preferred_element_type=jnp.float32)
    scale = 0.5 / softness_level
    return (2.0 * scale) * inner - scale * row_sq - scale * cent_sq


def first_kernel(n_chunks, shard, cents, *refs):
    chunks = refs[:n_chunks]
    stats_ref, row_sq_ref, rows_ref = refs[n_chunks:]
    at = 0
    for chunk in chunks:
        rows_ref[at : at + chunk.shape[0], :] = chunk[...]
        at += chunk.shape[0]
    piece = cents[...]
    cent_sq = centroid_squares(piece)
    tile = 2 * shard
    for j in range(at // tile):
        span = slice(j * tile, (j + 1) * tile)
        rows = rows_ref[span, :]
        row_sq = row_squares(rows)
        score = scores(piece, cent_sq, rows, row_sq)
        top = jnp.max(score, axis=0, keepdims=True)
        total = jnp.sum(jnp.exp(score - top), axis=0, keepdims=True)
        row_sq_ref[:, span] = row_sq
        for i in range(2):
            stats_ref[0, 2 * j + i : 2 * j + i + 1, :] = top[:, i * shard : (i + 1) * shard]
            stats_ref[1, 2 * j + i : 2 * j + i + 1, :] = total[:, i * shard : (i + 1) * shard]


def first_pass(cents, chunks):
    shard, width = chunks[0].shape
    n_k = cents.shape[0]
    n_rows = sum(c.shape[0] for c in chunks)
    return pl.pallas_call(
        functools.partial(first_kernel, len(chunks), shard),
        out_shape=(
            jax.ShapeDtypeStruct((2, n_rows // shard, shard), jnp.float32),
            jax.ShapeDtypeStruct((1, n_rows), jnp.float32),
            jax.ShapeDtypeStruct((n_rows, width), jnp.bfloat16),
        ),
        in_specs=[VMEM] * (1 + len(chunks)),
        out_specs=(VMEM,) * 3,
        compiler_params=params(),
        cost_estimate=pl.CostEstimate(
            flops=2 * n_k * n_rows * width, bytes_accessed=2 * n_rows * width, transcendentals=n_k * n_rows
        ),
        name="first_pass",
    )(cents, *chunks)


def sums_kernel(first, last, n, cents, *refs):
    stats, row_sqs, rows, priors = refs[:n], refs[n : 2 * n], refs[2 * n : 3 * n], refs[3 * n : -1]
    out_ref = refs[-1]
    width = cents.shape[1]
    piece = cents[first:last, :]
    cent_sq = centroid_squares(piece)
    counts = 0.0
    for s in range(n):
        score = scores(piece, cent_sq, rows[s][...], row_sqs[s][...])
        resp = (jnp.exp(score - stats[s][0:1, :]) * (1.0 / stats[s][1:2, :])).astype(jnp.bfloat16)
        counts = counts + jnp.sum(resp.astype(jnp.float32), axis=1, keepdims=True)
        part = jnp.dot(resp, rows[s][...], preferred_element_type=jnp.float32)
        if s:
            part = part + out_ref[:, :width]
        out_ref[:, :width] = part
    out_ref[:, width:] = jnp.broadcast_to(counts, (last - first, 128))
    for prior in priors:
        held = prior.shape[0]
        out_ref[:held, :width] += prior_mass * prior[...]
        out_ref[:held, width:] += prior_mass


def sums_pass(cents, stats, row_sqs, rows, first, last, priors=()):
    n = len(rows)
    width = rows[0].shape[1]
    n_rows = sum(r.shape[0] for r in rows)
    return pl.pallas_call(
        functools.partial(sums_kernel, first, last, n),
        out_shape=jax.ShapeDtypeStruct((last - first, width + 128), jnp.float32),
        in_specs=[VMEM] * (1 + 3 * n + len(priors)),
        out_specs=VMEM,
        compiler_params=params(),
        cost_estimate=pl.CostEstimate(
            flops=4 * (last - first) * n_rows * width,
            bytes_accessed=2 * n_rows * width,
            transcendentals=(last - first) * n_rows,
        ),
        name="sums_pass",
    )(cents, *stats, *row_sqs, *rows, *priors)


def second_kernel(shard, n, cents, *refs):
    row_sqs, rows, stats = refs[:n], refs[n : 2 * n], refs[2 * n :]
    piece = cents[...]
    cent_sq = centroid_squares(piece)
    tile = 2 * shard
    for s in range(n):
        for j in range(rows[s].shape[0] // tile):
            span = slice(j * tile, (j + 1) * tile)
            score = scores(piece, cent_sq, rows[s][span, :], row_sqs[s][:, span])
            top = jnp.max(score, axis=0, keepdims=True)
            shifted = score - top
            weight = jnp.exp(shifted)
            total = jnp.sum(weight, axis=0, keepdims=True)
            spread = jnp.sum(weight * shifted, axis=0, keepdims=True)
            for i in range(2):
                part = slice(i * shard, (i + 1) * shard)
                at = slice(2 * j + i, 2 * j + i + 1)
                stats[s][0, at, :] = top[:, part]
                stats[s][1, at, :] = total[:, part]
                stats[s][2, at, :] = spread[:, part]


def second_pass(cents, row_sqs, rows, shard):
    n = len(rows)
    n_k, width = cents.shape
    n_rows = sum(r.shape[0] for r in rows)
    out = pl.pallas_call(
        functools.partial(second_kernel, shard, n),
        out_shape=tuple(jax.ShapeDtypeStruct((3, r.shape[0] // shard, shard), jnp.float32) for r in rows),
        in_specs=[VMEM] * (1 + 2 * n),
        out_specs=(VMEM,) * n,
        compiler_params=params(),
        cost_estimate=pl.CostEstimate(
            flops=2 * n_k * n_rows * width, bytes_accessed=2 * n_rows * width, transcendentals=n_k * n_rows
        ),
        name="second_pass",
    )(cents, *row_sqs, *rows)
    return by_chunk(out)


def hold(*values):
    return lax.optimization_barrier(values)


def merge(a, b):
    top = jnp.maximum(a[0], b[0])
    drops = (a[0] - top, b[0] - top)
    factors = (jnp.exp(drops[0]), jnp.exp(drops[1]))
    out = [top, factors[0] * a[1] + factors[1] * b[1]]
    if a.shape[0] == 3:
        out.append(factors[0] * (a[2] + drops[0] * a[1]) + factors[1] * (b[2] + drops[1] * b[1]))
    return jnp.stack(out)


def by_chunk(groups):
    place = {b: (g, i) for g, bits in enumerate(GROUPS) for i, b in enumerate(bits)}
    return jnp.stack([groups[place[b][0]][:, place[b][1]] for b in range(CUBE)], axis=1)


def solution(mesh):
    n_dp = mesh.shape["dp"]
    n_cent = mesh.shape["cent"]
    high = n_dp // 2
    top_bit = n_dp // 4

    def flip(value, bits):
        return lax.ppermute(value, "dp", [(i, i ^ bits) for i in range(n_dp)])

    def member(place):
        return (place & 3) | (high if place & 4 else 0)

    def rows_from(value, place):
        return flip(value, member(place))

    def across(value, bits):
        return lax.ppermute(value, "cent", [(i, i ^ bits) for i in range(n_cent)])

    def gather_cent(value):
        blocks = [value]
        bits = 1
        while bits < n_cent:
            blocks = blocks + [across(b, bits) for b in blocks]
            bits *= 2
        return blocks

    def scatter_cent(value, other=None):
        bits = n_cent // 2
        while bits:
            half = value.shape[0] // 2
            if other is not None:
                value, other = value + across(other, bits), None
            else:
                value = value[:half] + across(value[half:], bits)
            bits //= 2
        return value

    def gather_near(value):
        bits = 4
        while bits < top_bit:
            value = jnp.concatenate([value, flip(value, bits)], axis=0)
            bits *= 2
        return value

    def scatter_near(value):
        bits = top_bit // 2
        while bits >= 4:
            half = value.shape[0] // 2
            value = value[:half] + flip(value[half:], bits)
            bits //= 2
        return value

    def by_position(stats):
        place = lax.axis_index("dp")
        for bit in (1, 2, 4):
            swapped = jnp.stack([stats[:, b ^ bit] for b in range(CUBE)], axis=1)
            stats = jnp.where((place & member(bit)) != 0, swapped, stats)
        return stats

    def exchange(value):
        groups = [[i + member(place) for place in range(CUBE)] for i in range(0, high, 4)]
        return lax.all_to_all(value, "dp", 0, 0, axis_index_groups=groups)

    def everywhere(stats):
        return exchange(jnp.broadcast_to(stats[None], (CUBE,) + stats.shape))

    def to_owner(stats):
        return exchange(stats.transpose(1, 0, 2))

    def on_device(embeddings, centroids):
        shard, width = embeddings.shape
        half = shard // 2
        chunk = {0: embeddings.astype(jnp.bfloat16)}
        for bit in (4, 1, 2):
            chunk[bit] = rows_from(chunk[0], bit)
        chunk[3] = rows_from(chunk[1], 2)
        near_own = gather_near(centroids.astype(jnp.bfloat16))
        far_own = flip(near_own, top_bit)
        near = gather_cent(near_own)
        n_near = len(near) * near_own.shape[0]
        far = gather_cent(far_own)
        chunk[4], chunk[3], chunk[2], far = hold(chunk[4], chunk[3], chunk[2], far)
        chunk[5] = rows_from(chunk[4], 1)
        chunk[6] = rows_from(chunk[4], 2)
        parts = (rows_from(chunk[3][:half], 4), rows_from(chunk[4][half:], 3))
        piece = jnp.concatenate(near + far, axis=0)
        passes = [first_pass(piece, [chunk[b] for b in bits]) for bits in GROUPS[:2]]
        parts, passes = hold(parts, passes)
        passes.append(first_pass(piece, [chunk[GROUPS[2][0]], *parts]))
        local, row_sqs, rows = zip(*passes)

        stats = by_position(by_chunk(local))
        stats = everywhere(stats)
        top = jnp.max(stats[:, 0], axis=0)
        total = jnp.sum(stats[:, 1] * jnp.exp(stats[:, 0] - top), axis=0)
        stats = by_position(jnp.stack([top, total]))
        final = [jnp.concatenate([stats[:, b] for b in bits], axis=1) for bits in GROUPS]

        far = scatter_cent(sums_pass(piece, final, row_sqs, rows, n_near, 2 * n_near))
        count = far[:, width:]
        coarse = lax.reduce_precision(count, 8, 7)
        lane = lax.broadcasted_iota(jnp.int32, count.shape, 1)
        far = jnp.concatenate([far[:, :width], jnp.where(lane < 64, coarse, count - coarse)], axis=1)
        far = far.astype(jnp.bfloat16)
        n_half = n_near // 2
        other = sums_pass(piece, final, row_sqs, rows, n_half, n_near)
        near = sums_pass(piece, hold(final, far)[0], row_sqs, rows, 0, n_half, [centroids])
        near = scatter_cent(near, other)
        far = flip(far, top_bit).astype(jnp.float32)
        counts = far[:, width : width + 1] + far[:, width + 64 : width + 65]
        far = jnp.concatenate([far[:, :width], jnp.broadcast_to(counts, count.shape)], axis=1)
        sums = scatter_near(near + far)
        updated = sums[:, :width] / sums[:, width : width + 1]
        near_own = gather_near(updated.astype(jnp.bfloat16))
        far_own = flip(near_own, top_bit)
        stats = second_pass(jnp.concatenate(gather_cent(near_own), axis=0), row_sqs, rows, shard)
        far_own, stats = hold(far_own, stats)
        far = gather_cent(far_own)
        stats = merge(stats, second_pass(far_own, row_sqs, rows, shard))
        stats = merge(stats, second_pass(jnp.concatenate(far[1:], axis=0), row_sqs, rows, shard))
        stats = to_owner(by_position(stats))
        drop = stats[:, 0] - jnp.max(stats[:, 0], axis=0)
        factor = jnp.exp(drop)
        total = jnp.sum(factor * stats[:, 1], axis=0)
        spread = jnp.sum(factor * (stats[:, 2] + drop * stats[:, 1]), axis=0)
        entropy = jnp.log(total) - spread / total
        return (updated, entropy)

    in_specs = (P(("dp", "cent"), None), P(("dp", "cent"), None))
    out_specs = (P(("dp", "cent"), None), P(("dp", "cent")))
    return jax.shard_map(
        on_device, mesh=mesh, in_specs=in_specs, out_specs=out_specs, check_vma=False
    )
```

```python
import functools

import jax
import jax.numpy as jnp
from jax import lax
from jax.experimental import pallas as pl
from jax.experimental.pallas import tpu as pltpu
from jax.sharding import PartitionSpec as P

softness_level = 32.0
prior_mass = 4.0
CUBE = 8
GROUPS = ((0, 1, 2, 3), (4, 5), (6, 7))
VMEM = pl.BlockSpec(memory_space=pltpu.VMEM)
GRANT = 12 << 20


def params():
    return pltpu.CompilerParams(vmem_limit_bytes=GRANT)


def row_squares(rows):
    wide = rows.astype(jnp.float32)
    square = wide * wide
    part = square[:, :128]
    for j in range(128, square.shape[1], 128):
        part = part + square[:, j : j + 128]
    return jnp.sum(part.T, axis=0, keepdims=True)


def centroid_squares(piece):
    wide = piece.astype(jnp.float32)
    return jnp.sum(wide * wide, axis=1, keepdims=True)


def scores(piece, cent_sq, rows, row_sq):
    inner = lax.dot_general(piece, rows, (((1,), (1,)), ((), ())), preferred_element_type=jnp.float32)
    scale = 0.5 / softness_level
    return (2.0 * scale) * inner - scale * row_sq - scale * cent_sq


def first_kernel(n_chunks, shard, cents, *refs):
    chunks = refs[:n_chunks]
    stats_ref, row_sq_ref, rows_ref = refs[n_chunks:]
    at = 0
    for chunk in chunks:
        rows_ref[at : at + chunk.shape[0], :] = chunk[...]
        at += chunk.shape[0]
    piece = cents[...]
    cent_sq = centroid_squares(piece)
    tile = 2 * shard
    for j in range(at // tile):
        span = slice(j * tile, (j + 1) * tile)
        rows = rows_ref[span, :]
        row_sq = row_squares(rows)
        score = scores(piece, cent_sq, rows, row_sq)
        top = jnp.max(score, axis=0, keepdims=True)
        total = jnp.sum(jnp.exp(score - top), axis=0, keepdims=True)
        row_sq_ref[:, span] = row_sq
        for i in range(2):
            stats_ref[0, 2 * j + i : 2 * j + i + 1, :] = top[:, i * shard : (i + 1) * shard]
            stats_ref[1, 2 * j + i : 2 * j + i + 1, :] = total[:, i * shard : (i + 1) * shard]


def first_pass(cents, chunks):
    shard, width = chunks[0].shape
    n_k = cents.shape[0]
    n_rows = sum(c.shape[0] for c in chunks)
    return pl.pallas_call(
        functools.partial(first_kernel, len(chunks), shard),
        out_shape=(
            jax.ShapeDtypeStruct((2, n_rows // shard, shard), jnp.float32),
            jax.ShapeDtypeStruct((1, n_rows), jnp.float32),
            jax.ShapeDtypeStruct((n_rows, width), jnp.bfloat16),
        ),
        in_specs=[VMEM] * (1 + len(chunks)),
        out_specs=(VMEM,) * 3,
        compiler_params=params(),
        cost_estimate=pl.CostEstimate(
            flops=2 * n_k * n_rows * width, bytes_accessed=2 * n_rows * width, transcendentals=n_k * n_rows
        ),
        name="first_pass",
    )(cents, *chunks)


def sums_kernel(first, last, n, cents, *refs):
    stats, row_sqs, rows, priors = refs[:n], refs[n : 2 * n], refs[2 * n : 3 * n], refs[3 * n : -1]
    out_ref = refs[-1]
    width = cents.shape[1]
    piece = cents[first:last, :]
    cent_sq = centroid_squares(piece)
    counts = 0.0
    for s in range(n):
        score = scores(piece, cent_sq, rows[s][...], row_sqs[s][...])
        resp = (jnp.exp(score - stats[s][0:1, :]) * (1.0 / stats[s][1:2, :])).astype(jnp.bfloat16)
        counts = counts + jnp.sum(resp.astype(jnp.float32), axis=1, keepdims=True)
        part = jnp.dot(resp, rows[s][...], preferred_element_type=jnp.float32)
        if s:
            part = part + out_ref[:, :width]
        out_ref[:, :width] = part
    out_ref[:, width:] = jnp.broadcast_to(counts, (last - first, 128))
    for prior in priors:
        held = prior.shape[0]
        out_ref[:held, :width] += prior_mass * prior[...]
        out_ref[:held, width:] += prior_mass


def sums_pass(cents, stats, row_sqs, rows, first, last, priors=()):
    n = len(rows)
    width = rows[0].shape[1]
    n_rows = sum(r.shape[0] for r in rows)
    return pl.pallas_call(
        functools.partial(sums_kernel, first, last, n),
        out_shape=jax.ShapeDtypeStruct((last - first, width + 128), jnp.float32),
        in_specs=[VMEM] * (1 + 3 * n + len(priors)),
        out_specs=VMEM,
        compiler_params=params(),
        cost_estimate=pl.CostEstimate(
            flops=4 * (last - first) * n_rows * width,
            bytes_accessed=2 * n_rows * width,
            transcendentals=(last - first) * n_rows,
        ),
        name="sums_pass",
    )(cents, *stats, *row_sqs, *rows, *priors)


def second_kernel(shard, n, cents, *refs):
    row_sqs, rows, stats = refs[:n], refs[n : 2 * n], refs[2 * n :]
    piece = cents[...]
    cent_sq = centroid_squares(piece)
    tile = 2 * shard
    for s in range(n):
        for j in range(rows[s].shape[0] // tile):
            span = slice(j * tile, (j + 1) * tile)
            score = scores(piece, cent_sq, rows[s][span, :], row_sqs[s][:, span])
            top = jnp.max(score, axis=0, keepdims=True)
            shifted = score - top
            weight = jnp.exp(shifted)
            total = jnp.sum(weight, axis=0, keepdims=True)
            spread = jnp.sum(weight * shifted, axis=0, keepdims=True)
            for i in range(2):
                part = slice(i * shard, (i + 1) * shard)
                at = slice(2 * j + i, 2 * j + i + 1)
                stats[s][0, at, :] = top[:, part]
                stats[s][1, at, :] = total[:, part]
                stats[s][2, at, :] = spread[:, part]


def second_pass(cents, row_sqs, rows, shard):
    n = len(rows)
    n_k, width = cents.shape
    n_rows = sum(r.shape[0] for r in rows)
    out = pl.pallas_call(
        functools.partial(second_kernel, shard, n),
        out_shape=tuple(jax.ShapeDtypeStruct((3, r.shape[0] // shard, shard), jnp.float32) for r in rows),
        in_specs=[VMEM] * (1 + 2 * n),
        out_specs=(VMEM,) * n,
        compiler_params=params(),
        cost_estimate=pl.CostEstimate(
            flops=2 * n_k * n_rows * width, bytes_accessed=2 * n_rows * width, transcendentals=n_k * n_rows
        ),
        name="second_pass",
    )(cents, *row_sqs, *rows)
    return by_chunk(out)


def hold(*values):
    return lax.optimization_barrier(values)


def merge(a, b):
    top = jnp.maximum(a[0], b[0])
    drops = (a[0] - top, b[0] - top)
    factors = (jnp.exp(drops[0]), jnp.exp(drops[1]))
    out = [top, factors[0] * a[1] + factors[1] * b[1]]
    if a.shape[0] == 3:
        out.append(factors[0] * (a[2] + drops[0] * a[1]) + factors[1] * (b[2] + drops[1] * b[1]))
    return jnp.stack(out)


def by_chunk(groups):
    place = {b: (g, i) for g, bits in enumerate(GROUPS) for i, b in enumerate(bits)}
    return jnp.stack([groups[place[b][0]][:, place[b][1]] for b in range(CUBE)], axis=1)


def solution(mesh):
    n_dp = mesh.shape["dp"]
    n_cent = mesh.shape["cent"]
    high = n_dp // 2
    top_bit = n_dp // 4

    def flip(value, bits):
        return lax.ppermute(value, "dp", [(i, i ^ bits) for i in range(n_dp)])

    def member(place):
        return (place & 3) | (high if place & 4 else 0)

    def rows_from(value, place):
        return flip(value, member(place))

    def across(value, bits):
        return lax.ppermute(value, "cent", [(i, i ^ bits) for i in range(n_cent)])

    def gather_cent(value):
        blocks = [value]
        bits = 1
        while bits < n_cent:
            blocks = blocks + [across(b, bits) for b in blocks]
            bits *= 2
        return blocks

    def scatter_cent(value, other=None):
        bits = n_cent // 2
        while bits:
            half = value.shape[0] // 2
            if other is not None:
                value, other = value + across(other, bits), None
            else:
                value = value[:half] + across(value[half:], bits)
            bits //= 2
        return value

    def gather_near(value):
        bits = 4
        while bits < top_bit:
            value = jnp.concatenate([value, flip(value, bits)], axis=0)
            bits *= 2
        return value

    def scatter_near(value):
        bits = top_bit // 2
        while bits >= 4:
            half = value.shape[0] // 2
            value = value[:half] + flip(value[half:], bits)
            bits //= 2
        return value

    def by_position(stats):
        place = lax.axis_index("dp")
        for bit in (1, 2, 4):
            swapped = jnp.stack([stats[:, b ^ bit] for b in range(CUBE)], axis=1)
            stats = jnp.where((place & member(bit)) != 0, swapped, stats)
        return stats

    def exchange(value):
        groups = [[i + member(place) for place in range(CUBE)] for i in range(0, high, 4)]
        return lax.all_to_all(value, "dp", 0, 0, axis_index_groups=groups)

    def everywhere(stats):
        return exchange(jnp.broadcast_to(stats[None], (CUBE,) + stats.shape))

    def to_owner(stats):
        return exchange(stats.transpose(1, 0, 2))

    def on_device(embeddings, centroids):
        shard, width = embeddings.shape
        half = shard // 2
        chunk = {0: embeddings.astype(jnp.bfloat16)}
        for bit in (4, 1, 2):
            chunk[bit] = rows_from(chunk[0], bit)
        chunk[3] = rows_from(chunk[1], 2)
        near_own = gather_near(centroids.astype(jnp.bfloat16))
        far_own = flip(near_own, top_bit)
        near = gather_cent(near_own)
        n_near = len(near) * near_own.shape[0]
        far = gather_cent(far_own)
        chunk[4], chunk[3], chunk[2], far = hold(chunk[4], chunk[3], chunk[2], far)
        chunk[5] = rows_from(chunk[4], 1)
        chunk[6] = rows_from(chunk[4], 2)
        parts = (rows_from(chunk[3][:half], 4), rows_from(chunk[4][half:], 3))
        piece = jnp.concatenate(near + far, axis=0)
        passes = [first_pass(piece, [chunk[b] for b in bits]) for bits in GROUPS[:2]]
        parts, passes = hold(parts, passes)
        passes.append(first_pass(piece, [chunk[GROUPS[2][0]], *parts]))
        local, row_sqs, rows = zip(*passes)

        stats = by_position(by_chunk(local))
        stats = everywhere(stats)
        top = jnp.max(stats[:, 0], axis=0)
        total = jnp.sum(stats[:, 1] * jnp.exp(stats[:, 0] - top), axis=0)
        stats = by_position(jnp.stack([top, total]))
        final = [jnp.concatenate([stats[:, b] for b in bits], axis=1) for bits in GROUPS]

        n_half = n_near // 2
        far_other = sums_pass(piece, final, row_sqs, rows, n_near + n_half, 2 * n_near)
        middle = sums_pass(piece, final, row_sqs, rows, n_half, n_near + n_half)
        far = scatter_cent(middle[n_half:], far_other)
        count = far[:, width:]
        coarse = lax.reduce_precision(count, 8, 7)
        lane = lax.broadcasted_iota(jnp.int32, count.shape, 1)
        far = jnp.concatenate([far[:, :width], jnp.where(lane < 64, coarse, count - coarse)], axis=1)
        far = far.astype(jnp.bfloat16)
        near = sums_pass(piece, hold(final, far)[0], row_sqs, rows, 0, n_half, [centroids])
        near = scatter_cent(near, middle[:n_half])
        far = flip(far, top_bit).astype(jnp.float32)
        counts = far[:, width : width + 1] + far[:, width + 64 : width + 65]
        far = jnp.concatenate([far[:, :width], jnp.broadcast_to(counts, count.shape)], axis=1)
        sums = scatter_near(near + far)
        updated = sums[:, :width] / sums[:, width : width + 1]
        near_own = gather_near(updated.astype(jnp.bfloat16))
        far_own = flip(near_own, top_bit)
        stats = second_pass(jnp.concatenate(gather_cent(near_own), axis=0), row_sqs, rows, shard)
        far_own, stats = hold(far_own, stats)
        far = gather_cent(far_own)
        stats = merge(stats, second_pass(far_own, row_sqs, rows, shard))
        stats = merge(stats, second_pass(jnp.concatenate(far[1:], axis=0), row_sqs, rows, shard))
        stats = to_owner(by_position(stats))
        drop = stats[:, 0] - jnp.max(stats[:, 0], axis=0)
        factor = jnp.exp(drop)
        total = jnp.sum(factor * stats[:, 1], axis=0)
        spread = jnp.sum(factor * (stats[:, 2] + drop * stats[:, 1]), axis=0)
        entropy = jnp.log(total) - spread / total
        return (updated, entropy)

    in_specs = (P(("dp", "cent"), None), P(("dp", "cent"), None))
    out_specs = (P(("dp", "cent"), None), P(("dp", "cent")))
    return jax.shard_map(
        on_device, mesh=mesh, in_specs=in_specs, out_specs=out_specs, check_vma=False
    )
```

```python
import functools

import jax
import jax.numpy as jnp
from jax import lax
from jax.experimental import pallas as pl
from jax.experimental.pallas import tpu as pltpu
from jax.sharding import PartitionSpec as P

softness_level = 32.0
prior_mass = 4.0
CUBE = 8
GROUPS = ((0, 1, 2, 3), (4, 5), (6, 7))
VMEM = pl.BlockSpec(memory_space=pltpu.VMEM)
GRANT = 12 << 20


def params():
    return pltpu.CompilerParams(vmem_limit_bytes=GRANT)


def row_squares(rows):
    wide = rows.astype(jnp.float32)
    square = wide * wide
    part = square[:, :128]
    for j in range(128, square.shape[1], 128):
        part = part + square[:, j : j + 128]
    return jnp.sum(part.T, axis=0, keepdims=True)


def centroid_squares(piece):
    wide = piece.astype(jnp.float32)
    return jnp.sum(wide * wide, axis=1, keepdims=True)


def scores(piece, cent_sq, rows, row_sq):
    inner = lax.dot_general(piece, rows, (((1,), (1,)), ((), ())), preferred_element_type=jnp.float32)
    scale = 0.5 / softness_level
    return (2.0 * scale) * inner - scale * row_sq - scale * cent_sq


def first_kernel(n_chunks, shard, cents, *refs):
    chunks = refs[:n_chunks]
    stats_ref, row_sq_ref, rows_ref = refs[n_chunks:]
    at = 0
    for chunk in chunks:
        rows_ref[at : at + chunk.shape[0], :] = chunk[...]
        at += chunk.shape[0]
    piece = cents[...]
    cent_sq = centroid_squares(piece)
    tile = 2 * shard
    for j in range(at // tile):
        span = slice(j * tile, (j + 1) * tile)
        rows = rows_ref[span, :]
        row_sq = row_squares(rows)
        score = scores(piece, cent_sq, rows, row_sq)
        top = jnp.max(score, axis=0, keepdims=True)
        total = jnp.sum(jnp.exp(score - top), axis=0, keepdims=True)
        row_sq_ref[:, span] = row_sq
        for i in range(2):
            stats_ref[0, 2 * j + i : 2 * j + i + 1, :] = top[:, i * shard : (i + 1) * shard]
            stats_ref[1, 2 * j + i : 2 * j + i + 1, :] = total[:, i * shard : (i + 1) * shard]


def first_pass(cents, chunks):
    shard, width = chunks[0].shape
    n_k = cents.shape[0]
    n_rows = sum(c.shape[0] for c in chunks)
    return pl.pallas_call(
        functools.partial(first_kernel, len(chunks), shard),
        out_shape=(
            jax.ShapeDtypeStruct((2, n_rows // shard, shard), jnp.float32),
            jax.ShapeDtypeStruct((1, n_rows), jnp.float32),
            jax.ShapeDtypeStruct((n_rows, width), jnp.bfloat16),
        ),
        in_specs=[VMEM] * (1 + len(chunks)),
        out_specs=(VMEM,) * 3,
        compiler_params=params(),
        cost_estimate=pl.CostEstimate(
            flops=2 * n_k * n_rows * width, bytes_accessed=2 * n_rows * width, transcendentals=n_k * n_rows
        ),
        name="first_pass",
    )(cents, *chunks)


def sums_kernel(first, last, n, cents, *refs):
    stats, row_sqs, rows, priors = refs[:n], refs[n : 2 * n], refs[2 * n : 3 * n], refs[3 * n : -1]
    out_ref = refs[-1]
    width = cents.shape[1]
    piece = cents[first:last, :]
    cent_sq = centroid_squares(piece)
    counts = 0.0
    for s in range(n):
        score = scores(piece, cent_sq, rows[s][...], row_sqs[s][...])
        resp = (jnp.exp(score - stats[s][0:1, :]) * (1.0 / stats[s][1:2, :])).astype(jnp.bfloat16)
        counts = counts + jnp.sum(resp.astype(jnp.float32), axis=1, keepdims=True)
        part = jnp.dot(resp, rows[s][...], preferred_element_type=jnp.float32)
        if s:
            part = part + out_ref[:, :width]
        out_ref[:, :width] = part
    out_ref[:, width:] = jnp.broadcast_to(counts, (last - first, 128))
    for prior in priors:
        held = prior.shape[0]
        out_ref[:held, :width] += prior_mass * prior[...]
        out_ref[:held, width:] += prior_mass


def sums_pass(cents, stats, row_sqs, rows, first, last, priors=()):
    n = len(rows)
    width = rows[0].shape[1]
    n_rows = sum(r.shape[0] for r in rows)
    return pl.pallas_call(
        functools.partial(sums_kernel, first, last, n),
        out_shape=jax.ShapeDtypeStruct((last - first, width + 128), jnp.float32),
        in_specs=[VMEM] * (1 + 3 * n + len(priors)),
        out_specs=VMEM,
        compiler_params=params(),
        cost_estimate=pl.CostEstimate(
            flops=4 * (last - first) * n_rows * width,
            bytes_accessed=2 * n_rows * width,
            transcendentals=(last - first) * n_rows,
        ),
        name="sums_pass",
    )(cents, *stats, *row_sqs, *rows, *priors)


def second_kernel(shard, n, cents, *refs):
    row_sqs, rows, stats = refs[:n], refs[n : 2 * n], refs[2 * n :]
    piece = cents[...]
    cent_sq = centroid_squares(piece)
    tile = 2 * shard
    for s in range(n):
        for j in range(rows[s].shape[0] // tile):
            span = slice(j * tile, (j + 1) * tile)
            score = scores(piece, cent_sq, rows[s][span, :], row_sqs[s][:, span])
            top = jnp.max(score, axis=0, keepdims=True)
            shifted = score - top
            weight = jnp.exp(shifted)
            total = jnp.sum(weight, axis=0, keepdims=True)
            spread = jnp.sum(weight * shifted, axis=0, keepdims=True)
            for i in range(2):
                part = slice(i * shard, (i + 1) * shard)
                at = slice(2 * j + i, 2 * j + i + 1)
                stats[s][0, at, :] = top[:, part]
                stats[s][1, at, :] = total[:, part]
                stats[s][2, at, :] = spread[:, part]


def second_pass(cents, row_sqs, rows, shard):
    n = len(rows)
    n_k, width = cents.shape
    n_rows = sum(r.shape[0] for r in rows)
    out = pl.pallas_call(
        functools.partial(second_kernel, shard, n),
        out_shape=tuple(jax.ShapeDtypeStruct((3, r.shape[0] // shard, shard), jnp.float32) for r in rows),
        in_specs=[VMEM] * (1 + 2 * n),
        out_specs=(VMEM,) * n,
        compiler_params=params(),
        cost_estimate=pl.CostEstimate(
            flops=2 * n_k * n_rows * width, bytes_accessed=2 * n_rows * width, transcendentals=n_k * n_rows
        ),
        name="second_pass",
    )(cents, *row_sqs, *rows)
    return by_chunk(out)


def hold(*values):
    return lax.optimization_barrier(values)


def merge(a, b):
    top = jnp.maximum(a[0], b[0])
    drops = (a[0] - top, b[0] - top)
    factors = (jnp.exp(drops[0]), jnp.exp(drops[1]))
    out = [top, factors[0] * a[1] + factors[1] * b[1]]
    if a.shape[0] == 3:
        out.append(factors[0] * (a[2] + drops[0] * a[1]) + factors[1] * (b[2] + drops[1] * b[1]))
    return jnp.stack(out)


def by_chunk(groups):
    place = {b: (g, i) for g, bits in enumerate(GROUPS) for i, b in enumerate(bits)}
    return jnp.stack([groups[place[b][0]][:, place[b][1]] for b in range(CUBE)], axis=1)


def solution(mesh):
    n_dp = mesh.shape["dp"]
    n_cent = mesh.shape["cent"]
    high = n_dp // 2
    top_bit = n_dp // 4

    def flip(value, bits):
        return lax.ppermute(value, "dp", [(i, i ^ bits) for i in range(n_dp)])

    def member(place):
        return (place & 3) | (high if place & 4 else 0)

    def rows_from(value, place):
        return flip(value, member(place))

    def across(value, bits):
        return lax.ppermute(value, "cent", [(i, i ^ bits) for i in range(n_cent)])

    def gather_cent(value):
        blocks = [value]
        bits = 1
        while bits < n_cent:
            blocks = blocks + [across(b, bits) for b in blocks]
            bits *= 2
        return blocks

    def scatter_cent(value, other=None):
        bits = n_cent // 2
        while bits:
            half = value.shape[0] // 2
            if other is not None:
                value, other = value + across(other, bits), None
            else:
                value = value[:half] + across(value[half:], bits)
            bits //= 2
        return value

    def gather_near(value):
        bits = 4
        while bits < top_bit:
            value = jnp.concatenate([value, flip(value, bits)], axis=0)
            bits *= 2
        return value

    def scatter_near(value):
        bits = top_bit // 2
        while bits >= 4:
            half = value.shape[0] // 2
            value = value[:half] + flip(value[half:], bits)
            bits //= 2
        return value

    def by_position(stats):
        place = lax.axis_index("dp")
        for bit in (1, 2, 4):
            swapped = jnp.stack([stats[:, b ^ bit] for b in range(CUBE)], axis=1)
            stats = jnp.where((place & member(bit)) != 0, swapped, stats)
        return stats

    def exchange(value):
        groups = [[i + member(place) for place in range(CUBE)] for i in range(0, high, 4)]
        return lax.all_to_all(value, "dp", 0, 0, axis_index_groups=groups)

    def everywhere(stats):
        return exchange(jnp.broadcast_to(stats[None], (CUBE,) + stats.shape))

    def to_owner(stats):
        return exchange(stats.transpose(1, 0, 2))

    def on_device(embeddings, centroids):
        shard, width = embeddings.shape
        half = shard // 2
        chunk = {0: embeddings.astype(jnp.bfloat16)}
        for bit in (4, 1, 2):
            chunk[bit] = rows_from(chunk[0], bit)
        chunk[3] = rows_from(chunk[1], 2)
        near_own = gather_near(centroids.astype(jnp.bfloat16))
        far_own = flip(near_own, top_bit)
        near = gather_cent(near_own)
        n_near = len(near) * near_own.shape[0]
        far = gather_cent(far_own)
        chunk[4], chunk[3], chunk[2], far = hold(chunk[4], chunk[3], chunk[2], far)
        chunk[5] = rows_from(chunk[4], 1)
        chunk[6] = rows_from(chunk[4], 2)
        parts = (rows_from(chunk[3][:half], 4), rows_from(chunk[4][half:], 3))
        piece = jnp.concatenate(near + far, axis=0)
        passes = [first_pass(piece, [chunk[b] for b in bits]) for bits in GROUPS[:2]]
        parts, passes = hold(parts, passes)
        passes.append(first_pass(piece, [chunk[GROUPS[2][0]], *parts]))
        local, row_sqs, rows = zip(*passes)

        stats = by_position(by_chunk(local))
        stats = everywhere(stats)
        top = jnp.max(stats[:, 0], axis=0)
        total = jnp.sum(stats[:, 1] * jnp.exp(stats[:, 0] - top), axis=0)
        stats = by_position(jnp.stack([top, total]))
        final = [jnp.concatenate([stats[:, b] for b in bits], axis=1) for bits in GROUPS]

        far = scatter_cent(sums_pass(piece, final, row_sqs, rows, n_near, 2 * n_near))
        count = far[:, width:]
        coarse = lax.reduce_precision(count, 8, 7)
        lane = lax.broadcasted_iota(jnp.int32, count.shape, 1)
        far = jnp.concatenate([far[:, :width], jnp.where(lane < 64, coarse, count - coarse)], axis=1)
        far = far.astype(jnp.bfloat16)
        n_half = n_near // 2
        other = sums_pass(piece, final, row_sqs, rows, n_half, n_near)
        near = sums_pass(piece, hold(final, far)[0], row_sqs, rows, 0, n_half, [centroids])
        near = scatter_cent(near, other)
        far = flip(far, top_bit).astype(jnp.float32)
        counts = far[:, width : width + 1] + far[:, width + 64 : width + 65]
        far = jnp.concatenate([far[:, :width], jnp.broadcast_to(counts, count.shape)], axis=1)
        sums = scatter_near(near + far)
        rounded = (sums[:, :width] / sums[:, width : width + 1]).astype(jnp.bfloat16)
        sums = hold(sums, rounded)[0]
        updated = sums[:, :width] / sums[:, width : width + 1]
        near_own = gather_near(rounded)
        far_own = flip(near_own, top_bit)
        stats = second_pass(jnp.concatenate(gather_cent(near_own), axis=0), row_sqs, rows, shard)
        far_own, stats = hold(far_own, stats)
        far = gather_cent(far_own)
        stats = merge(stats, second_pass(far_own, row_sqs, rows, shard))
        stats = merge(stats, second_pass(jnp.concatenate(far[1:], axis=0), row_sqs, rows, shard))
        stats = to_owner(by_position(stats))
        drop = stats[:, 0] - jnp.max(stats[:, 0], axis=0)
        factor = jnp.exp(drop)
        total = jnp.sum(factor * stats[:, 1], axis=0)
        spread = jnp.sum(factor * (stats[:, 2] + drop * stats[:, 1]), axis=0)
        entropy = jnp.log(total) - spread / total
        return (updated, entropy)

    in_specs = (P(("dp", "cent"), None), P(("dp", "cent"), None))
    out_specs = (P(("dp", "cent"), None), P(("dp", "cent")))
    return jax.shard_map(
        on_device, mesh=mesh, in_specs=in_specs, out_specs=out_specs, check_vma=False
    )
```

```python
import functools

import jax
import jax.numpy as jnp
from jax import lax
from jax.experimental import pallas as pl
from jax.experimental.pallas import tpu as pltpu
from jax.sharding import PartitionSpec as P

softness_level = 32.0
prior_mass = 4.0
CUBE = 8
GROUPS = ((0, 1, 2, 3), (4, 5), (6, 7))
VMEM = pl.BlockSpec(memory_space=pltpu.VMEM)
GRANT = 12 << 20


def params():
    return pltpu.CompilerParams(vmem_limit_bytes=GRANT)


def row_squares(rows):
    wide = rows.astype(jnp.float32)
    square = wide * wide
    part = square[:, :128]
    for j in range(128, square.shape[1], 128):
        part = part + square[:, j : j + 128]
    return jnp.sum(part.T, axis=0, keepdims=True)


def centroid_squares(piece):
    wide = piece.astype(jnp.float32)
    return jnp.sum(wide * wide, axis=1, keepdims=True)


def scores(piece, cent_sq, rows, row_sq):
    inner = lax.dot_general(piece, rows, (((1,), (1,)), ((), ())), preferred_element_type=jnp.float32)
    scale = 0.5 / softness_level
    return (2.0 * scale) * inner - scale * row_sq - scale * cent_sq


def first_kernel(n_chunks, shard, cents, *refs):
    chunks = refs[:n_chunks]
    stats_ref, row_sq_ref, rows_ref = refs[n_chunks:]
    at = 0
    for chunk in chunks:
        rows_ref[at : at + chunk.shape[0], :] = chunk[...]
        at += chunk.shape[0]
    piece = cents[...]
    cent_sq = centroid_squares(piece)
    tile = 2 * shard
    for j in range(at // tile):
        span = slice(j * tile, (j + 1) * tile)
        rows = rows_ref[span, :]
        row_sq = row_squares(rows)
        score = scores(piece, cent_sq, rows, row_sq)
        top = jnp.max(score, axis=0, keepdims=True)
        total = jnp.sum(jnp.exp(score - top), axis=0, keepdims=True)
        row_sq_ref[:, span] = row_sq
        for i in range(2):
            stats_ref[0, 2 * j + i : 2 * j + i + 1, :] = top[:, i * shard : (i + 1) * shard]
            stats_ref[1, 2 * j + i : 2 * j + i + 1, :] = total[:, i * shard : (i + 1) * shard]


def first_pass(cents, chunks):
    shard, width = chunks[0].shape
    n_k = cents.shape[0]
    n_rows = sum(c.shape[0] for c in chunks)
    return pl.pallas_call(
        functools.partial(first_kernel, len(chunks), shard),
        out_shape=(
            jax.ShapeDtypeStruct((2, n_rows // shard, shard), jnp.float32),
            jax.ShapeDtypeStruct((1, n_rows), jnp.float32),
            jax.ShapeDtypeStruct((n_rows, width), jnp.bfloat16),
        ),
        in_specs=[VMEM] * (1 + len(chunks)),
        out_specs=(VMEM,) * 3,
        compiler_params=params(),
        cost_estimate=pl.CostEstimate(
            flops=2 * n_k * n_rows * width, bytes_accessed=2 * n_rows * width, transcendentals=n_k * n_rows
        ),
        name="first_pass",
    )(cents, *chunks)


def sums_kernel(first, last, n, cents, *refs):
    stats, row_sqs, rows, priors = refs[:n], refs[n : 2 * n], refs[2 * n : 3 * n], refs[3 * n : -1]
    out_ref = refs[-1]
    width = cents.shape[1]
    piece = cents[first:last, :]
    cent_sq = centroid_squares(piece)
    counts = 0.0
    for s in range(n):
        score = scores(piece, cent_sq, rows[s][...], row_sqs[s][...])
        resp = (jnp.exp(score - stats[s][0:1, :]) * (1.0 / stats[s][1:2, :])).astype(jnp.bfloat16)
        counts = counts + jnp.sum(resp.astype(jnp.float32), axis=1, keepdims=True)
        part = jnp.dot(resp, rows[s][...], preferred_element_type=jnp.float32)
        if s:
            part = part + out_ref[:, :width]
        out_ref[:, :width] = part
    out_ref[:, width:] = jnp.broadcast_to(counts, (last - first, 128))
    for prior in priors:
        held = prior.shape[0]
        out_ref[:held, :width] += prior_mass * prior[...]
        out_ref[:held, width:] += prior_mass


def sums_pass(cents, stats, row_sqs, rows, first, last, priors=()):
    n = len(rows)
    width = rows[0].shape[1]
    n_rows = sum(r.shape[0] for r in rows)
    return pl.pallas_call(
        functools.partial(sums_kernel, first, last, n),
        out_shape=jax.ShapeDtypeStruct((last - first, width + 128), jnp.float32),
        in_specs=[VMEM] * (1 + 3 * n + len(priors)),
        out_specs=VMEM,
        compiler_params=params(),
        cost_estimate=pl.CostEstimate(
            flops=4 * (last - first) * n_rows * width,
            bytes_accessed=2 * n_rows * width,
            transcendentals=(last - first) * n_rows,
        ),
        name="sums_pass",
    )(cents, *stats, *row_sqs, *rows, *priors)


def second_kernel(shard, n, cents, *refs):
    row_sqs, rows, stats = refs[:n], refs[n : 2 * n], refs[2 * n :]
    piece = cents[...]
    cent_sq = centroid_squares(piece)
    tile = 2 * shard
    for s in range(n):
        for j in range(rows[s].shape[0] // tile):
            span = slice(j * tile, (j + 1) * tile)
            score = scores(piece, cent_sq, rows[s][span, :], row_sqs[s][:, span])
            top = jnp.max(score, axis=0, keepdims=True)
            shifted = score - top
            weight = jnp.exp(shifted)
            total = jnp.sum(weight, axis=0, keepdims=True)
            spread = jnp.sum(weight * shifted, axis=0, keepdims=True)
            for i in range(2):
                part = slice(i * shard, (i + 1) * shard)
                at = slice(2 * j + i, 2 * j + i + 1)
                stats[s][0, at, :] = top[:, part]
                stats[s][1, at, :] = total[:, part]
                stats[s][2, at, :] = spread[:, part]


def second_pass(cents, row_sqs, rows, shard):
    n = len(rows)
    n_k, width = cents.shape
    n_rows = sum(r.shape[0] for r in rows)
    out = pl.pallas_call(
        functools.partial(second_kernel, shard, n),
        out_shape=tuple(jax.ShapeDtypeStruct((3, r.shape[0] // shard, shard), jnp.float32) for r in rows),
        in_specs=[VMEM] * (1 + 2 * n),
        out_specs=(VMEM,) * n,
        compiler_params=params(),
        cost_estimate=pl.CostEstimate(
            flops=2 * n_k * n_rows * width, bytes_accessed=2 * n_rows * width, transcendentals=n_k * n_rows
        ),
        name="second_pass",
    )(cents, *row_sqs, *rows)
    return by_chunk(out)


def hold(*values):
    return lax.optimization_barrier(values)


def merge(a, b):
    top = jnp.maximum(a[0], b[0])
    drops = (a[0] - top, b[0] - top)
    factors = (jnp.exp(drops[0]), jnp.exp(drops[1]))
    out = [top, factors[0] * a[1] + factors[1] * b[1]]
    if a.shape[0] == 3:
        out.append(factors[0] * (a[2] + drops[0] * a[1]) + factors[1] * (b[2] + drops[1] * b[1]))
    return jnp.stack(out)


def by_chunk(groups):
    place = {b: (g, i) for g, bits in enumerate(GROUPS) for i, b in enumerate(bits)}
    return jnp.stack([groups[place[b][0]][:, place[b][1]] for b in range(CUBE)], axis=1)


def solution(mesh):
    n_dp = mesh.shape["dp"]
    n_cent = mesh.shape["cent"]
    high = n_dp // 2
    top_bit = n_dp // 4

    def flip(value, bits):
        return lax.ppermute(value, "dp", [(i, i ^ bits) for i in range(n_dp)])

    def member(place):
        return (place & 3) | (high if place & 4 else 0)

    def rows_from(value, place):
        return flip(value, member(place))

    def across(value, bits):
        return lax.ppermute(value, "cent", [(i, i ^ bits) for i in range(n_cent)])

    def gather_cent(value):
        blocks = [value]
        bits = 1
        while bits < n_cent:
            blocks = blocks + [across(b, bits) for b in blocks]
            bits *= 2
        return blocks

    def scatter_cent(value, other=None):
        bits = n_cent // 2
        while bits:
            half = value.shape[0] // 2
            if other is not None:
                value, other = value + across(other, bits), None
            else:
                value = value[:half] + across(value[half:], bits)
            bits //= 2
        return value

    def gather_near(value):
        bits = 4
        while bits < top_bit:
            value = jnp.concatenate([value, flip(value, bits)], axis=0)
            bits *= 2
        return value

    def scatter_near(value):
        bits = top_bit // 2
        while bits >= 4:
            half = value.shape[0] // 2
            value = value[:half] + flip(value[half:], bits)
            bits //= 2
        return value

    def by_position(stats):
        place = lax.axis_index("dp")
        for bit in (1, 2, 4):
            swapped = jnp.stack([stats[:, b ^ bit] for b in range(CUBE)], axis=1)
            stats = jnp.where((place & member(bit)) != 0, swapped, stats)
        return stats

    def exchange(value):
        groups = [[i + member(place) for place in range(CUBE)] for i in range(0, high, 4)]
        return lax.all_to_all(value, "dp", 0, 0, axis_index_groups=groups)

    def everywhere(stats):
        return exchange(jnp.broadcast_to(stats[None], (CUBE,) + stats.shape))

    def to_owner(stats):
        return exchange(stats.transpose(1, 0, 2))

    def on_device(embeddings, centroids):
        shard, width = embeddings.shape
        half = shard // 2
        chunk = {0: embeddings.astype(jnp.bfloat16)}
        for bit in (4, 1, 2):
            chunk[bit] = rows_from(chunk[0], bit)
        chunk[3] = rows_from(chunk[1], 2)
        near_own = gather_near(centroids.astype(jnp.bfloat16))
        far_own = flip(near_own, top_bit)
        near = gather_cent(near_own)
        n_near = len(near) * near_own.shape[0]
        far = gather_cent(far_own)
        chunk[4], chunk[3], chunk[2], far = hold(chunk[4], chunk[3], chunk[2], far)
        chunk[5] = rows_from(chunk[4], 1)
        chunk[6] = rows_from(chunk[4], 2)
        parts = (rows_from(chunk[3][:half], 4), rows_from(chunk[4][half:], 3))
        piece = jnp.concatenate(near + far, axis=0)
        passes = [first_pass(piece, [chunk[b] for b in bits]) for bits in GROUPS[:2]]
        parts, passes = hold(parts, passes)
        passes.append(first_pass(piece, [chunk[GROUPS[2][0]], *parts]))
        local, row_sqs, rows = zip(*passes)

        stats = by_position(by_chunk(local))
        stats = everywhere(stats)
        top = jnp.max(stats[:, 0], axis=0)
        total = jnp.sum(stats[:, 1] * jnp.exp(stats[:, 0] - top), axis=0)
        stats = by_position(jnp.stack([top, total]))
        final = [jnp.concatenate([stats[:, b] for b in bits], axis=1) for bits in GROUPS]

        far = scatter_cent(sums_pass(piece, final, row_sqs, rows, n_near, 2 * n_near))
        count = far[:, width:]
        coarse = lax.reduce_precision(count, 8, 7)
        lane = lax.broadcasted_iota(jnp.int32, count.shape, 1)
        far = jnp.concatenate([far[:, :width], jnp.where(lane < 64, coarse, count - coarse)], axis=1)
        far = far.astype(jnp.bfloat16)
        n_half = n_near // 2
        other = sums_pass(piece, final, row_sqs, rows, n_half, n_near)
        near = sums_pass(piece, hold(final, far)[0], row_sqs, rows, 0, n_half, [centroids])
        near = scatter_cent(near, other)
        far = flip(far, top_bit).astype(jnp.float32)
        counts = far[:, width : width + 1] + far[:, width + 64 : width + 65]
        far = jnp.concatenate([far[:, :width], jnp.broadcast_to(counts, count.shape)], axis=1)
        sums = scatter_near(near + far)
        rounded = (sums[:, :width] / sums[:, width : width + 1]).astype(jnp.bfloat16)
        sums = hold(sums, rounded)[0]
        updated = sums[:, :width] / sums[:, width : width + 1]
        near_own = gather_near(rounded)
        far_own = flip(near_own, top_bit)
        stats = second_pass(jnp.concatenate(gather_cent(near_own), axis=0), row_sqs, rows, shard)
        far_own, stats, updated = hold(far_own, stats, updated)
        far = gather_cent(far_own)
        stats = merge(stats, second_pass(far_own, row_sqs, rows, shard))
        stats = merge(stats, second_pass(jnp.concatenate(far[1:], axis=0), row_sqs, rows, shard))
        stats = to_owner(by_position(stats))
        drop = stats[:, 0] - jnp.max(stats[:, 0], axis=0)
        factor = jnp.exp(drop)
        total = jnp.sum(factor * stats[:, 1], axis=0)
        spread = jnp.sum(factor * (stats[:, 2] + drop * stats[:, 1]), axis=0)
        entropy = jnp.log(total) - spread / total
        return (updated, entropy)

    in_specs = (P(("dp", "cent"), None), P(("dp", "cent"), None))
    out_specs = (P(("dp", "cent"), None), P(("dp", "cent")))
    return jax.shard_map(
        on_device, mesh=mesh, in_specs=in_specs, out_specs=out_specs, check_vma=False
    )
```
